32 devices in a mesh: gx: 16 (over z, x, core), gy: 2 (over y).
Axes of the slice: x: 2, y: 2, z: 4, core: 2. Of those that a mesh axis runs over, the one named last changes fastest.
Arguments:
- orbitals: float32 [2, 32, 1024, 256], P(None, None, 'gx', 'gy'), may hold values from -12 to 12
- potential: float32 [32, 1024, 256], P(None, 'gx', 'gy'), may hold values from 0.5 to 2
- shift_ratio: float32 [1], replicated, may hold values from 16 to 48
Outputs:
- orbitals_next: float32 [2, 32, 1024, 256], P(None, None, 'gx', 'gy')
The draws below stay inside these ranges and needn't reach their ends.
All inputs are finite; a program needn't handle non-finite values.
Results may differ from the reference program's by a relative error of at most 0.0003.
Values sent between devices are 32-bit elements; how exact they have to be, the bound alone decides.
A program may use at most 128 MiB of HBM per device.

```python
import math
import jax
import jax.numpy as jnp
from jax import lax

COMPS = 2
NX = 1024
NY = 256
NZ = 32


def draw_orbitals(key, part):
    first, second, third, fourth, fifth, sixth, seventh = jax.random.split(key, 7)
    position = jnp.arange(NX, dtype=jnp.float32) / NX
    row_scale = jnp.exp(math.log(3.0) * position + jax.random.uniform(second, (NX,), jnp.float32, -1.2, 0.0))
    column_scale = jnp.exp(jax.random.uniform(third, (NZ, 1, NY), jnp.float32, -1.2, 0.0))
    wave_mode = jax.random.randint(fourth, (COMPS, NZ, 1, 1), 37, 41).astype(jnp.float32)
    wave_phase = jax.random.uniform(fifth, (COMPS, NZ, 1, 1), jnp.float32, -math.pi, math.pi)
    wave_sign = (2 * jax.random.randint(sixth, (COMPS, NZ, 1, NY), 0, 2) - 1).astype(jnp.float32)
    wave_size = jax.random.uniform(seventh, (COMPS, NZ, 1, NY), jnp.float32, 0.5, 1.2)
    wave = 1.6 * wave_sign * wave_size * jnp.cos(2.0 * math.pi * wave_mode * position[None, None, :, None] + wave_phase)
    base = jnp.clip(jax.random.normal(first, (COMPS, NZ, NX, NY), jnp.float32), -2.0, 2.0)
    return ((base * column_scale[None] + wave) * row_scale[None, None, :, None]).astype(jnp.float32)


def block_levels(key, dims, pieces, least, top_value):
    def one(dim, blocks):
        steps = jax.random.uniform(jax.random.fold_in(jax.random.fold_in(key, 6), dim), (blocks,), jnp.float32, least / len(pieces), top_value / len(pieces))
        return jnp.repeat(jnp.exp(steps), dims[dim] // blocks).reshape((-1,) + (1,) * (len(dims) - dim - 1))

    factor_of = one(*pieces[0])
    for cut in pieces[1:]:
        factor_of = factor_of * one(*cut)
    return factor_of


def setup_inputs(seed: int = 0) -> dict:
    splits = jax.random.split(jax.random.key(seed), 4)
    orbitals = draw_orbitals(jax.random.fold_in(splits[3], 71), 0)
    potential = jnp.clip(0.5 + 1.5 * jax.random.uniform(splits[1], (NZ, NX, NY), jnp.float32) ** block_levels(splits[1], (NZ, NX, NY), ((1, 16), (2, 2)), -0.2, 0.2), 0.5, 2.0)
    shift_ratio = jnp.clip(jnp.exp(jax.random.uniform(splits[2], (1,), jnp.float32, math.log(16.0), math.log(48.0))), 16.0, 48.0)
    return dict(orbitals=orbitals, potential=potential, shift_ratio=shift_ratio)


def reference(orbitals, potential, shift_ratio):
    neighbours = jnp.roll(orbitals, 1, axis=2) + jnp.roll(orbitals, -1, axis=2)
    neighbours = neighbours + jnp.roll(orbitals, 1, axis=3) + jnp.roll(orbitals, -1, axis=3)
    neighbours = neighbours + jnp.roll(orbitals, 1, axis=1) + jnp.roll(orbitals, -1, axis=1)
    laplace = neighbours - 6.0 * orbitals
    squares = orbitals * orbitals
    density = jnp.stack([0.06 * squares[0] + 0.04 * squares[1], 0.04 * squares[0] + 0.05 * squares[1]])
    applied = -0.5 * laplace + (potential[None] + density) * orbitals
    mean_square = lax.optimization_barrier(jnp.mean(squares, axis=(1, 2, 3)))
    energy = lax.optimization_barrier(jnp.mean(orbitals * applied, axis=(1, 2, 3))) / (mean_square + 1e-06)
    residual = applied - energy[:, None, None, None] * orbitals
    sigma = shift_ratio[0] / float(NX * NX)
    freq = jnp.arange(NX).astype(residual.dtype)
    denom = sigma + 2.0 * jnp.sin(jnp.pi * freq / NX) ** 2
    gain = sigma / denom
    flat = residual.reshape(COMPS * NZ, NX, NY)

    def solve_plane(plane):
        spectrum = jnp.fft.fft(plane, axis=0)
        return jnp.real(jnp.fft.ifft(spectrum * gain[:, None], axis=0)).astype(plane.dtype)
    direction = lax.map(solve_plane, flat).reshape(residual.shape)
    update = orbitals - 4.0 * direction
    mean_update = lax.optimization_barrier(jnp.mean(update * update, axis=(1, 2, 3)))
    ratio = jnp.sqrt(mean_square / (mean_update + 1e-06))
    return update * ratio[:, None, None, None]
```

```python
import functools

import jax
import jax.numpy as jnp
from jax import lax
from jax.experimental import pallas as pl
from jax.experimental.pallas import tpu as pltpu
from jax.sharding import PartitionSpec as P

TAU = 4.0
EPS = 1e-06
COUPLING_FIRST = 0.06
COUPLING_SECOND = 0.05
COUPLING_CROSS = 0.04
MESH = pl.DeviceIdType.MESH
LANES = 128


def wait_bytes(ref, sem):
    pltpu.make_async_copy(ref, ref, sem).wait()


def step_kernel(
    groups,
    owners,
    cells,
    params,
    orb_hbm,
    pot_hbm,
    out_hbm,
    ratio_ref,
    orb,
    pot,
    app,
    table,
    weights,
    x_send,
    x_halo,
    y_send,
    y_halo,
    tip_send,
    tip_recv,
    carry_send,
    carry,
    sums_send,
    sums_recv,
    mass_send,
    mass_recv,
    load_sem,
    halo_send_sem,
    halo_recv_sem,
    send_sem,
    recv_sem,
    out_sem,
):
    comps, levels, width, lanes = orb.shape
    per = levels // owners
    rows = comps * per
    devices = 2 * groups
    gx = lax.axis_index("gx")
    gy = lax.axis_index("gy")
    lane = lax.broadcasted_iota(jnp.int32, (width, lanes), 1)
    row = lax.broadcasted_iota(jnp.int32, (width, lanes), 0)
    lane_row = lax.broadcasted_iota(jnp.int32, (1, lanes), 1)

    def device_at(step):
        return (lax.rem(gx + step // 2, groups), lax.rem(gy + step % 2, 2))

    def slot_at(step):
        return lax.rem(groups - step // 2, groups) * 2 + step % 2

    load_orb = pltpu.make_async_copy(orb_hbm, orb, load_sem.at[0])
    load_pot = pltpu.make_async_copy(pot_hbm, pot, load_sem.at[1])
    load_orb.start()
    load_pot.start()

    barrier = pltpu.get_barrier_semaphore()

    def greet(step, _):
        pl.semaphore_signal(barrier, inc=1, device_id=device_at(step), device_id_type=MESH)
        return 0

    lax.fori_loop(1, devices, greet, 0)

    decay, gain, tip_gain, block, inv_wrap = (params[i] for i in range(5))
    position = row.astype(jnp.float32)
    weights[0] = jnp.exp(-decay * (float(width - 1) - position))
    weights[1] = jnp.exp(-decay * position)
    t_row = lax.broadcasted_iota(jnp.int32, (width, 3 * width), 0)
    t_col = lax.broadcasted_iota(jnp.int32, (width, 3 * width), 1)
    t_mod = jnp.where(t_col >= 2 * width, t_col - 2 * width, jnp.where(t_col >= width, t_col - width, t_col))
    green = gain * jnp.exp(-decay * jnp.abs(t_row - t_mod).astype(jnp.float32))
    high = green.astype(jnp.bfloat16)
    low = (green - high.astype(jnp.float32)).astype(jnp.bfloat16)
    table[...] = jnp.where(t_col >= 2 * width, low.astype(jnp.float32), high.astype(jnp.float32)).astype(jnp.bfloat16)

    load_orb.wait()

    def pack(z, held):
        for c in range(comps):
            plane = orb[c, z]
            index = z * comps + c
            held = jnp.where(lane // 2 == index, pltpu.roll(plane, 2 * index + 1, 1), held)
            x_send[0, pl.ds(index, 1), :] = orb[c, z, width - 1 : width, :]
            x_send[1, pl.ds(index, 1), :] = orb[c, z, 0:1, :]
        return held

    y_send[...] = lax.fori_loop(0, levels, pack, jnp.zeros((width, lanes), jnp.float32))

    pl.semaphore_wait(barrier, devices - 1)
    right = lax.rem(gx + 1, groups)
    left = lax.rem(gx + groups - 1, groups)
    halos = [
        pltpu.make_async_remote_copy(
            src, dst, halo_send_sem.at[i], halo_recv_sem.at[i], device_id=target, device_id_type=MESH
        )
        for i, (src, dst, target) in enumerate(
            (
                (y_send, y_halo, (gx, 1 - gy)),
                (x_send.at[0], x_halo.at[0], (right, gy)),
                (x_send.at[1], x_halo.at[1], (left, gy)),
            )
        )
    ]
    for copy in halos:
        copy.start()
    load_pot.wait()
    for copy in halos:
        copy.wait()

    lack = y_halo[...] - y_send[...]
    y_halo[...] = jnp.where(lane % 2 == 0, pltpu.roll(lack, lanes - 1, 1), pltpu.roll(lack, 1, 1))

    def fold(x):
        total = x[0:8]
        for i in range(8, width, 8):
            total = total + x[i : i + 8]
        return total

    def apply_level(z, owner, local, sums):
        o = [orb[c, z] for c in range(comps)]
        before = lax.rem(z + levels - 1, levels)
        after = lax.rem(z + 1, levels)
        squares = [x * x for x in o]
        density = (
            COUPLING_FIRST * squares[0] + COUPLING_CROSS * squares[1],
            COUPLING_CROSS * squares[0] + COUPLING_SECOND * squares[1],
        )
        trap = pot[z]
        result = []
        for c in range(comps):
            index = z * comps + c
            mine = o[c]
            ends = pltpu.roll(y_halo[...], lanes - 1 - 2 * index, 1)
            ends = jnp.where((lane == 0) | (lane == lanes - 1), ends, 0.0)
            prior = jnp.where(row == 0, x_halo[0, pl.ds(index, 1), :], pltpu.roll(mine, 1, 0))
            later = jnp.where(row == width - 1, x_halo[1, pl.ds(index, 1), :], pltpu.roll(mine, width - 1, 0))
            near = pltpu.roll(mine, 1, 1) + pltpu.roll(mine, lanes - 1, 1) + ends
            near = near + prior + later + orb[c, before] + orb[c, after]
            applied = -0.5 * (near - 6.0 * mine) + (trap + density[c]) * mine
            app[c, z] = applied
            for i, x in enumerate((applied, mine)):
                for j in range(2):
                    at = (2 * i + j) * rows + local * comps + c
                    tip_send[owner, at : at + 1, :] = jnp.sum(fold(weights[j] * x), axis=0, keepdims=True)
            result.append(sums[2 * c] + fold(mine * applied))
            result.append(sums[2 * c + 1] + fold(squares[c]))
        return tuple(result)

    def apply_owner(step, sums):
        owner = lax.rem(lax.rem(gx, owners) + 1 + step, owners)
        for local in range(per):
            sums = apply_level(owner * per + local, owner, local, sums)

        @pl.when(owner != gx)
        def _():
            pltpu.make_async_remote_copy(
                tip_send.at[owner],
                tip_recv.at[lax.rem(gx - owner + groups, groups)],
                send_sem.at[0],
                recv_sem.at[0],
                device_id=(owner, gy),
                device_id_type=MESH,
            ).start()

        return sums

    zero = jnp.zeros((8, lanes), jnp.float32)
    sums = lax.fori_loop(0, owners, apply_owner, (zero,) * (2 * comps))

    def lane_of(values):
        packed = jnp.zeros((1, lanes), jnp.float32)
        for i, x in enumerate(values):
            whole = jnp.sum(jnp.sum(x, axis=0, keepdims=True), axis=1, keepdims=True)
            packed = jnp.where(lane_row == i, whole, packed)
        return packed

    def spread(source, target, which):
        def send(step, _):
            pltpu.make_async_remote_copy(
                source.at[0],
                target.at[slot_at(step)],
                send_sem.at[which],
                recv_sem.at[which],
                device_id=device_at(step),
                device_id_type=MESH,
            ).start()
            return 0

        lax.fori_loop(1, devices, send, 0)

    def gathered(target, which, count):
        wait_bytes(target.at[pl.ds(1, devices - 1)], recv_sem.at[which])
        total = jnp.sum(target[...], axis=0)
        return [
            jnp.sum(jnp.where(lane_row == i, total, 0.0), axis=1, keepdims=True) for i in range(count)
        ]

    own = lane_of(sums)
    sums_send[0] = own
    sums_recv[0] = own
    spread(sums_send, sums_recv, 1)

    @pl.when(gx < owners)
    def _():
        tip_recv[0] = tip_send[lax.rem(gx, owners)]

    totals = gathered(sums_recv, 1, 2 * comps)
    mean_square = [totals[2 * c + 1] / cells for c in range(comps)]
    energy = [totals[2 * c] / cells / (mean_square[c] + EPS) for c in range(comps)]

    @pl.when(gx < owners)
    def _():
        wait_bytes(tip_recv.at[pl.ds(1, groups - 1)], recv_sem.at[0])
        tip_row = lax.broadcasted_iota(jnp.int32, (2 * rows, lanes), 0)
        scale = jnp.where(tip_row % 2 == 0, energy[0], energy[1])

        def tips(k):
            return tip_recv[k, 0 : 2 * rows, :] - scale * tip_recv[k, 2 * rows : 4 * rows, :]

        def collect(k, held):
            ahead, behind = held
            return block * ahead + tips(k), block * behind + tips(groups - 1 - k)

        start = jnp.zeros((2 * rows, lanes), jnp.float32)
        ahead, behind = lax.fori_loop(0, groups, collect, (start, start))

        def hand_out(k, held):
            ahead, behind = held
            back = groups - 1 - k
            carry_send[k, 0:rows, :] = ahead[0:rows]
            carry_send[back, rows : 2 * rows, :] = behind[rows : 2 * rows]
            return block * ahead + tip_gain * tips(k), block * behind + tip_gain * tips(back)

        factor = tip_gain * inv_wrap
        lax.fori_loop(0, groups, hand_out, (factor * ahead, factor * behind))

        def send(step, _):
            pltpu.make_async_remote_copy(
                carry_send.at[step],
                carry.at[gx],
                send_sem.at[2],
                recv_sem.at[2],
                device_id=(lax.rem(gx + step, groups), gy),
                device_id_type=MESH,
            ).start()
            return 0

        lax.fori_loop(1, groups, send, 0)
        carry[lax.rem(gx, owners)] = carry_send[0]

    def solve(z, _):
        pair = jnp.concatenate([app[c, z] - energy[c] * orb[c, z] for c in range(comps)], axis=1)
        high = pair.astype(jnp.bfloat16)
        low = (pair - high.astype(jnp.float32)).astype(jnp.bfloat16)
        local = jnp.dot(
            table[...], jnp.concatenate([high, low, high], axis=0), preferred_element_type=jnp.float32
        )
        for c in range(comps):
            app[c, z] = orb[c, z] - local[:, c * lanes : (c + 1) * lanes]
        return 0

    lax.fori_loop(0, levels, solve, 0, unroll=2)

    @pl.when(gx < owners)
    def _():
        wait_bytes(carry.at[pl.ds(0, owners - 1)], recv_sem.at[2])

    @pl.when(gx >= owners)
    def _():
        wait_bytes(carry, recv_sem.at[2])

    def update_owner(owner, masses):
        masses = list(masses)
        for local in range(per):
            z = owner * per + local
            for c in range(comps):
                at = local * comps + c
                update = app[c, z] - (
                    weights[1] * carry[owner, at : at + 1, :]
                    + weights[0] * carry[owner, rows + at : rows + at + 1, :]
                )
                app[c, z] = update
                masses[c] = masses[c] + fold(update * update)
        levels_here = pl.ds(owner * per, per)
        pltpu.make_async_copy(app.at[:, levels_here], out_hbm.at[:, levels_here], out_sem).start()
        return tuple(masses)

    masses = lax.fori_loop(0, owners, update_owner, (zero,) * comps)
    own = lane_of(masses)
    mass_send[0] = own
    mass_recv[0] = own
    spread(mass_send, mass_recv, 3)
    totals = gathered(mass_recv, 3, comps)
    for c in range(comps):
        ratio = jnp.sqrt(mean_square[c] / (totals[c] / cells + EPS))
        ratio_ref[c : c + 1, :] = jnp.broadcast_to(ratio, (1, lanes))

    @pl.when(gx < owners)
    def _():
        wait_bytes(tip_send.at[pl.ds(0, owners - 1)], send_sem.at[0])
        wait_bytes(carry_send.at[pl.ds(1, groups - 1)], send_sem.at[2])

    @pl.when(gx >= owners)
    def _():
        wait_bytes(tip_send, send_sem.at[0])

    wait_bytes(sums_recv.at[pl.ds(1, devices - 1)], send_sem.at[1])
    wait_bytes(mass_recv.at[pl.ds(1, devices - 1)], send_sem.at[3])
    pltpu.make_async_copy(app, out_hbm, out_sem).wait()


def shards(orbitals, potential, shift_ratio):
    groups = lax.axis_size("gx")
    columns = lax.axis_size("gy")
    comps, levels, width, lanes = orbitals.shape
    assert columns == 2 and lanes == LANES and 2 * comps * levels == lanes
    owners = min(groups, levels)
    rows = comps * (levels // owners)
    planes = comps * levels
    devices = groups * columns
    line_cells = width * groups
    cells = float(levels * line_cells * lanes * columns)
    sigma = shift_ratio[0] / float(line_cells * line_cells)
    decay = jnp.log1p(sigma + jnp.sqrt(sigma * (sigma + 2.0)))
    gain = TAU * jnp.tanh(0.5 * decay)
    params = jnp.stack(
        [
            decay,
            gain,
            gain * jnp.exp(-decay),
            jnp.exp(-decay * width),
            -1.0 / jnp.expm1(-decay * line_cells),
        ]
    )
    f32 = jnp.float32
    update, ratio = pl.pallas_call(
        functools.partial(step_kernel, groups, owners, cells),
        out_shape=(
            jax.ShapeDtypeStruct(orbitals.shape, f32),
            jax.ShapeDtypeStruct((comps, lanes), f32),
        ),
        in_specs=[
            pl.BlockSpec(memory_space=pltpu.SMEM),
            pl.BlockSpec(memory_space=pl.ANY),
            pl.BlockSpec(memory_space=pl.ANY),
        ],
        out_specs=(
            pl.BlockSpec(memory_space=pl.ANY),
            pl.BlockSpec(memory_space=pltpu.VMEM),
        ),
        scratch_shapes=[
            pltpu.VMEM(orbitals.shape, f32),
            pltpu.VMEM(potential.shape, f32),
            pltpu.VMEM(orbitals.shape, f32),
            pltpu.VMEM((width, 3 * width), jnp.bfloat16),
            pltpu.VMEM((2, width, lanes), f32),
            pltpu.VMEM((2, planes, lanes), f32),
            pltpu.VMEM((2, planes, lanes), f32),
            pltpu.VMEM((width, lanes), f32),
            pltpu.VMEM((width, lanes), f32),
            pltpu.VMEM((owners, 4 * rows, lanes), f32),
            pltpu.VMEM((groups, 4 * rows, lanes), f32),
            pltpu.VMEM((groups, 2 * rows, lanes), f32),
            pltpu.VMEM((owners, 2 * rows, lanes), f32),
            pltpu.VMEM((1, 1, lanes), f32),
            pltpu.VMEM((devices, 1, lanes), f32),
            pltpu.VMEM((1, 1, lanes), f32),
            pltpu.VMEM((devices, 1, lanes), f32),
            pltpu.SemaphoreType.DMA((2,)),
            pltpu.SemaphoreType.DMA((3,)),
            pltpu.SemaphoreType.DMA((3,)),
            pltpu.SemaphoreType.DMA((4,)),
            pltpu.SemaphoreType.DMA((4,)),
            pltpu.SemaphoreType.DMA,
        ],
        compiler_params=pltpu.CompilerParams(
            collective_id=0, has_side_effects=True, vmem_limit_bytes=32 * 1024 * 1024
        ),
        name="power_step",
    )(params, orbitals, potential)
    return update * ratio[:, None, None, :]


def solution(mesh):
    in_specs = (P(None, None, "gx", "gy"), P(None, "gx", "gy"), P())
    out_specs = P(None, None, "gx", "gy")
    return jax.shard_map(shards, mesh=mesh, in_specs=in_specs, out_specs=out_specs, check_vma=False)
```

```python
import functools

import jax
import jax.numpy as jnp
from jax import lax
from jax.experimental import pallas as pl
from jax.experimental.pallas import tpu as pltpu
from jax.sharding import PartitionSpec as P

TAU = 4.0
EPS = 1e-06
COUPLING_FIRST = 0.06
COUPLING_SECOND = 0.05
COUPLING_CROSS = 0.04
MESH = pl.DeviceIdType.MESH
LANES = 128
CHUNKS = 4


def wait_bytes(ref, sem):
    pltpu.make_async_copy(ref, ref, sem).wait()


def step_kernel(
    groups,
    owners,
    cells,
    params,
    orb_hbm,
    pot_hbm,
    out_hbm,
    ratio_ref,
    orb,
    pot,
    app,
    shift,
    table,
    weights,
    x_send,
    x_halo,
    y_send,
    y_halo,
    tips_ref,
    tip_send,
    tip_recv,
    carry_send,
    carry,
    sums_send,
    sums_recv,
    mass_send,
    mass_recv,
    load_sem,
    halo_send_sem,
    halo_recv_sem,
    send_sem,
    recv_sem,
    out_sem,
):
    comps, levels, width, lanes = orb.shape
    per = levels // owners
    early = shift.shape[1]
    rows = comps * per
    devices = 2 * groups
    gx = lax.axis_index("gx")
    gy = lax.axis_index("gy")
    lane = lax.broadcasted_iota(jnp.int32, (width, lanes), 1)
    row = lax.broadcasted_iota(jnp.int32, (width, lanes), 0)
    lane_row = lax.broadcasted_iota(jnp.int32, (1, lanes), 1)

    def peer(step):
        other = gx + step
        return jnp.where(other >= groups, other - groups, other)

    def device_at(step, side):
        return (peer(step), gy if side == 0 else 1 - gy)

    chunk = levels // CHUNKS
    loads = [
        pltpu.make_async_copy(
            orb_hbm.at[:, pl.ds(i * chunk, chunk)], orb.at[:, pl.ds(i * chunk, chunk)], load_sem.at[i]
        )
        for i in range(CHUNKS)
    ]
    loads.append(pltpu.make_async_copy(pot_hbm, pot, load_sem.at[CHUNKS]))
    for copy in loads:
        copy.start()

    barrier = pltpu.get_barrier_semaphore()

    def greet(step, _):
        for side in range(2):
            pl.semaphore_signal(barrier, inc=1, device_id=device_at(step, side), device_id_type=MESH)
        return 0

    pl.semaphore_signal(barrier, inc=1, device_id=(gx, 1 - gy), device_id_type=MESH)
    lax.fori_loop(1, groups, greet, 0)

    decay, gain, tip_gain, block, inv_wrap, edge = (params[i] for i in range(6))
    position = row.astype(jnp.float32)
    weights[0] = jnp.exp(-decay * (float(width - 1) - position))
    weights[1] = jnp.exp(-decay * position)
    t_row = lax.broadcasted_iota(jnp.int32, (width, 3 * width), 0)
    t_col = lax.broadcasted_iota(jnp.int32, (width, 3 * width), 1)
    t_mod = jnp.where(t_col >= 2 * width, t_col - 2 * width, jnp.where(t_col >= width, t_col - width, t_col))
    green = gain * jnp.exp(-decay * jnp.abs(t_row - t_mod).astype(jnp.float32))
    high = green.astype(jnp.bfloat16)
    low = (green - high.astype(jnp.float32)).astype(jnp.bfloat16)
    table[...] = jnp.where(t_col >= 2 * width, low.astype(jnp.float32), high.astype(jnp.float32)).astype(jnp.bfloat16)

    def pack(z, held):
        for c in range(comps):
            plane = orb[c, z]
            index = z * comps + c
            held = jnp.where(lane // 2 == index, pltpu.roll(plane, 2 * index + 1, 1), held)
            x_send[0, pl.ds(index, 1), :] = orb[c, z, width - 1 : width, :]
            x_send[1, pl.ds(index, 1), :] = orb[c, z, 0:1, :]
        return held

    held = jnp.zeros((width, lanes), jnp.float32)
    for i in range(CHUNKS):
        loads[i].wait()
        held = lax.fori_loop(i * chunk, (i + 1) * chunk, pack, held, unroll=2)
    y_send[...] = held

    pl.semaphore_wait(barrier, devices - 1)
    halos = [
        pltpu.make_async_remote_copy(
            src, dst, halo_send_sem.at[i], halo_recv_sem.at[i], device_id=target, device_id_type=MESH
        )
        for i, (src, dst, target) in enumerate(
            (
                (y_send, y_halo, (gx, 1 - gy)),
                (x_send.at[0], x_halo.at[0], (peer(1), gy)),
                (x_send.at[1], x_halo.at[1], (peer(groups - 1), gy)),
            )
        )
    ]
    for copy in halos:
        copy.start()
    loads[CHUNKS].wait()

    def fold(x):
        total = x[0:8]
        for i in range(8, width, 8):
            total = total + x[i : i + 8]
        return total

    def apply_level(z, sums):
        o = [orb[c, z] for c in range(comps)]
        before = lax.rem(z + levels - 1, levels)
        after = lax.rem(z + 1, levels)
        squares = [x * x for x in o]
        density = (
            COUPLING_FIRST * squares[0] + COUPLING_CROSS * squares[1],
            COUPLING_CROSS * squares[0] + COUPLING_SECOND * squares[1],
        )
        trap = pot[z] + 3.0
        result = []
        for c in range(comps):
            mine = o[c]
            near = pltpu.roll(mine, 1, 1) + pltpu.roll(mine, lanes - 1, 1)
            near = near + pltpu.roll(mine, 1, 0) + pltpu.roll(mine, width - 1, 0)
            near = near + orb[c, before] + orb[c, after]
            applied = (trap + density[c]) * mine - 0.5 * near
            app[c, z] = applied
            for i, x in enumerate((applied, mine)):
                for j in range(2):
                    tip = jnp.sum(fold(weights[j] * x), axis=0, keepdims=True)
                    tips_ref[2 * i + j, pl.ds(z * comps + c, 1), :] = tip
            result.append(sums[2 * c] + fold(mine * applied))
            result.append(sums[2 * c + 1] + fold(squares[c]))
        return tuple(result)

    zero = jnp.zeros((8, lanes), jnp.float32)
    sums = list(lax.fori_loop(0, levels, apply_level, (zero,) * (2 * comps), unroll=2))

    for copy in halos:
        copy.wait()
    lack = y_halo[...] - y_send[...]
    lack = jnp.where(lane % 2 == 0, pltpu.roll(lack, lanes - 1, 1), pltpu.roll(lack, 1, 1))
    y_halo[...] = lack
    x_lack = [x_halo[j] - x_send[j] for j in range(2)]
    for j in range(2):
        x_halo[j] = x_lack[j]
    x_cross = x_send[1] * x_lack[0] + x_send[0] * x_lack[1]
    y_cross = y_send[...] * lack
    for c in range(comps):
        more = jnp.where(row % comps == c, x_cross, 0.0) + jnp.where(lane // 2 % comps == c, y_cross, 0.0)
        sums[2 * c] = sums[2 * c] - 0.5 * fold(more)
    for j in range(2):
        ends = jnp.sum(fold(weights[j] * lack), axis=0, keepdims=True)
        last = jnp.sum(jnp.where(lane == 2 * row, ends, 0.0), axis=1, keepdims=True)
        first = jnp.sum(jnp.where(lane == 2 * row + 1, ends, 0.0), axis=1, keepdims=True)
        more = jnp.where(lane == 0, first, jnp.where(lane == lanes - 1, last, 0.0))
        more = more + x_lack[1 - j] + edge * x_lack[j]
        tips_ref[j] = tips_ref[j] - 0.5 * more

    def lane_of(values):
        packed = jnp.zeros((1, lanes), jnp.float32)
        for i, x in enumerate(values):
            whole = jnp.sum(jnp.sum(x, axis=0, keepdims=True), axis=1, keepdims=True)
            packed = jnp.where(lane_row == i, whole, packed)
        return packed

    def spread(source, target, which):
        def copy_to(slot, device):
            pltpu.make_async_remote_copy(
                source.at[0],
                target.at[slot],
                send_sem.at[which],
                recv_sem.at[which],
                device_id=device,
                device_id_type=MESH,
            ).start()

        def send(step, _):
            for side in range(2):
                copy_to(2 * (groups - step) + side, device_at(step, side))
            return 0

        copy_to(1, (gx, 1 - gy))
        lax.fori_loop(1, groups, send, 0)

    def gathered(target, which, count):
        wait_bytes(target.at[pl.ds(1, devices - 1)], recv_sem.at[which])
        total = jnp.sum(target[...], axis=0)
        return [
            jnp.sum(jnp.where(lane_row == i, total, 0.0), axis=1, keepdims=True) for i in range(count)
        ]

    own = lane_of(sums)
    sums_send[0] = own
    sums_recv[0] = own
    spread(sums_send, sums_recv, 1)

    def send_tips(step, _):
        owner = lax.rem(gx + 1 + step, owners)
        for q in range(4):
            tip_send[owner, q * rows : (q + 1) * rows, :] = tips_ref[q, pl.ds(owner * rows, rows), :]

        @pl.when(owner != gx)
        def _():
            pltpu.make_async_remote_copy(
                tip_send.at[owner],
                tip_recv.at[lax.rem(gx - owner + groups, groups)],
                send_sem.at[0],
                recv_sem.at[0],
                device_id=(owner, gy),
                device_id_type=MESH,
            ).start()

        return 0

    lax.fori_loop(0, owners, send_tips, 0)

    @pl.when(gx < owners)
    def _():
        tip_recv[0] = tip_send[lax.rem(gx, owners)]

    def split_dot(fields):
        wide = jnp.concatenate(fields, axis=1)
        high = wide.astype(jnp.bfloat16)
        low = (wide - high.astype(jnp.float32)).astype(jnp.bfloat16)
        local = jnp.dot(
            table[...], jnp.concatenate([high, low, high], axis=0), preferred_element_type=jnp.float32
        )
        return [local[:, i * lanes : (i + 1) * lanes] for i in range(len(fields))]

    def whole_applied(c, z):
        index = z * comps + c
        ends = pltpu.roll(y_halo[...], lanes - 1 - 2 * index, 1)
        ends = jnp.where((lane == 0) | (lane == lanes - 1), ends, 0.0)
        ends = ends + jnp.where(row == 0, x_halo[0, pl.ds(index, 1), :], 0.0)
        ends = ends + jnp.where(row == width - 1, x_halo[1, pl.ds(index, 1), :], 0.0)
        return app[c, z] - 0.5 * ends

    def solve_early(z, _):
        o = [orb[c, z] for c in range(comps)]
        local = split_dot([whole_applied(c, z) for c in range(comps)] + o)
        for c in range(comps):
            app[c, z] = o[c] - local[c]
            shift[c, z] = local[comps + c]
        return 0

    lax.fori_loop(0, early, solve_early, 0, unroll=2)

    totals = gathered(sums_recv, 1, 2 * comps)
    mean_square = [totals[2 * c + 1] / cells for c in range(comps)]
    energy = [totals[2 * c] / cells / (mean_square[c] + EPS) for c in range(comps)]

    @pl.when(gx < owners)
    def _():
        wait_bytes(tip_recv.at[pl.ds(1, groups - 1)], recv_sem.at[0])
        tip_row = lax.broadcasted_iota(jnp.int32, (2 * rows, lanes), 0)
        scale = jnp.where(tip_row % 2 == 0, energy[0], energy[1])

        def tips(k):
            return tip_recv[k, 0 : 2 * rows, :] - scale * tip_recv[k, 2 * rows : 4 * rows, :]

        def collect(k, held):
            ahead, behind = held
            return block * ahead + tips(k), block * behind + tips(groups - 1 - k)

        start = jnp.zeros((2 * rows, lanes), jnp.float32)
        ahead, behind = lax.fori_loop(0, groups, collect, (start, start))

        def hand_out(k, held):
            ahead, behind = held
            back = groups - 1 - k
            carry_send[k, 0:rows, :] = ahead[0:rows]
            carry_send[back, rows : 2 * rows, :] = behind[rows : 2 * rows]
            return block * ahead + tip_gain * tips(k), block * behind + tip_gain * tips(back)

        factor = tip_gain * inv_wrap
        lax.fori_loop(0, groups, hand_out, (factor * ahead, factor * behind))

        def send(step, _):
            pltpu.make_async_remote_copy(
                carry_send.at[step],
                carry.at[gx],
                send_sem.at[2],
                recv_sem.at[2],
                device_id=(peer(step), gy),
                device_id_type=MESH,
            ).start()
            return 0

        lax.fori_loop(1, groups, send, 0)
        carry[lax.rem(gx, owners)] = carry_send[0]

    def solve_late(z, _):
        o = [orb[c, z] for c in range(comps)]
        local = split_dot([whole_applied(c, z) - energy[c] * o[c] for c in range(comps)])
        for c in range(comps):
            app[c, z] = o[c] - local[c]
        return 0

    lax.fori_loop(early, levels, solve_late, 0, unroll=2)

    @pl.when(gx < owners)
    def _():
        wait_bytes(carry.at[pl.ds(0, owners - 1)], recv_sem.at[2])

    @pl.when(gx >= owners)
    def _():
        wait_bytes(carry, recv_sem.at[2])

    def update_owner(is_early, owner, masses):
        masses = list(masses)
        for local in range(per):
            z = owner * per + local
            for c in range(comps):
                at = local * comps + c
                update = app[c, z]
                if is_early:
                    update = update + energy[c] * shift[c, z]
                update = update - (
                    weights[1] * carry[owner, at : at + 1, :]
                    + weights[0] * carry[owner, rows + at : rows + at + 1, :]
                )
                app[c, z] = update
                masses[c] = masses[c] + fold(update * update)
        levels_here = pl.ds(owner * per, per)
        pltpu.make_async_copy(app.at[:, levels_here], out_hbm.at[:, levels_here], out_sem).start()
        return tuple(masses)

    masses = lax.fori_loop(0, early // per, functools.partial(update_owner, True), (zero,) * comps)
    masses = lax.fori_loop(early // per, owners, functools.partial(update_owner, False), masses)
    own = lane_of(masses)
    mass_send[0] = own
    mass_recv[0] = own
    spread(mass_send, mass_recv, 3)
    totals = gathered(mass_recv, 3, comps)
    for c in range(comps):
        ratio = jnp.sqrt(mean_square[c] / (totals[c] / cells + EPS))
        ratio_ref[c : c + 1, :] = jnp.broadcast_to(ratio, (1, lanes))

    @pl.when(gx < owners)
    def _():
        wait_bytes(tip_send.at[pl.ds(0, owners - 1)], send_sem.at[0])
        wait_bytes(carry_send.at[pl.ds(1, groups - 1)], send_sem.at[2])

    @pl.when(gx >= owners)
    def _():
        wait_bytes(tip_send, send_sem.at[0])

    wait_bytes(sums_recv.at[pl.ds(1, devices - 1)], send_sem.at[1])
    wait_bytes(mass_recv.at[pl.ds(1, devices - 1)], send_sem.at[3])
    pltpu.make_async_copy(app, out_hbm, out_sem).wait()


def shards(orbitals, potential, shift_ratio):
    groups = lax.axis_size("gx")
    columns = lax.axis_size("gy")
    comps, levels, width, lanes = orbitals.shape
    assert columns == 2 and lanes == LANES and 2 * comps * levels == lanes
    assert comps * levels == width
    owners = min(groups, levels)
    rows = comps * (levels // owners)
    early = levels // 2
    planes = comps * levels
    devices = groups * columns
    line_cells = width * groups
    cells = float(levels * line_cells * lanes * columns)
    sigma = shift_ratio[0] / float(line_cells * line_cells)
    decay = jnp.log1p(sigma + jnp.sqrt(sigma * (sigma + 2.0)))
    gain = TAU * jnp.tanh(0.5 * decay)
    params = jnp.stack(
        [
            decay,
            gain,
            gain * jnp.exp(-decay),
            jnp.exp(-decay * width),
            -1.0 / jnp.expm1(-decay * line_cells),
            jnp.exp(-decay * (width - 1)),
        ]
    )
    f32 = jnp.float32
    update, ratio = pl.pallas_call(
        functools.partial(step_kernel, groups, owners, cells),
        out_shape=(
            jax.ShapeDtypeStruct(orbitals.shape, f32),
            jax.ShapeDtypeStruct((comps, lanes), f32),
        ),
        in_specs=[
            pl.BlockSpec(memory_space=pltpu.SMEM),
            pl.BlockSpec(memory_space=pl.ANY),
            pl.BlockSpec(memory_space=pl.ANY),
        ],
        out_specs=(
            pl.BlockSpec(memory_space=pl.ANY),
            pl.BlockSpec(memory_space=pltpu.VMEM),
        ),
        scratch_shapes=[
            pltpu.VMEM(orbitals.shape, f32),
            pltpu.VMEM(potential.shape, f32),
            pltpu.VMEM(orbitals.shape, f32),
            pltpu.VMEM((comps, early, width, lanes), f32),
            pltpu.VMEM((width, 3 * width), jnp.bfloat16),
            pltpu.VMEM((2, width, lanes), f32),
            pltpu.VMEM((2, planes, lanes), f32),
            pltpu.VMEM((2, planes, lanes), f32),
            pltpu.VMEM((width, lanes), f32),
            pltpu.VMEM((width, lanes), f32),
            pltpu.VMEM((4, planes, lanes), f32),
            pltpu.VMEM((owners, 4 * rows, lanes), f32),
            pltpu.VMEM((groups, 4 * rows, lanes), f32),
            pltpu.VMEM((groups, 2 * rows, lanes), f32),
            pltpu.VMEM((owners, 2 * rows, lanes), f32),
            pltpu.VMEM((1, 1, lanes), f32),
            pltpu.VMEM((devices, 1, lanes), f32),
            pltpu.VMEM((1, 1, lanes), f32),
            pltpu.VMEM((devices, 1, lanes), f32),
            pltpu.SemaphoreType.DMA((CHUNKS + 1,)),
            pltpu.SemaphoreType.DMA((3,)),
            pltpu.SemaphoreType.DMA((3,)),
            pltpu.SemaphoreType.DMA((4,)),
            pltpu.SemaphoreType.DMA((4,)),
            pltpu.SemaphoreType.DMA,
        ],
        compiler_params=pltpu.CompilerParams(
            collective_id=0, has_side_effects=True
        ),
        name="power_step",
    )(params, orbitals, potential)
    return update * ratio[:, None, None, :]


def solution(mesh):
    in_specs = (P(None, None, "gx", "gy"), P(None, "gx", "gy"), P())
    out_specs = P(None, None, "gx", "gy")
    return jax.shard_map(shards, mesh=mesh, in_specs=in_specs, out_specs=out_specs, check_vma=False)
```

```python
import functools

import jax
import jax.numpy as jnp
from jax import lax
from jax.experimental import pallas as pl
from jax.experimental.pallas import tpu as pltpu
from jax.sharding import PartitionSpec as P

TAU = 4.0
EPS = 1e-06
COUPLING_FIRST = 0.06
COUPLING_SECOND = 0.05
COUPLING_CROSS = 0.04
MESH = pl.DeviceIdType.MESH
LANES = 128
CHUNKS = 4


def wait_bytes(ref, sem):
    pltpu.make_async_copy(ref, ref, sem).wait()


def step_kernel(
    groups,
    owners,
    cells,
    shift_ratio,
    orb_hbm,
    pot_hbm,
    out_hbm,
    ratio_ref,
    orb,
    pot,
    app,
    shift,
    table,
    weights,
    x_send,
    x_halo,
    y_send,
    y_halo,
    tips_ref,
    moments,
    tip_send,
    tip_recv,
    carry_send,
    carry,
    sums_send,
    sums_recv,
    mass_send,
    mass_recv,
    load_sem,
    halo_send_sem,
    halo_recv_sem,
    send_sem,
    recv_sem,
    out_sem,
):
    comps, levels, width, lanes = orb.shape
    per = levels // owners
    early = shift.shape[1]
    rows = comps * per
    devices = 2 * groups
    gx = lax.axis_index("gx")
    gy = lax.axis_index("gy")
    lane = lax.broadcasted_iota(jnp.int32, (width, lanes), 1)
    row = lax.broadcasted_iota(jnp.int32, (width, lanes), 0)
    lane_row = lax.broadcasted_iota(jnp.int32, (1, lanes), 1)

    def peer(step):
        other = gx + step
        return jnp.where(other >= groups, other - groups, other)

    def device_at(step, side):
        return (peer(step), gy if side == 0 else 1 - gy)

    chunk = levels // CHUNKS
    loads = [
        pltpu.make_async_copy(
            orb_hbm.at[:, pl.ds(i * chunk, chunk)], orb.at[:, pl.ds(i * chunk, chunk)], load_sem.at[i]
        )
        for i in range(CHUNKS)
    ]
    loads.append(pltpu.make_async_copy(pot_hbm, pot, load_sem.at[CHUNKS]))
    for copy in loads:
        copy.start()

    barrier = pltpu.get_barrier_semaphore()

    def greet(step, _):
        for side in range(2):
            pl.semaphore_signal(barrier, inc=1, device_id=device_at(step, side), device_id_type=MESH)
        return 0

    pl.semaphore_signal(barrier, inc=1, device_id=(gx, 1 - gy), device_id_type=MESH)
    lax.fori_loop(1, groups, greet, 0)

    line_cells = width * groups
    sigma_wide = jnp.full((1, 2 * lanes), shift_ratio[0] / float(line_cells * line_cells), jnp.float32)
    decay_wide = jnp.log1p(sigma_wide + jnp.sqrt(sigma_wide * (sigma_wide + 2.0)))
    gain_wide = TAU * jnp.sqrt(sigma_wide / (sigma_wide + 2.0))
    sigma, decay, gain = (x[:, :lanes] for x in (sigma_wide, decay_wide, gain_wide))
    tip_gain = gain * jnp.exp(-decay)
    block = jnp.exp(-decay * float(width))
    inv_wrap = 1.0 / (1.0 - jnp.exp(-decay * float(line_cells)))
    edge = jnp.exp(-decay * float(width - 1))
    eight = jnp.exp(-8.0 * decay)
    keep = 1.0 - TAU * sigma
    position = row.astype(jnp.float32)
    weights[0] = jnp.exp(-decay * (float(width - 1) - position))
    weights[1] = jnp.exp(-decay * position)
    near_last = weights[0, width - 8 : width, :]
    near_first = weights[1, 0:8, :]
    t_row = lax.broadcasted_iota(jnp.int32, (width, 3 * width), 0)
    t_col = lax.broadcasted_iota(jnp.int32, (width, 3 * width), 1)
    t_mod = jnp.where(t_col >= 2 * width, t_col - 2 * width, jnp.where(t_col >= width, t_col - width, t_col))
    distance = jnp.abs(t_row - t_mod).astype(jnp.float32)
    green = gain_wide[:, : 3 * width] * jnp.exp(-decay_wide[:, : 3 * width] * distance)
    high = green.astype(jnp.bfloat16)
    low = (green - high.astype(jnp.float32)).astype(jnp.bfloat16)
    table[...] = jnp.where(t_col >= 2 * width, low.astype(jnp.float32), high.astype(jnp.float32)).astype(jnp.bfloat16)

    def pack(z, held):
        for c in range(comps):
            plane = orb[c, z]
            index = z * comps + c
            held = jnp.where(lane // 2 == index, pltpu.roll(plane, 2 * index + 1, 1), held)
            x_send[0, pl.ds(index, 1), :] = orb[c, z, width - 1 : width, :]
            x_send[1, pl.ds(index, 1), :] = orb[c, z, 0:1, :]
        return held

    held = jnp.zeros((width, lanes), jnp.float32)
    for i in range(CHUNKS):
        loads[i].wait()
        held = lax.fori_loop(i * chunk, (i + 1) * chunk, pack, held, unroll=4)
    y_send[...] = held

    pl.semaphore_wait(barrier, devices - 1)
    halos = [
        pltpu.make_async_remote_copy(
            src, dst, halo_send_sem.at[i], halo_recv_sem.at[i], device_id=target, device_id_type=MESH
        )
        for i, (src, dst, target) in enumerate(
            (
                (y_send, y_halo, (gx, 1 - gy)),
                (x_send.at[1], x_halo, (peer(groups - 1), gy)),
            )
        )
    ]
    for copy in halos:
        copy.start()
    loads[CHUNKS].wait()

    def fold(x):
        total = x[0:8]
        for i in range(8, width, 8):
            total = total + x[i : i + 8]
        return total

    def weighted(x):
        parts = [x[i : i + 8] for i in range(0, width, 8)]
        to_last, to_first = parts[0], parts[-1]
        for i in range(1, len(parts)):
            to_last = to_last * eight + parts[i]
            to_first = to_first * eight + parts[-1 - i]
        return (
            jnp.sum(to_last * near_last, axis=0, keepdims=True),
            jnp.sum(to_first * near_first, axis=0, keepdims=True),
        )

    def apply_level(z, sums):
        o = [orb[c, z] for c in range(comps)]
        before = lax.rem(z + levels - 1, levels)
        after = lax.rem(z + 1, levels)
        squares = [x * x for x in o]
        density = (
            COUPLING_FIRST * squares[0] + COUPLING_CROSS * squares[1],
            COUPLING_CROSS * squares[0] + COUPLING_SECOND * squares[1],
        )
        trap = pot[z] + 2.0
        result = []
        for c in range(comps):
            mine = o[c]
            near = pltpu.roll(mine, 1, 1) + pltpu.roll(mine, lanes - 1, 1)
            near = near + orb[c, before] + orb[c, after]
            applied = (trap + density[c]) * mine - 0.5 * near
            app[c, z] = applied
            for i, x in enumerate((applied, mine)):
                for j, tip in enumerate(weighted(x)):
                    tips_ref[2 * i + j, pl.ds(z * comps + c, 1), :] = tip
            along = mine - pltpu.roll(mine, width - 1, 0)
            result.append(sums[2 * c] + fold(mine * (applied + along)))
            result.append(sums[2 * c + 1] + fold(squares[c]))
        return tuple(result)

    zero = jnp.zeros((8, lanes), jnp.float32)
    sums = list(lax.fori_loop(0, levels, apply_level, (zero,) * (2 * comps), unroll=2))

    for copy in halos:
        copy.wait()
    lack = y_halo[...] - y_send[...]
    lack = jnp.where(lane % 2 == 0, pltpu.roll(lack, lanes - 1, 1), pltpu.roll(lack, 1, 1))
    y_halo[...] = lack
    x_cross = x_send[0] * (x_halo[...] - x_send[1])
    y_cross = y_send[...] * lack
    for c in range(comps):
        sums[2 * c] = sums[2 * c] - fold(jnp.where(row % comps == c, x_cross, 0.0))
        sums[2 * c] = sums[2 * c] - 0.5 * fold(jnp.where(lane // 2 % comps == c, y_cross, 0.0))
    for j in range(2):
        ends = jnp.sum(fold(weights[j] * lack), axis=0, keepdims=True)
        last = jnp.sum(jnp.where(lane == 2 * row, ends, 0.0), axis=1, keepdims=True)
        first = jnp.sum(jnp.where(lane == 2 * row + 1, ends, 0.0), axis=1, keepdims=True)
        more = jnp.where(lane == 0, first, jnp.where(lane == lanes - 1, last, 0.0))
        tips_ref[j] = tips_ref[j] - 0.5 * more

    def lane_of(values):
        packed = jnp.zeros((1, lanes), jnp.float32)
        for i, x in enumerate(values):
            whole = jnp.sum(jnp.sum(x, axis=0, keepdims=True), axis=1, keepdims=True)
            packed = jnp.where(lane_row == i, whole, packed)
        return packed

    def spread(source, target, which):
        def copy_to(slot, device):
            pltpu.make_async_remote_copy(
                source.at[0],
                target.at[slot],
                send_sem.at[which],
                recv_sem.at[which],
                device_id=device,
                device_id_type=MESH,
            ).start()

        def send(step, _):
            for side in range(2):
                copy_to(2 * (groups - step) + side, device_at(step, side))
            return 0

        copy_to(1, (gx, 1 - gy))
        lax.fori_loop(1, groups, send, 0)

    def gathered(target, which, count):
        wait_bytes(target.at[pl.ds(1, devices - 1)], recv_sem.at[which])
        total = jnp.sum(target[...], axis=0)
        return [
            jnp.sum(jnp.where(lane_row == i, total, 0.0), axis=1, keepdims=True) for i in range(count)
        ]

    own = lane_of(sums)
    sums_send[0] = own
    sums_recv[0] = own
    def send_tips(step, _):
        owner = lax.rem(gx + 1 + step, owners)
        for q in range(4):
            tip_send[owner, q * rows : (q + 1) * rows, :] = tips_ref[q, pl.ds(owner * rows, rows), :]

        @pl.when(owner != gx)
        def _():
            pltpu.make_async_remote_copy(
                tip_send.at[owner],
                tip_recv.at[lax.rem(gx - owner + groups, groups)],
                send_sem.at[0],
                recv_sem.at[0],
                device_id=(owner, gy),
                device_id_type=MESH,
            ).start()

        return 0

    lax.fori_loop(0, owners, send_tips, 0)
    spread(sums_send, sums_recv, 1)

    @pl.when(gx < owners)
    def _():
        tip_recv[0] = tip_send[lax.rem(gx, owners)]

    def split_dot(fields):
        wide = jnp.concatenate(fields, axis=1)
        high = wide.astype(jnp.bfloat16)
        low = (wide - high.astype(jnp.float32)).astype(jnp.bfloat16)
        local = jnp.dot(
            table[...], jnp.concatenate([high, low, high], axis=0), preferred_element_type=jnp.float32
        )
        return [local[:, i * lanes : (i + 1) * lanes] for i in range(len(fields))]

    def whole_applied(c, z):
        index = z * comps + c
        ends = pltpu.roll(y_halo[...], lanes - 1 - 2 * index, 1)
        ends = jnp.where((lane == 0) | (lane == lanes - 1), ends, 0.0)
        return app[c, z] - 0.5 * ends

    def solve_early(z, _):
        o = [orb[c, z] for c in range(comps)]
        local = split_dot([whole_applied(c, z) for c in range(comps)] + o)
        for c in range(comps):
            app[c, z] = keep * o[c] - local[c]
            shift[c, z] = local[comps + c]
        return 0

    lax.fori_loop(0, early, solve_early, 0, unroll=2)

    totals = gathered(sums_recv, 1, 2 * comps)
    mean_square = [totals[2 * c + 1] / cells for c in range(comps)]
    energy = [totals[2 * c] / cells / (mean_square[c] + EPS) + sigma for c in range(comps)]

    @pl.when(gx < owners)
    def _():
        wait_bytes(tip_recv.at[pl.ds(1, groups - 1)], recv_sem.at[0])
        tip_row = lax.broadcasted_iota(jnp.int32, (2 * rows, lanes), 0)
        scale = jnp.where(tip_row % 2 == 0, energy[0], energy[1])

        def tips(k):
            return tip_recv[k, 0 : 2 * rows, :] - scale * tip_recv[k, 2 * rows : 4 * rows, :]

        def collect(k, held):
            ahead, behind = held
            return block * ahead + tips(k), block * behind + tips(groups - 1 - k)

        start = jnp.zeros((2 * rows, lanes), jnp.float32)
        ahead, behind = lax.fori_loop(0, groups, collect, (start, start))

        def hand_out(k, held):
            ahead, behind = held
            back = groups - 1 - k
            carry_send[k, 0:rows, :] = ahead[0:rows]
            carry_send[back, rows : 2 * rows, :] = behind[rows : 2 * rows]
            return block * ahead + tip_gain * tips(k), block * behind + tip_gain * tips(back)

        factor = tip_gain * inv_wrap
        lax.fori_loop(0, groups, hand_out, (factor * ahead, factor * behind))

        def send(step, _):
            pltpu.make_async_remote_copy(
                carry_send.at[step],
                carry.at[gx],
                send_sem.at[2],
                recv_sem.at[2],
                device_id=(peer(step), gy),
                device_id_type=MESH,
            ).start()
            return 0

        lax.fori_loop(1, groups, send, 0)
        carry[lax.rem(gx, owners)] = carry_send[0]

    def finish(c, z, own, mass):
        app[c, z] = own
        to_last, to_first = weighted(own)
        moments[0, pl.ds(z * comps + c, 1), :] = to_first
        moments[1, pl.ds(z * comps + c, 1), :] = to_last
        return mass + fold(own * own)

    def finish_early(z, masses):
        return tuple(
            finish(c, z, app[c, z] + energy[c] * shift[c, z], masses[c]) for c in range(comps)
        )

    def solve_late(z, masses):
        o = [orb[c, z] for c in range(comps)]
        local = split_dot([whole_applied(c, z) - energy[c] * o[c] for c in range(comps)])
        return tuple(finish(c, z, keep * o[c] - local[c], masses[c]) for c in range(comps))

    masses = lax.fori_loop(0, early, finish_early, (zero,) * comps, unroll=2)
    masses = list(lax.fori_loop(early, levels, solve_late, masses, unroll=2))
    square = jnp.sum(weights[1] * weights[1], axis=0, keepdims=True)

    @pl.when(gx < owners)
    def _():
        wait_bytes(carry.at[pl.ds(0, owners - 1)], recv_sem.at[2])

    @pl.when(gx >= owners)
    def _():
        wait_bytes(carry, recv_sem.at[2])

    def join_mass(owner, held):
        forward, backward = carry[owner, 0:rows, :], carry[owner, rows : 2 * rows, :]
        here = pl.ds(owner * rows, rows)
        held = held + forward * (square * forward - 2.0 * moments[0, here, :])
        held = held + backward * (square * backward - 2.0 * moments[1, here, :])
        return held + 2.0 * float(width) * edge * forward * backward

    joined = lax.fori_loop(0, owners, join_mass, jnp.zeros((rows, lanes), jnp.float32), unroll=4)
    line_row = lax.broadcasted_iota(jnp.int32, (rows, lanes), 0)
    for c in range(comps):
        more = jnp.sum(jnp.where(line_row % comps == c, joined, 0.0), axis=0, keepdims=True)
        masses[c] = jnp.sum(masses[c], axis=0, keepdims=True) + more
    own = lane_of(masses)
    mass_send[0] = own
    mass_recv[0] = own
    spread(mass_send, mass_recv, 3)

    def update_owner(owner, _):
        for local in range(per):
            z = owner * per + local
            for c in range(comps):
                at = local * comps + c
                app[c, z] = app[c, z] - (
                    weights[1] * carry[owner, at : at + 1, :]
                    + weights[0] * carry[owner, rows + at : rows + at + 1, :]
                )
        levels_here = pl.ds(owner * per, per)
        pltpu.make_async_copy(app.at[:, levels_here], out_hbm.at[:, levels_here], out_sem).start()
        return 0

    lax.fori_loop(0, owners, update_owner, 0)
    totals = gathered(mass_recv, 3, comps)
    for c in range(comps):
        ratio = jnp.sqrt(mean_square[c] / (totals[c] / cells + EPS))
        ratio_ref[c : c + 1, :] = jnp.broadcast_to(ratio, (1, lanes))

    @pl.when(gx < owners)
    def _():
        wait_bytes(tip_send.at[pl.ds(0, owners - 1)], send_sem.at[0])
        wait_bytes(carry_send.at[pl.ds(1, groups - 1)], send_sem.at[2])

    @pl.when(gx >= owners)
    def _():
        wait_bytes(tip_send, send_sem.at[0])

    wait_bytes(sums_recv.at[pl.ds(1, devices - 1)], send_sem.at[1])
    wait_bytes(mass_recv.at[pl.ds(1, devices - 1)], send_sem.at[3])
    pltpu.make_async_copy(app, out_hbm, out_sem).wait()


def shards(orbitals, potential, shift_ratio):
    groups = lax.axis_size("gx")
    columns = lax.axis_size("gy")
    comps, levels, width, lanes = orbitals.shape
    assert columns == 2 and lanes == LANES and 2 * comps * levels == lanes
    assert comps * levels == width
    owners = min(groups, levels)
    rows = comps * (levels // owners)
    early = levels // 2
    planes = comps * levels
    devices = groups * columns
    cells = float(levels * width * groups * lanes * columns)
    f32 = jnp.float32
    update, ratio = pl.pallas_call(
        functools.partial(step_kernel, groups, owners, cells),
        out_shape=(
            jax.ShapeDtypeStruct(orbitals.shape, f32),
            jax.ShapeDtypeStruct((comps, lanes), f32),
        ),
        in_specs=[
            pl.BlockSpec(memory_space=pltpu.SMEM),
            pl.BlockSpec(memory_space=pltpu.HBM),
            pl.BlockSpec(memory_space=pltpu.HBM),
        ],
        out_specs=(
            pl.BlockSpec(memory_space=pl.ANY),
            pl.BlockSpec(memory_space=pltpu.VMEM),
        ),
        scratch_shapes=[
            pltpu.VMEM(orbitals.shape, f32),
            pltpu.VMEM(potential.shape, f32),
            pltpu.VMEM(orbitals.shape, f32),
            pltpu.VMEM((comps, early, width, lanes), f32),
            pltpu.VMEM((width, 3 * width), jnp.bfloat16),
            pltpu.VMEM((2, width, lanes), f32),
            pltpu.VMEM((2, planes, lanes), f32),
            pltpu.VMEM((planes, lanes), f32),
            pltpu.VMEM((width, lanes), f32),
            pltpu.VMEM((width, lanes), f32),
            pltpu.VMEM((4, planes, lanes), f32),
            pltpu.VMEM((2, planes, lanes), f32),
            pltpu.VMEM((owners, 4 * rows, lanes), f32),
            pltpu.VMEM((groups, 4 * rows, lanes), f32),
            pltpu.VMEM((groups, 2 * rows, lanes), f32),
            pltpu.VMEM((owners, 2 * rows, lanes), f32),
            pltpu.VMEM((1, 1, lanes), f32),
            pltpu.VMEM((devices, 1, lanes), f32),
            pltpu.VMEM((1, 1, lanes), f32),
            pltpu.VMEM((devices, 1, lanes), f32),
            pltpu.SemaphoreType.DMA((CHUNKS + 1,)),
            pltpu.SemaphoreType.DMA((2,)),
            pltpu.SemaphoreType.DMA((2,)),
            pltpu.SemaphoreType.DMA((4,)),
            pltpu.SemaphoreType.DMA((4,)),
            pltpu.SemaphoreType.DMA,
        ],
        compiler_params=pltpu.CompilerParams(
            collective_id=0, has_side_effects=True, vmem_limit_bytes=32 * 1024 * 1024
        ),
        name="power_step",
    )(shift_ratio, orbitals, potential)
    return update * ratio[:, None, None, :]


def solution(mesh):
    in_specs = (P(None, None, "gx", "gy"), P(None, "gx", "gy"), P())
    out_specs = P(None, None, "gx", "gy")
    return jax.shard_map(shards, mesh=mesh, in_specs=in_specs, out_specs=out_specs, check_vma=False)
```

```python
import functools

import jax
import jax.numpy as jnp
from jax import lax
from jax.experimental import pallas as pl
from jax.experimental.pallas import tpu as pltpu
from jax.sharding import PartitionSpec as P

TAU = 4.0
EPS = 1e-06
COUPLING_FIRST = 0.06
COUPLING_SECOND = 0.05
COUPLING_CROSS = 0.04
MESH = pl.DeviceIdType.MESH
LANES = 128
CHUNKS = 4
GROUP = 4


def wait_bytes(ref, sem):
    pltpu.make_async_copy(ref, ref, sem).wait()


def step_kernel(
    groups,
    owners,
    cells,
    shift_ratio,
    orb_hbm,
    pot_hbm,
    out_hbm,
    ratio_ref,
    orb,
    pot,
    app,
    shift,
    table,
    weights,
    x_send,
    x_halo,
    y_send,
    y_halo,
    tips_ref,
    moments,
    tip_send,
    tip_recv,
    carry_send,
    carry,
    sums_send,
    sums_recv,
    mass_send,
    mass_recv,
    load_sem,
    halo_send_sem,
    halo_recv_sem,
    send_sem,
    recv_sem,
    out_sem,
):
    comps, levels, width, lanes = orb.shape
    per = levels // owners
    early = shift.shape[1]
    rows = comps * per
    devices = 2 * groups
    gx = lax.axis_index("gx")
    gy = lax.axis_index("gy")
    lane = lax.broadcasted_iota(jnp.int32, (width, lanes), 1)
    row = lax.broadcasted_iota(jnp.int32, (width, lanes), 0)
    lane_row = lax.broadcasted_iota(jnp.int32, (1, lanes), 1)

    def peer(step):
        other = gx + step
        return jnp.where(other >= groups, other - groups, other)

    def device_at(step, side):
        return (peer(step), gy if side == 0 else 1 - gy)

    chunk = levels // CHUNKS
    loads = [
        pltpu.make_async_copy(
            orb_hbm.at[:, pl.ds(i * chunk, chunk)], orb.at[:, pl.ds(i * chunk, chunk)], load_sem.at[i]
        )
        for i in range(CHUNKS)
    ]
    loads.append(pltpu.make_async_copy(pot_hbm, pot, load_sem.at[CHUNKS]))
    for copy in loads:
        copy.start()

    barrier = pltpu.get_barrier_semaphore()

    def greet(step, _):
        for side in range(2):
            pl.semaphore_signal(barrier, inc=1, device_id=device_at(step, side), device_id_type=MESH)
        return 0

    pl.semaphore_signal(barrier, inc=1, device_id=(gx, 1 - gy), device_id_type=MESH)
    lax.fori_loop(1, groups, greet, 0)

    line_cells = width * groups
    sigma_wide = jnp.full((1, 2 * lanes), shift_ratio[0] / float(line_cells * line_cells), jnp.float32)
    decay_wide = jnp.log1p(sigma_wide + jnp.sqrt(sigma_wide * (sigma_wide + 2.0)))
    gain_wide = TAU * jnp.sqrt(sigma_wide / (sigma_wide + 2.0))
    sigma, decay, gain = (x[:, :lanes] for x in (sigma_wide, decay_wide, gain_wide))
    tip_gain = gain * jnp.exp(-decay)
    block = jnp.exp(-decay * float(width))
    inv_wrap = 1.0 / (1.0 - jnp.exp(-decay * float(line_cells)))
    edge = jnp.exp(-decay * float(width - 1))
    eight = jnp.exp(-8.0 * decay)
    keep = 1.0 - TAU * sigma
    position = row.astype(jnp.float32)
    weights[0] = jnp.exp(-decay * (float(width - 1) - position))
    weights[1] = jnp.exp(-decay * position)
    near_last = weights[0, width - 8 : width, :]
    near_first = weights[1, 0:8, :]
    t_row = lax.broadcasted_iota(jnp.int32, (width, 3 * width), 0)
    t_col = lax.broadcasted_iota(jnp.int32, (width, 3 * width), 1)
    t_mod = jnp.where(t_col >= 2 * width, t_col - 2 * width, jnp.where(t_col >= width, t_col - width, t_col))
    distance = jnp.abs(t_row - t_mod).astype(jnp.float32)
    green = gain_wide[:, : 3 * width] * jnp.exp(-decay_wide[:, : 3 * width] * distance)
    high = green.astype(jnp.bfloat16)
    low = (green - high.astype(jnp.float32)).astype(jnp.bfloat16)
    table[...] = jnp.where(t_col >= 2 * width, low.astype(jnp.float32), high.astype(jnp.float32)).astype(jnp.bfloat16)

    def groups_of(size, first, last, body, held):
        return lax.fori_loop(0, (last - first) // size, lambda i, x: body(first + i * size, x), held)

    def pack(start, held):
        rows_out = []
        for i in range(GROUP):
            z = start + i
            for c in range(comps):
                plane = orb[c, z]
                index = z * comps + c
                held = jnp.where(lane // 2 == index, pltpu.roll(plane, 2 * index + 1, 1), held)
                rows_out.append((index, plane[width - 1 : width], plane[0:1]))
        for index, last, first in rows_out:
            x_send[0, pl.ds(index, 1), :] = last
            x_send[1, pl.ds(index, 1), :] = first
        return held

    held = jnp.zeros((width, lanes), jnp.float32)
    for i in range(CHUNKS):
        loads[i].wait()
        held = groups_of(GROUP, i * chunk, (i + 1) * chunk, pack, held)
    y_send[...] = held

    pl.semaphore_wait(barrier, devices - 1)
    halos = [
        pltpu.make_async_remote_copy(
            src, dst, halo_send_sem.at[i], halo_recv_sem.at[i], device_id=target, device_id_type=MESH
        )
        for i, (src, dst, target) in enumerate(
            (
                (y_send, y_halo, (gx, 1 - gy)),
                (x_send.at[1], x_halo, (peer(groups - 1), gy)),
            )
        )
    ]
    for copy in halos:
        copy.start()
    loads[CHUNKS].wait()

    def fold(x):
        total = x[0:8]
        for i in range(8, width, 8):
            total = total + x[i : i + 8]
        return total

    def weighted(x):
        parts = [x[i : i + 8] for i in range(0, width, 8)]
        to_last, to_first = parts[0], parts[-1]
        for i in range(1, len(parts)):
            to_last = to_last * eight + parts[i]
            to_first = to_first * eight + parts[-1 - i]
        return (
            jnp.sum(to_last * near_last, axis=0, keepdims=True),
            jnp.sum(to_first * near_first, axis=0, keepdims=True),
        )

    def apply_level(z, sums, stores):
        o = [orb[c, z] for c in range(comps)]
        before = lax.rem(z + levels - 1, levels)
        after = lax.rem(z + 1, levels)
        squares = [x * x for x in o]
        density = (
            COUPLING_FIRST * squares[0] + COUPLING_CROSS * squares[1],
            COUPLING_CROSS * squares[0] + COUPLING_SECOND * squares[1],
        )
        trap = pot[z] + 2.0
        result = []
        for c in range(comps):
            mine = o[c]
            near = pltpu.roll(mine, 1, 1) + pltpu.roll(mine, lanes - 1, 1)
            near = near + orb[c, before] + orb[c, after]
            applied = (trap + density[c]) * mine - 0.5 * near
            stores.append((c, z, applied, [tip for x in (applied, mine) for tip in weighted(x)]))
            along = mine - pltpu.roll(mine, width - 1, 0)
            result.append(sums[2 * c] + fold(mine * (applied + along)))
            result.append(sums[2 * c + 1] + fold(squares[c]))
        return tuple(result)

    def apply_pair(start, sums):
        stores = []
        for i in range(2):
            sums = apply_level(start + i, sums, stores)
        for c, z, applied, tips in stores:
            app[c, z] = applied
            for q, tip in enumerate(tips):
                tips_ref[q, pl.ds(z * comps + c, 1), :] = tip
        return sums

    zero = jnp.zeros((8, lanes), jnp.float32)
    sums = list(groups_of(2, 0, levels, apply_pair, (zero,) * (2 * comps)))

    for copy in halos:
        copy.wait()
    lack = y_halo[...] - y_send[...]
    lack = jnp.where(lane % 2 == 0, pltpu.roll(lack, lanes - 1, 1), pltpu.roll(lack, 1, 1))
    y_halo[...] = lack
    x_cross = x_send[0] * (x_halo[...] - x_send[1])
    y_cross = y_send[...] * lack
    for c in range(comps):
        sums[2 * c] = sums[2 * c] - fold(jnp.where(row % comps == c, x_cross, 0.0))
        sums[2 * c] = sums[2 * c] - 0.5 * fold(jnp.where(lane // 2 % comps == c, y_cross, 0.0))
    for j in range(2):
        ends = jnp.sum(fold(weights[j] * lack), axis=0, keepdims=True)
        last = jnp.sum(jnp.where(lane == 2 * row, ends, 0.0), axis=1, keepdims=True)
        first = jnp.sum(jnp.where(lane == 2 * row + 1, ends, 0.0), axis=1, keepdims=True)
        more = jnp.where(lane == 0, first, jnp.where(lane == lanes - 1, last, 0.0))
        tips_ref[j] = tips_ref[j] - 0.5 * more

    def lane_of(values):
        packed = jnp.zeros((1, lanes), jnp.float32)
        for i, x in enumerate(values):
            whole = jnp.sum(jnp.sum(x, axis=0, keepdims=True), axis=1, keepdims=True)
            packed = jnp.where(lane_row == i, whole, packed)
        return packed

    def spread(source, target, which):
        def copy_to(slot, device):
            pltpu.make_async_remote_copy(
                source.at[0],
                target.at[slot],
                send_sem.at[which],
                recv_sem.at[which],
                device_id=device,
                device_id_type=MESH,
            ).start()

        def send(step, _):
            for side in range(2):
                copy_to(2 * (groups - step) + side, device_at(step, side))
            return 0

        copy_to(1, (gx, 1 - gy))
        lax.fori_loop(1, groups, send, 0)

    def gathered(target, which, count):
        wait_bytes(target.at[pl.ds(1, devices - 1)], recv_sem.at[which])
        total = jnp.sum(target[...], axis=0)
        return [
            jnp.sum(jnp.where(lane_row == i, total, 0.0), axis=1, keepdims=True) for i in range(count)
        ]

    own = lane_of(sums)
    sums_send[0] = own
    sums_recv[0] = own
    def send_tips(step, _):
        owner = lax.rem(gx + 1 + step, owners)
        for q in range(4):
            tip_send[owner, q * rows : (q + 1) * rows, :] = tips_ref[q, pl.ds(owner * rows, rows), :]

        @pl.when(owner != gx)
        def _():
            pltpu.make_async_remote_copy(
                tip_send.at[owner],
                tip_recv.at[lax.rem(gx - owner + groups, groups)],
                send_sem.at[0],
                recv_sem.at[0],
                device_id=(owner, gy),
                device_id_type=MESH,
            ).start()

        return 0

    lax.fori_loop(0, owners, send_tips, 0)
    spread(sums_send, sums_recv, 1)

    @pl.when(gx < owners)
    def _():
        tip_recv[0] = tip_send[lax.rem(gx, owners)]

    def split_dot(fields):
        wide = jnp.concatenate(fields, axis=1)
        high = wide.astype(jnp.bfloat16)
        low = (wide - high.astype(jnp.float32)).astype(jnp.bfloat16)
        local = jnp.dot(
            table[...], jnp.concatenate([high, low, high], axis=0), preferred_element_type=jnp.float32
        )
        return [local[:, i * lanes : (i + 1) * lanes] for i in range(len(fields))]

    def whole_applied(c, z):
        index = z * comps + c
        ends = pltpu.roll(y_halo[...], lanes - 1 - 2 * index, 1)
        ends = jnp.where((lane == 0) | (lane == lanes - 1), ends, 0.0)
        return app[c, z] - 0.5 * ends

    def solve_early(start, _):
        places = [(c, start + i) for i in range(GROUP) for c in range(comps)]
        o = [orb[c, z] for c, z in places]
        local = split_dot([whole_applied(c, z) for c, z in places] + o)
        for i, (c, z) in enumerate(places):
            app[c, z] = keep * o[i] - local[i]
            shift[c, z] = local[len(places) + i]
        return 0

    groups_of(GROUP, 0, early, solve_early, 0)

    totals = gathered(sums_recv, 1, 2 * comps)
    mean_square = [totals[2 * c + 1] / cells for c in range(comps)]
    energy = [totals[2 * c] / cells / (mean_square[c] + EPS) + sigma for c in range(comps)]

    @pl.when(gx < owners)
    def _():
        wait_bytes(tip_recv.at[pl.ds(1, groups - 1)], recv_sem.at[0])
        tip_row = lax.broadcasted_iota(jnp.int32, (2 * rows, lanes), 0)
        scale = jnp.where(tip_row % 2 == 0, energy[0], energy[1])

        def tips(k):
            return tip_recv[k, 0 : 2 * rows, :] - scale * tip_recv[k, 2 * rows : 4 * rows, :]

        def collect(k, held):
            ahead, behind = held
            return block * ahead + tips(k), block * behind + tips(groups - 1 - k)

        start = jnp.zeros((2 * rows, lanes), jnp.float32)
        ahead, behind = lax.fori_loop(0, groups, collect, (start, start), unroll=4)

        def hand_out(k, held):
            ahead, behind = held
            back = groups - 1 - k
            carry_send[k, 0:rows, :] = ahead[0:rows]
            carry_send[back, rows : 2 * rows, :] = behind[rows : 2 * rows]
            return block * ahead + tip_gain * tips(k), block * behind + tip_gain * tips(back)

        factor = tip_gain * inv_wrap
        lax.fori_loop(0, groups, hand_out, (factor * ahead, factor * behind), unroll=4)

        def send(step, _):
            pltpu.make_async_remote_copy(
                carry_send.at[step],
                carry.at[gx],
                send_sem.at[2],
                recv_sem.at[2],
                device_id=(peer(step), gy),
                device_id_type=MESH,
            ).start()
            return 0

        lax.fori_loop(1, groups, send, 0)
        carry[lax.rem(gx, owners)] = carry_send[0]

    def finish(places, fields, masses):
        masses = list(masses)
        ends = []
        for (c, z), own in zip(places, fields):
            ends.append(weighted(own))
            masses[c] = masses[c] + fold(own * own)
        for (c, z), own, (to_last, to_first) in zip(places, fields, ends):
            app[c, z] = own
            moments[0, pl.ds(z * comps + c, 1), :] = to_first
            moments[1, pl.ds(z * comps + c, 1), :] = to_last
        return tuple(masses)

    def finish_early(start, masses):
        places = [(c, start + i) for i in range(2) for c in range(comps)]
        return finish(places, [app[c, z] + energy[c] * shift[c, z] for c, z in places], masses)

    def solve_late(start, masses):
        places = [(c, start + i) for i in range(GROUP) for c in range(comps)]
        o = [orb[c, z] for c, z in places]
        local = split_dot([whole_applied(c, z) - energy[c] * x for (c, z), x in zip(places, o)])
        return finish(places, [keep * x - y for x, y in zip(o, local)], masses)

    masses = groups_of(2, 0, early, finish_early, (zero,) * comps)
    masses = list(groups_of(GROUP, early, levels, solve_late, masses))
    square = jnp.sum(weights[1] * weights[1], axis=0, keepdims=True)

    @pl.when(gx < owners)
    def _():
        wait_bytes(carry.at[pl.ds(0, owners - 1)], recv_sem.at[2])

    @pl.when(gx >= owners)
    def _():
        wait_bytes(carry, recv_sem.at[2])

    def join_mass(owner, held):
        forward, backward = carry[owner, 0:rows, :], carry[owner, rows : 2 * rows, :]
        here = pl.ds(owner * rows, rows)
        held = held + forward * (square * forward - 2.0 * moments[0, here, :])
        held = held + backward * (square * backward - 2.0 * moments[1, here, :])
        return held + 2.0 * float(width) * edge * forward * backward

    joined = lax.fori_loop(0, owners, join_mass, jnp.zeros((rows, lanes), jnp.float32), unroll=4)
    line_row = lax.broadcasted_iota(jnp.int32, (rows, lanes), 0)
    for c in range(comps):
        more = jnp.sum(jnp.where(line_row % comps == c, joined, 0.0), axis=0, keepdims=True)
        masses[c] = jnp.sum(masses[c], axis=0, keepdims=True) + more
    own = lane_of(masses)
    mass_send[0] = own
    mass_recv[0] = own
    spread(mass_send, mass_recv, 3)

    def update_owner(owner, _):
        places = [(c, owner * per + local, local * comps + c) for local in range(per) for c in range(comps)]
        fields = [
            app[c, z]
            - (
                weights[1] * carry[owner, at : at + 1, :]
                + weights[0] * carry[owner, rows + at : rows + at + 1, :]
            )
            for c, z, at in places
        ]
        for (c, z, at), field in zip(places, fields):
            app[c, z] = field
        levels_here = pl.ds(owner * per, per)
        pltpu.make_async_copy(app.at[:, levels_here], out_hbm.at[:, levels_here], out_sem).start()
        return 0

    lax.fori_loop(0, owners, update_owner, 0)
    totals = gathered(mass_recv, 3, comps)
    for c in range(comps):
        ratio = jnp.sqrt(mean_square[c] / (totals[c] / cells + EPS))
        ratio_ref[c : c + 1, :] = jnp.broadcast_to(ratio, (1, lanes))

    @pl.when(gx < owners)
    def _():
        wait_bytes(tip_send.at[pl.ds(0, owners - 1)], send_sem.at[0])
        wait_bytes(carry_send.at[pl.ds(1, groups - 1)], send_sem.at[2])

    @pl.when(gx >= owners)
    def _():
        wait_bytes(tip_send, send_sem.at[0])

    wait_bytes(sums_recv.at[pl.ds(1, devices - 1)], send_sem.at[1])
    wait_bytes(mass_recv.at[pl.ds(1, devices - 1)], send_sem.at[3])
    pltpu.make_async_copy(app, out_hbm, out_sem).wait()


def shards(orbitals, potential, shift_ratio):
    groups = lax.axis_size("gx")
    columns = lax.axis_size("gy")
    comps, levels, width, lanes = orbitals.shape
    assert columns == 2 and lanes == LANES and 2 * comps * levels == lanes
    assert comps * levels == width
    owners = min(groups, levels)
    rows = comps * (levels // owners)
    early = levels // 2
    planes = comps * levels
    devices = groups * columns
    cells = float(levels * width * groups * lanes * columns)
    f32 = jnp.float32
    update, ratio = pl.pallas_call(
        functools.partial(step_kernel, groups, owners, cells),
        out_shape=(
            jax.ShapeDtypeStruct(orbitals.shape, f32),
            jax.ShapeDtypeStruct((comps, lanes), f32),
        ),
        in_specs=[
            pl.BlockSpec(memory_space=pltpu.SMEM),
            pl.BlockSpec(memory_space=pltpu.HBM),
            pl.BlockSpec(memory_space=pltpu.HBM),
        ],
        out_specs=(
            pl.BlockSpec(memory_space=pl.ANY),
            pl.BlockSpec(memory_space=pltpu.VMEM),
        ),
        scratch_shapes=[
            pltpu.VMEM(orbitals.shape, f32),
            pltpu.VMEM(potential.shape, f32),
            pltpu.VMEM(orbitals.shape, f32),
            pltpu.VMEM((comps, early, width, lanes), f32),
            pltpu.VMEM((width, 3 * width), jnp.bfloat16),
            pltpu.VMEM((2, width, lanes), f32),
            pltpu.VMEM((2, planes, lanes), f32),
            pltpu.VMEM((planes, lanes), f32),
            pltpu.VMEM((width, lanes), f32),
            pltpu.VMEM((width, lanes), f32),
            pltpu.VMEM((4, planes, lanes), f32),
            pltpu.VMEM((2, planes, lanes), f32),
            pltpu.VMEM((owners, 4 * rows, lanes), f32),
            pltpu.VMEM((groups, 4 * rows, lanes), f32),
            pltpu.VMEM((groups, 2 * rows, lanes), f32),
            pltpu.VMEM((owners, 2 * rows, lanes), f32),
            pltpu.VMEM((1, 1, lanes), f32),
            pltpu.VMEM((devices, 1, lanes), f32),
            pltpu.VMEM((1, 1, lanes), f32),
            pltpu.VMEM((devices, 1, lanes), f32),
            pltpu.SemaphoreType.DMA((CHUNKS + 1,)),
            pltpu.SemaphoreType.DMA((2,)),
            pltpu.SemaphoreType.DMA((2,)),
            pltpu.SemaphoreType.DMA((4,)),
            pltpu.SemaphoreType.DMA((4,)),
            pltpu.SemaphoreType.DMA,
        ],
        compiler_params=pltpu.CompilerParams(
            collective_id=0, has_side_effects=True, vmem_limit_bytes=32 * 1024 * 1024
        ),
        name="power_step",
    )(
        shift_ratio,
        pltpu.with_memory_space_constraint(orbitals, pltpu.HBM),
        pltpu.with_memory_space_constraint(potential, pltpu.HBM),
    )
    return update * ratio[:, None, None, :]


def solution(mesh):
    in_specs = (P(None, None, "gx", "gy"), P(None, "gx", "gy"), P())
    out_specs = P(None, None, "gx", "gy")
    return jax.shard_map(shards, mesh=mesh, in_specs=in_specs, out_specs=out_specs, check_vma=False)
```

```python
import functools

import jax
import jax.numpy as jnp
from jax import lax
from jax.experimental import pallas as pl
from jax.experimental.pallas import tpu as pltpu
from jax.sharding import PartitionSpec as P

TAU = 4.0
EPS = 1e-06
COUPLING_FIRST = 0.06
COUPLING_SECOND = 0.05
COUPLING_CROSS = 0.04
MESH = pl.DeviceIdType.MESH
LANES = 128
CHUNKS = 4
GROUP = 4


def wait_bytes(ref, sem):
    pltpu.make_async_copy(ref, ref, sem).wait()


def step_kernel(
    groups,
    owners,
    cells,
    shift_ratio,
    orb_hbm,
    pot_hbm,
    out_hbm,
    ratio_ref,
    orb,
    pot,
    app,
    shift,
    table,
    weights,
    x_send,
    x_halo,
    y_send,
    y_halo,
    tips_ref,
    moments,
    tip_send,
    tip_recv,
    orb_tip_send,
    orb_tip_recv,
    carry_send,
    carry,
    sums_send,
    sums_recv,
    mass_send,
    mass_recv,
    load_sem,
    halo_send_sem,
    halo_recv_sem,
    send_sem,
    recv_sem,
    out_sem,
):
    comps, levels, width, lanes = orb.shape
    per = levels // owners
    early = shift.shape[1]
    rows = comps * per
    devices = 2 * groups
    gx = lax.axis_index("gx")
    gy = lax.axis_index("gy")
    lane = lax.broadcasted_iota(jnp.int32, (width, lanes), 1)
    row = lax.broadcasted_iota(jnp.int32, (width, lanes), 0)
    lane_row = lax.broadcasted_iota(jnp.int32, (1, lanes), 1)

    def peer(step):
        other = gx + step
        return jnp.where(other >= groups, other - groups, other)

    def device_at(step, side):
        return (peer(step), gy if side == 0 else 1 - gy)

    chunk = levels // CHUNKS
    loads = [
        pltpu.make_async_copy(
            orb_hbm.at[:, pl.ds(i * chunk, chunk)], orb.at[:, pl.ds(i * chunk, chunk)], load_sem.at[i]
        )
        for i in range(CHUNKS)
    ]
    loads.append(pltpu.make_async_copy(pot_hbm, pot, load_sem.at[CHUNKS]))
    for copy in loads:
        copy.start()

    barrier = pltpu.get_barrier_semaphore()

    def greet(step, _):
        for side in range(2):
            pl.semaphore_signal(barrier, inc=1, device_id=device_at(step, side), device_id_type=MESH)
        return 0

    pl.semaphore_signal(barrier, inc=1, device_id=(gx, 1 - gy), device_id_type=MESH)
    lax.fori_loop(1, groups, greet, 0)

    line_cells = width * groups
    sigma_wide = jnp.full((1, 2 * lanes), shift_ratio[0] / float(line_cells * line_cells), jnp.float32)
    decay_wide = jnp.log1p(sigma_wide + jnp.sqrt(sigma_wide * (sigma_wide + 2.0)))
    gain_wide = TAU * jnp.sqrt(sigma_wide / (sigma_wide + 2.0))
    sigma, decay, gain = (x[:, :lanes] for x in (sigma_wide, decay_wide, gain_wide))
    tip_gain = gain * jnp.exp(-decay)
    block = jnp.exp(-decay * float(width))
    inv_wrap = 1.0 / (1.0 - jnp.exp(-decay * float(line_cells)))
    edge = jnp.exp(-decay * float(width - 1))
    eight = jnp.exp(-8.0 * decay)
    keep = 1.0 - TAU * sigma
    position = row.astype(jnp.float32)
    weights[0] = jnp.exp(-decay * (float(width - 1) - position))
    weights[1] = jnp.exp(-decay * position)
    near_last = weights[0, width - 8 : width, :]
    near_first = weights[1, 0:8, :]
    t_row = lax.broadcasted_iota(jnp.int32, (width, 3 * width), 0)
    t_col = lax.broadcasted_iota(jnp.int32, (width, 3 * width), 1)
    t_mod = jnp.where(t_col >= 2 * width, t_col - 2 * width, jnp.where(t_col >= width, t_col - width, t_col))
    distance = jnp.abs(t_row - t_mod).astype(jnp.float32)
    green = gain_wide[:, : 3 * width] * jnp.exp(-decay_wide[:, : 3 * width] * distance)
    high = green.astype(jnp.bfloat16)
    low = (green - high.astype(jnp.float32)).astype(jnp.bfloat16)
    table[...] = jnp.where(t_col >= 2 * width, low.astype(jnp.float32), high.astype(jnp.float32)).astype(jnp.bfloat16)

    def groups_of(size, first, last, body, held):
        return lax.fori_loop(0, (last - first) // size, lambda i, x: body(first + i * size, x), held)

    def weighted(x):
        parts = [x[i : i + 8] for i in range(0, width, 8)]
        to_last, to_first = parts[0], parts[-1]
        for i in range(1, len(parts)):
            to_last = to_last * eight + parts[i]
            to_first = to_first * eight + parts[-1 - i]
        return (
            jnp.sum(to_last * near_last, axis=0, keepdims=True),
            jnp.sum(to_first * near_first, axis=0, keepdims=True),
        )

    def copy_tips(source, target, which, step):
        def go():
            pltpu.make_async_remote_copy(
                source.at[peer(step)],
                target.at[groups - step],
                send_sem.at[which],
                recv_sem.at[which],
                device_id=device_at(step, 0),
                device_id_type=MESH,
            ).start()

        if owners == groups:
            go()
        else:
            pl.when(peer(step) < owners)(go)

    def pack(start, held):
        rows_out = []
        ends = []
        for i in range(GROUP):
            z = start + i
            for c in range(comps):
                plane = orb[c, z]
                index = z * comps + c
                held = jnp.where(lane // 2 == index, pltpu.roll(plane, 2 * index + 1, 1), held)
                rows_out.append((index, plane[width - 1 : width], plane[0:1]))
                ends.append((lax.div(start, per) + i // per, i % per * comps + c, weighted(plane)))
        for index, last, first in rows_out:
            x_send[0, pl.ds(index, 1), :] = last
            x_send[1, pl.ds(index, 1), :] = first
        for owner, at, tips in ends:
            for j, tip in enumerate(tips):
                orb_tip_send[owner, j * rows + at : j * rows + at + 1, :] = tip
        return held

    held = jnp.zeros((width, lanes), jnp.float32)
    for i in range(CHUNKS):
        loads[i].wait()
        held = groups_of(GROUP, i * chunk, (i + 1) * chunk, pack, held)
    y_send[...] = held

    pl.semaphore_wait(barrier, devices - 1)
    halos = [
        pltpu.make_async_remote_copy(
            src, dst, halo_send_sem.at[i], halo_recv_sem.at[i], device_id=target, device_id_type=MESH
        )
        for i, (src, dst, target) in enumerate(
            (
                (y_send, y_halo, (gx, 1 - gy)),
                (x_send.at[1], x_halo, (peer(groups - 1), gy)),
            )
        )
    ]
    for copy in halos:
        copy.start()
    loads[CHUNKS].wait()

    def fold(x):
        total = x[0:8]
        for i in range(8, width, 8):
            total = total + x[i : i + 8]
        return total

    def apply_level(z, sums, stores):
        o = [orb[c, z] for c in range(comps)]
        before = lax.rem(z + levels - 1, levels)
        after = lax.rem(z + 1, levels)
        squares = [x * x for x in o]
        density = (
            COUPLING_FIRST * squares[0] + COUPLING_CROSS * squares[1],
            COUPLING_CROSS * squares[0] + COUPLING_SECOND * squares[1],
        )
        trap = pot[z] + 2.0
        result = []
        for c in range(comps):
            mine = o[c]
            near = pltpu.roll(mine, 1, 1) + pltpu.roll(mine, lanes - 1, 1)
            near = near + orb[c, before] + orb[c, after]
            applied = (trap + density[c]) * mine - 0.5 * near
            stores.append((c, z, applied, weighted(applied)))
            along = mine - pltpu.roll(mine, width - 1, 0)
            result.append(sums[2 * c] + fold(mine * (applied + along)))
            result.append(sums[2 * c + 1] + fold(squares[c]))
        return tuple(result)

    def apply_pair(start, sums):
        stores = []
        for i in range(2):
            sums = apply_level(start + i, sums, stores)
        for c, z, applied, tips in stores:
            app[c, z] = applied
            for q, tip in enumerate(tips):
                tips_ref[q, pl.ds(z * comps + c, 1), :] = tip
        return sums

    zero = jnp.zeros((8, lanes), jnp.float32)
    sums = (zero,) * (2 * comps)
    if owners == groups and levels == 2 * groups:

        def apply_and_send(step, sums):
            copy_tips(orb_tip_send, orb_tip_recv, 4, step)
            return apply_pair(2 * step, sums)

        sums = lax.fori_loop(1, groups, apply_and_send, apply_pair(0, sums))
    else:

        def send_early(step, _):
            copy_tips(orb_tip_send, orb_tip_recv, 4, step)
            return 0

        lax.fori_loop(1, groups, send_early, 0)
        sums = groups_of(2, 0, levels, apply_pair, sums)
    sums = list(sums)

    for copy in halos:
        copy.wait()
    lack = y_halo[...] - y_send[...]
    lack = jnp.where(lane % 2 == 0, pltpu.roll(lack, lanes - 1, 1), pltpu.roll(lack, 1, 1))
    y_halo[...] = lack
    x_cross = x_send[0] * (x_halo[...] - x_send[1])
    y_cross = y_send[...] * lack
    for c in range(comps):
        sums[2 * c] = sums[2 * c] - fold(jnp.where(row % comps == c, x_cross, 0.0))
        sums[2 * c] = sums[2 * c] - 0.5 * fold(jnp.where(lane // 2 % comps == c, y_cross, 0.0))
    for j in range(2):
        ends = jnp.sum(fold(weights[j] * lack), axis=0, keepdims=True)
        last = jnp.sum(jnp.where(lane == 2 * row, ends, 0.0), axis=1, keepdims=True)
        first = jnp.sum(jnp.where(lane == 2 * row + 1, ends, 0.0), axis=1, keepdims=True)
        more = jnp.where(lane == 0, first, jnp.where(lane == lanes - 1, last, 0.0))
        tips_ref[j] = tips_ref[j] - 0.5 * more

    def lane_of(values):
        packed = jnp.zeros((1, lanes), jnp.float32)
        for i, x in enumerate(values):
            whole = jnp.sum(jnp.sum(x, axis=0, keepdims=True), axis=1, keepdims=True)
            packed = jnp.where(lane_row == i, whole, packed)
        return packed

    def copy_sums(source, target, which, slot, device):
        pltpu.make_async_remote_copy(
            source.at[0],
            target.at[slot],
            send_sem.at[which],
            recv_sem.at[which],
            device_id=device,
            device_id_type=MESH,
        ).start()

    def spread(source, target, which, step):
        for side in range(2):
            copy_sums(source, target, which, 2 * (groups - step) + side, device_at(step, side))

    def gathered(target, which, count):
        wait_bytes(target.at[pl.ds(1, devices - 1)], recv_sem.at[which])
        total = jnp.sum(target[...], axis=0)
        return [
            jnp.sum(jnp.where(lane_row == i, total, 0.0), axis=1, keepdims=True) for i in range(count)
        ]

    own = lane_of(sums)
    sums_send[0] = own
    sums_recv[0] = own
    def fill_tips(owner, _):
        for j in range(2):
            tip_send[owner, j * rows : (j + 1) * rows, :] = tips_ref[j, pl.ds(owner * rows, rows), :]
        return 0

    lax.fori_loop(0, owners, fill_tips, 0, unroll=4)

    def send_line_ends(step, _):
        copy_tips(tip_send, tip_recv, 0, step)
        spread(sums_send, sums_recv, 1, step)
        return 0

    copy_sums(sums_send, sums_recv, 1, 1, (gx, 1 - gy))
    lax.fori_loop(1, groups, send_line_ends, 0)

    @pl.when(gx < owners)
    def _():
        tip_recv[0] = tip_send[lax.rem(gx, owners)]
        orb_tip_recv[0] = orb_tip_send[lax.rem(gx, owners)]

    def split_dot(fields):
        wide = jnp.concatenate(fields, axis=1)
        high = wide.astype(jnp.bfloat16)
        low = (wide - high.astype(jnp.float32)).astype(jnp.bfloat16)
        local = jnp.dot(
            table[...], jnp.concatenate([high, low, high], axis=0), preferred_element_type=jnp.float32
        )
        return [local[:, i * lanes : (i + 1) * lanes] for i in range(len(fields))]

    def whole_applied(c, z):
        index = z * comps + c
        ends = pltpu.roll(y_halo[...], lanes - 1 - 2 * index, 1)
        ends = jnp.where((lane == 0) | (lane == lanes - 1), ends, 0.0)
        return app[c, z] - 0.5 * ends

    def solve_early(start, _):
        places = [(c, start + i) for i in range(GROUP) for c in range(comps)]
        o = [orb[c, z] for c, z in places]
        local = split_dot([whole_applied(c, z) for c, z in places] + o)
        for i, (c, z) in enumerate(places):
            app[c, z] = keep * o[i] - local[i]
            shift[c, z] = local[len(places) + i]
        return 0

    groups_of(GROUP, 0, early, solve_early, 0)

    totals = gathered(sums_recv, 1, 2 * comps)
    mean_square = [totals[2 * c + 1] / cells for c in range(comps)]
    energy = [totals[2 * c] / cells / (mean_square[c] + EPS) + sigma for c in range(comps)]

    @pl.when(gx < owners)
    def _():
        wait_bytes(tip_recv.at[pl.ds(1, groups - 1)], recv_sem.at[0])
        wait_bytes(orb_tip_recv.at[pl.ds(1, groups - 1)], recv_sem.at[4])
        tip_row = lax.broadcasted_iota(jnp.int32, (2 * rows, lanes), 0)
        scale = jnp.where(tip_row % 2 == 0, energy[0], energy[1])

        def tips(k):
            return tip_recv[k] - scale * orb_tip_recv[k]

        def collect(k, held):
            ahead, behind = held
            return block * ahead + tips(k), block * behind + tips(groups - 1 - k)

        start = jnp.zeros((2 * rows, lanes), jnp.float32)
        ahead, behind = lax.fori_loop(0, groups, collect, (start, start), unroll=4)

        def hand_out(k, held):
            ahead, behind = held
            back = groups - 1 - k
            carry_send[k, 0:rows, :] = ahead[0:rows]
            carry_send[back, rows : 2 * rows, :] = behind[rows : 2 * rows]
            return block * ahead + tip_gain * tips(k), block * behind + tip_gain * tips(back)

        factor = tip_gain * inv_wrap
        lax.fori_loop(0, groups, hand_out, (factor * ahead, factor * behind), unroll=4)

        def send(step, _):
            pltpu.make_async_remote_copy(
                carry_send.at[step],
                carry.at[gx],
                send_sem.at[2],
                recv_sem.at[2],
                device_id=(peer(step), gy),
                device_id_type=MESH,
            ).start()
            return 0

        lax.fori_loop(1, groups, send, 0)
        carry[lax.rem(gx, owners)] = carry_send[0]

    def finish(places, fields, masses):
        masses = list(masses)
        ends = []
        for (c, z), own in zip(places, fields):
            ends.append(weighted(own))
            masses[c] = masses[c] + fold(own * own)
        for (c, z), own, (to_last, to_first) in zip(places, fields, ends):
            app[c, z] = own
            moments[0, pl.ds(z * comps + c, 1), :] = to_first
            moments[1, pl.ds(z * comps + c, 1), :] = to_last
        return tuple(masses)

    def finish_early(start, masses):
        places = [(c, start + i) for i in range(2) for c in range(comps)]
        return finish(places, [app[c, z] + energy[c] * shift[c, z] for c, z in places], masses)

    def solve_late(start, masses):
        places = [(c, start + i) for i in range(GROUP) for c in range(comps)]
        o = [orb[c, z] for c, z in places]
        local = split_dot([whole_applied(c, z) - energy[c] * x for (c, z), x in zip(places, o)])
        return finish(places, [keep * x - y for x, y in zip(o, local)], masses)

    masses = groups_of(2, 0, early, finish_early, (zero,) * comps)
    masses = list(groups_of(GROUP, early, levels, solve_late, masses))
    square = jnp.sum(weights[1] * weights[1], axis=0, keepdims=True)

    @pl.when(gx < owners)
    def _():
        wait_bytes(carry.at[pl.ds(0, owners - 1)], recv_sem.at[2])

    @pl.when(gx >= owners)
    def _():
        wait_bytes(carry, recv_sem.at[2])

    def join_mass(owner, held):
        forward, backward = carry[owner, 0:rows, :], carry[owner, rows : 2 * rows, :]
        here = pl.ds(owner * rows, rows)
        held = held + forward * (square * forward - 2.0 * moments[0, here, :])
        held = held + backward * (square * backward - 2.0 * moments[1, here, :])
        return held + 2.0 * float(width) * edge * forward * backward

    joined = lax.fori_loop(0, owners, join_mass, jnp.zeros((rows, lanes), jnp.float32), unroll=4)
    line_row = lax.broadcasted_iota(jnp.int32, (rows, lanes), 0)
    for c in range(comps):
        more = jnp.sum(jnp.where(line_row % comps == c, joined, 0.0), axis=0, keepdims=True)
        masses[c] = jnp.sum(masses[c], axis=0, keepdims=True) + more
    own = lane_of(masses)
    mass_send[0] = own
    mass_recv[0] = own
    copy_sums(mass_send, mass_recv, 3, 1, (gx, 1 - gy))

    def send_mass(step, _):
        spread(mass_send, mass_recv, 3, step)
        return 0

    lax.fori_loop(1, groups, send_mass, 0)

    def update_owner(owner, _):
        places = [(c, owner * per + local, local * comps + c) for local in range(per) for c in range(comps)]
        fields = [
            app[c, z]
            - (
                weights[1] * carry[owner, at : at + 1, :]
                + weights[0] * carry[owner, rows + at : rows + at + 1, :]
            )
            for c, z, at in places
        ]
        for (c, z, at), field in zip(places, fields):
            app[c, z] = field
        levels_here = pl.ds(owner * per, per)
        pltpu.make_async_copy(app.at[:, levels_here], out_hbm.at[:, levels_here], out_sem).start()
        return 0

    lax.fori_loop(0, owners, update_owner, 0)
    totals = gathered(mass_recv, 3, comps)
    for c in range(comps):
        ratio = jnp.sqrt(mean_square[c] / (totals[c] / cells + EPS))
        ratio_ref[c : c + 1, :] = jnp.broadcast_to(ratio, (1, lanes))

    @pl.when(gx < owners)
    def _():
        wait_bytes(tip_send.at[pl.ds(0, owners - 1)], send_sem.at[0])
        wait_bytes(orb_tip_send.at[pl.ds(0, owners - 1)], send_sem.at[4])
        wait_bytes(carry_send.at[pl.ds(1, groups - 1)], send_sem.at[2])

    @pl.when(gx >= owners)
    def _():
        wait_bytes(tip_send, send_sem.at[0])
        wait_bytes(orb_tip_send, send_sem.at[4])

    wait_bytes(sums_recv.at[pl.ds(1, devices - 1)], send_sem.at[1])
    wait_bytes(mass_recv.at[pl.ds(1, devices - 1)], send_sem.at[3])
    pltpu.make_async_copy(app, out_hbm, out_sem).wait()


def shards(orbitals, potential, shift_ratio):
    groups = lax.axis_size("gx")
    columns = lax.axis_size("gy")
    comps, levels, width, lanes = orbitals.shape
    assert columns == 2 and lanes == LANES and 2 * comps * levels == lanes
    assert comps * levels == width
    owners = min(groups, levels)
    rows = comps * (levels // owners)
    early = levels // 2
    planes = comps * levels
    devices = groups * columns
    cells = float(levels * width * groups * lanes * columns)
    f32 = jnp.float32
    update, ratio = pl.pallas_call(
        functools.partial(step_kernel, groups, owners, cells),
        out_shape=(
            jax.ShapeDtypeStruct(orbitals.shape, f32),
            jax.ShapeDtypeStruct((comps, lanes), f32),
        ),
        in_specs=[
            pl.BlockSpec(memory_space=pltpu.SMEM),
            pl.BlockSpec(memory_space=pltpu.HBM),
            pl.BlockSpec(memory_space=pltpu.HBM),
        ],
        out_specs=(
            pl.BlockSpec(memory_space=pl.ANY),
            pl.BlockSpec(memory_space=pltpu.VMEM),
        ),
        scratch_shapes=[
            pltpu.VMEM(orbitals.shape, f32),
            pltpu.VMEM(potential.shape, f32),
            pltpu.VMEM(orbitals.shape, f32),
            pltpu.VMEM((comps, early, width, lanes), f32),
            pltpu.VMEM((width, 3 * width), jnp.bfloat16),
            pltpu.VMEM((2, width, lanes), f32),
            pltpu.VMEM((2, planes, lanes), f32),
            pltpu.VMEM((planes, lanes), f32),
            pltpu.VMEM((width, lanes), f32),
            pltpu.VMEM((width, lanes), f32),
            pltpu.VMEM((2, planes, lanes), f32),
            pltpu.VMEM((2, planes, lanes), f32),
            pltpu.VMEM((owners, 2 * rows, lanes), f32),
            pltpu.VMEM((groups, 2 * rows, lanes), f32),
            pltpu.VMEM((owners, 2 * rows, lanes), f32),
            pltpu.VMEM((groups, 2 * rows, lanes), f32),
            pltpu.VMEM((groups, 2 * rows, lanes), f32),
            pltpu.VMEM((owners, 2 * rows, lanes), f32),
            pltpu.VMEM((1, 1, lanes), f32),
            pltpu.VMEM((devices, 1, lanes), f32),
            pltpu.VMEM((1, 1, lanes), f32),
            pltpu.VMEM((devices, 1, lanes), f32),
            pltpu.SemaphoreType.DMA((CHUNKS + 1,)),
            pltpu.SemaphoreType.DMA((2,)),
            pltpu.SemaphoreType.DMA((2,)),
            pltpu.SemaphoreType.DMA((5,)),
            pltpu.SemaphoreType.DMA((5,)),
            pltpu.SemaphoreType.DMA,
        ],
        compiler_params=pltpu.CompilerParams(
            collective_id=0, has_side_effects=True, vmem_limit_bytes=32 * 1024 * 1024
        ),
        name="power_step",
    )(
        shift_ratio,
        pltpu.with_memory_space_constraint(orbitals, pltpu.HBM),
        pltpu.with_memory_space_constraint(potential, pltpu.HBM),
    )
    return update * ratio[:, None, None, :]


def solution(mesh):
    in_specs = (P(None, None, "gx", "gy"), P(None, "gx", "gy"), P())
    out_specs = P(None, None, "gx", "gy")
    return jax.shard_map(shards, mesh=mesh, in_specs=in_specs, out_specs=out_specs, check_vma=False)
```

```python
import functools

import jax
import jax.numpy as jnp
from jax import lax
from jax.experimental import pallas as pl
from jax.experimental.pallas import tpu as pltpu
from jax.sharding import PartitionSpec as P

TAU = 4.0
EPS = 1e-06
COUPLING_FIRST = 0.06
COUPLING_SECOND = 0.05
COUPLING_CROSS = 0.04
MESH = pl.DeviceIdType.MESH
LANES = 128
CHUNKS = 4
GROUP = 4


def wait_bytes(ref, sem):
    pltpu.make_async_copy(ref, ref, sem).wait()


def step_kernel(
    groups,
    owners,
    cells,
    shift_ratio,
    orb_hbm,
    pot_hbm,
    out_hbm,
    ratio_ref,
    orb,
    pot,
    app,
    shift,
    table,
    weights,
    x_send,
    x_halo,
    y_send,
    y_halo,
    tips_ref,
    moments,
    tip_send,
    tip_recv,
    orb_tip_send,
    orb_tip_recv,
    carry_send,
    carry,
    sums_send,
    sums_recv,
    mass_send,
    mass_recv,
    load_sem,
    halo_send_sem,
    halo_recv_sem,
    send_sem,
    recv_sem,
    out_sem,
):
    comps, levels, width, lanes = orb.shape
    per = levels // owners
    early = shift.shape[1]
    rows = comps * per
    devices = 2 * groups
    gx = lax.axis_index("gx")
    gy = lax.axis_index("gy")
    lane = lax.broadcasted_iota(jnp.int32, (width, lanes), 1)
    row = lax.broadcasted_iota(jnp.int32, (width, lanes), 0)
    plane_of = lax.shift_right_logical(lane, 1)
    odd_lane = lane & 1
    lane_row = lax.broadcasted_iota(jnp.int32, (1, lanes), 1)

    def peer(step):
        other = gx + step
        return jnp.where(other >= groups, other - groups, other)

    def device_at(step, side):
        return (peer(step), gy if side == 0 else 1 - gy)

    chunk = levels // CHUNKS
    loads = [
        pltpu.make_async_copy(
            orb_hbm.at[:, pl.ds(i * chunk, chunk)], orb.at[:, pl.ds(i * chunk, chunk)], load_sem.at[i]
        )
        for i in range(CHUNKS)
    ]
    loads.append(pltpu.make_async_copy(pot_hbm, pot, load_sem.at[CHUNKS]))
    for copy in loads:
        copy.start()

    barrier = pltpu.get_barrier_semaphore()

    def greet(step, _):
        for side in range(2):
            pl.semaphore_signal(barrier, inc=1, device_id=device_at(step, side), device_id_type=MESH)
        return 0

    pl.semaphore_signal(barrier, inc=1, device_id=(gx, 1 - gy), device_id_type=MESH)
    lax.fori_loop(1, groups, greet, 0, unroll=3)

    line_cells = width * groups
    sigma_wide = jnp.full((1, 2 * lanes), shift_ratio[0] / float(line_cells * line_cells), jnp.float32)
    decay_wide = jnp.log1p(sigma_wide + jnp.sqrt(sigma_wide * (sigma_wide + 2.0)))
    gain_wide = TAU * jnp.sqrt(sigma_wide / (sigma_wide + 2.0))
    sigma, decay, gain = (x[:, :lanes] for x in (sigma_wide, decay_wide, gain_wide))
    tip_gain = gain * jnp.exp(-decay)
    block = jnp.exp(-decay * float(width))
    inv_wrap = 1.0 / (1.0 - jnp.exp(-decay * float(line_cells)))
    edge = jnp.exp(-decay * float(width - 1))
    eight = jnp.exp(-8.0 * decay)
    keep = 1.0 - TAU * sigma
    position = row.astype(jnp.float32)
    weights[0] = jnp.exp(-decay * (float(width - 1) - position))
    weights[1] = jnp.exp(-decay * position)
    near_last = weights[0, width - 8 : width, :]
    near_first = weights[1, 0:8, :]
    t_row = lax.broadcasted_iota(jnp.int32, (width, 3 * width), 0)
    t_col = lax.broadcasted_iota(jnp.int32, (width, 3 * width), 1)
    t_mod = jnp.where(t_col >= 2 * width, t_col - 2 * width, jnp.where(t_col >= width, t_col - width, t_col))
    distance = jnp.abs(t_row - t_mod).astype(jnp.float32)
    green = gain_wide[:, : 3 * width] * jnp.exp(-decay_wide[:, : 3 * width] * distance)
    high = green.astype(jnp.bfloat16)
    low = (green - high.astype(jnp.float32)).astype(jnp.bfloat16)
    table[...] = jnp.where(t_col >= 2 * width, low.astype(jnp.float32), high.astype(jnp.float32)).astype(jnp.bfloat16)

    def groups_of(size, first, last, body, held):
        return lax.fori_loop(0, (last - first) // size, lambda i, x: body(first + i * size, x), held)

    def weighted(x):
        parts = [x[i : i + 8] for i in range(0, width, 8)]
        to_last, to_first = parts[0], parts[-1]
        for i in range(1, len(parts)):
            to_last = to_last * eight + parts[i]
            to_first = to_first * eight + parts[-1 - i]
        return (
            jnp.sum(to_last * near_last, axis=0, keepdims=True),
            jnp.sum(to_first * near_first, axis=0, keepdims=True),
        )

    def copy_tips(source, target, which, step):
        def go():
            pltpu.make_async_remote_copy(
                source.at[peer(step)],
                target.at[groups - step],
                send_sem.at[which],
                recv_sem.at[which],
                device_id=device_at(step, 0),
                device_id_type=MESH,
            ).start()

        if owners == groups:
            go()
        else:
            pl.when(peer(step) < owners)(go)

    def pack(start, held):
        rows_out = []
        ends = []
        for i in range(GROUP):
            z = start + i
            for c in range(comps):
                plane = orb[c, z]
                index = z * comps + c
                held = jnp.where(plane_of == index, pltpu.roll(plane, 2 * index + 1, 1), held)
                rows_out.append((index, plane[width - 1 : width], plane[0:1]))
                ends.append((lax.div(start, per) + i // per, i % per * comps + c, weighted(plane)))
        for index, last, first in rows_out:
            x_send[0, pl.ds(index, 1), :] = last
            x_send[1, pl.ds(index, 1), :] = first
        for owner, at, tips in ends:
            for j, tip in enumerate(tips):
                orb_tip_send[owner, j * rows + at : j * rows + at + 1, :] = tip
        return held

    held = jnp.zeros((width, lanes), jnp.float32)
    for i in range(CHUNKS):
        loads[i].wait()
        held = groups_of(GROUP, i * chunk, (i + 1) * chunk, pack, held)
    y_send[...] = held

    pl.semaphore_wait(barrier, devices - 1)
    halos = [
        pltpu.make_async_remote_copy(
            src, dst, halo_send_sem.at[i], halo_recv_sem.at[i], device_id=target, device_id_type=MESH
        )
        for i, (src, dst, target) in enumerate(
            (
                (y_send, y_halo, (gx, 1 - gy)),
                (x_send.at[1], x_halo, (peer(groups - 1), gy)),
            )
        )
    ]
    for copy in halos:
        copy.start()
    loads[CHUNKS].wait()

    def fold(x):
        total = x[0:8]
        for i in range(8, width, 8):
            total = total + x[i : i + 8]
        return total

    def apply_level(z, sums, stores):
        o = [orb[c, z] for c in range(comps)]
        before = lax.rem(z + levels - 1, levels)
        after = lax.rem(z + 1, levels)
        squares = [x * x for x in o]
        density = (
            COUPLING_FIRST * squares[0] + COUPLING_CROSS * squares[1],
            COUPLING_CROSS * squares[0] + COUPLING_SECOND * squares[1],
        )
        trap = pot[z] + 2.0
        result = []
        for c in range(comps):
            mine = o[c]
            near = pltpu.roll(mine, 1, 1) + pltpu.roll(mine, lanes - 1, 1)
            near = near + orb[c, before] + orb[c, after]
            applied = (trap + density[c]) * mine - 0.5 * near
            stores.append((c, z, applied, weighted(applied)))
            along = mine - pltpu.roll(mine, width - 1, 0)
            result.append(sums[2 * c] + fold(mine * (applied + along)))
            result.append(sums[2 * c + 1] + fold(squares[c]))
        return tuple(result)

    def apply_pair(start, sums):
        stores = []
        for i in range(2):
            sums = apply_level(start + i, sums, stores)
        for c, z, applied, tips in stores:
            app[c, z] = applied
            for q, tip in enumerate(tips):
                tips_ref[q, pl.ds(z * comps + c, 1), :] = tip
        return sums

    zero = jnp.zeros((8, lanes), jnp.float32)
    sums = (zero,) * (2 * comps)
    if owners == groups and levels == 2 * groups:

        def apply_and_send(step, sums):
            copy_tips(orb_tip_send, orb_tip_recv, 4, step)
            return apply_pair(2 * step, sums)

        sums = lax.fori_loop(1, groups, apply_and_send, apply_pair(0, sums))
    else:

        def send_early(step, _):
            copy_tips(orb_tip_send, orb_tip_recv, 4, step)
            return 0

        lax.fori_loop(1, groups, send_early, 0)
        sums = groups_of(2, 0, levels, apply_pair, sums)
    sums = list(sums)

    for copy in halos:
        copy.wait()
    lack = y_halo[...] - y_send[...]
    lack = jnp.where(odd_lane == 0, pltpu.roll(lack, lanes - 1, 1), pltpu.roll(lack, 1, 1))
    y_halo[...] = lack
    x_cross = x_send[0] * (x_halo[...] - x_send[1])
    y_cross = y_send[...] * lack
    for c in range(comps):
        sums[2 * c] = sums[2 * c] - fold(jnp.where((row & 1) == c, x_cross, 0.0))
        sums[2 * c] = sums[2 * c] - 0.5 * fold(jnp.where((plane_of & 1) == c, y_cross, 0.0))
    for j in range(2):
        ends = jnp.sum(fold(weights[j] * lack), axis=0, keepdims=True)
        last = jnp.sum(jnp.where((plane_of == row) & (odd_lane == 0), ends, 0.0), axis=1, keepdims=True)
        first = jnp.sum(jnp.where((plane_of == row) & (odd_lane == 1), ends, 0.0), axis=1, keepdims=True)
        more = jnp.where(lane == 0, first, jnp.where(lane == lanes - 1, last, 0.0))
        tips_ref[j] = tips_ref[j] - 0.5 * more

    def lane_of(values):
        packed = jnp.zeros((1, lanes), jnp.float32)
        for i, x in enumerate(values):
            whole = jnp.sum(jnp.sum(x, axis=0, keepdims=True), axis=1, keepdims=True)
            packed = jnp.where(lane_row == i, whole, packed)
        return packed

    def copy_sums(source, target, which, slot, device):
        pltpu.make_async_remote_copy(
            source.at[0],
            target.at[slot],
            send_sem.at[which],
            recv_sem.at[which],
            device_id=device,
            device_id_type=MESH,
        ).start()

    def spread(source, target, which, step):
        for side in range(2):
            copy_sums(source, target, which, 2 * (groups - step) + side, device_at(step, side))

    def gathered(target, which, count):
        wait_bytes(target.at[pl.ds(1, devices - 1)], recv_sem.at[which])
        total = jnp.sum(target[...], axis=0)
        return [
            jnp.sum(jnp.where(lane_row == i, total, 0.0), axis=1, keepdims=True) for i in range(count)
        ]

    own = lane_of(sums)
    sums_send[0] = own
    sums_recv[0] = own
    def fill_tips(owner, _):
        for j in range(2):
            tip_send[owner, j * rows : (j + 1) * rows, :] = tips_ref[j, pl.ds(owner * rows, rows), :]
        return 0

    lax.fori_loop(0, owners, fill_tips, 0, unroll=4)

    def send_line_ends(step, _):
        copy_tips(tip_send, tip_recv, 0, step)
        spread(sums_send, sums_recv, 1, step)
        return 0

    copy_sums(sums_send, sums_recv, 1, 1, (gx, 1 - gy))
    lax.fori_loop(1, groups, send_line_ends, 0, unroll=3)

    @pl.when(gx < owners)
    def _():
        tip_recv[0] = tip_send[lax.rem(gx, owners)]
        orb_tip_recv[0] = orb_tip_send[lax.rem(gx, owners)]

    def split_dot(fields):
        wide = jnp.concatenate(fields, axis=1)
        high = wide.astype(jnp.bfloat16)
        low = (wide - high.astype(jnp.float32)).astype(jnp.bfloat16)
        local = jnp.dot(
            table[...], jnp.concatenate([high, low, high], axis=0), preferred_element_type=jnp.float32
        )
        return [local[:, i * lanes : (i + 1) * lanes] for i in range(len(fields))]

    side = jnp.where((lane == 0) | (lane == lanes - 1), -0.5, 0.0)

    def whole_applied(c, z):
        index = z * comps + c
        return app[c, z] + side * pltpu.roll(y_halo[...], lanes - 1 - 2 * index, 1)

    def solve_early(start, _):
        places = [(c, start + i) for i in range(GROUP) for c in range(comps)]
        o = [orb[c, z] for c, z in places]
        local = split_dot([whole_applied(c, z) for c, z in places] + o)
        for i, (c, z) in enumerate(places):
            app[c, z] = keep * o[i] - local[i]
            shift[c, z] = local[len(places) + i]
        return 0

    groups_of(GROUP, 0, early, solve_early, 0)

    totals = gathered(sums_recv, 1, 2 * comps)
    mean_square = [totals[2 * c + 1] / cells for c in range(comps)]
    energy = [totals[2 * c] / cells / (mean_square[c] + EPS) + sigma for c in range(comps)]

    @pl.when(gx < owners)
    def _():
        wait_bytes(tip_recv.at[pl.ds(1, groups - 1)], recv_sem.at[0])
        wait_bytes(orb_tip_recv.at[pl.ds(1, groups - 1)], recv_sem.at[4])
        tip_row = lax.broadcasted_iota(jnp.int32, (2 * rows, lanes), 0)
        scale = jnp.where((tip_row & 1) == 0, energy[0], energy[1])

        def tips(k):
            return tip_recv[k] - scale * orb_tip_recv[k]

        def collect(k, held):
            ahead, behind = held
            return block * ahead + tips(k), block * behind + tips(groups - 1 - k)

        start = jnp.zeros((2 * rows, lanes), jnp.float32)
        ahead, behind = lax.fori_loop(0, groups, collect, (start, start), unroll=4)

        def hand_out(k, held):
            ahead, behind = held
            back = groups - 1 - k
            carry_send[k, 0:rows, :] = ahead[0:rows]
            carry_send[back, rows : 2 * rows, :] = behind[rows : 2 * rows]
            return block * ahead + tip_gain * tips(k), block * behind + tip_gain * tips(back)

        factor = tip_gain * inv_wrap
        lax.fori_loop(0, groups, hand_out, (factor * ahead, factor * behind), unroll=4)

        def send(step, _):
            pltpu.make_async_remote_copy(
                carry_send.at[step],
                carry.at[gx],
                send_sem.at[2],
                recv_sem.at[2],
                device_id=(peer(step), gy),
                device_id_type=MESH,
            ).start()
            return 0

        lax.fori_loop(1, groups, send, 0, unroll=3)
        carry[lax.rem(gx, owners)] = carry_send[0]

    def finish(places, fields, masses):
        masses = list(masses)
        ends = []
        for (c, z), own in zip(places, fields):
            ends.append(weighted(own))
            masses[c] = masses[c] + fold(own * own)
        for (c, z), own, (to_last, to_first) in zip(places, fields, ends):
            app[c, z] = own
            moments[0, pl.ds(z * comps + c, 1), :] = to_first
            moments[1, pl.ds(z * comps + c, 1), :] = to_last
        return tuple(masses)

    def finish_early(start, masses):
        places = [(c, start + i) for i in range(2) for c in range(comps)]
        return finish(places, [app[c, z] + energy[c] * shift[c, z] for c, z in places], masses)

    def solve_late(start, masses):
        places = [(c, start + i) for i in range(GROUP) for c in range(comps)]
        o = [orb[c, z] for c, z in places]
        local = split_dot([whole_applied(c, z) - energy[c] * x for (c, z), x in zip(places, o)])
        return finish(places, [keep * x - y for x, y in zip(o, local)], masses)

    masses = groups_of(2, 0, early, finish_early, (zero,) * comps)
    masses = list(groups_of(GROUP, early, levels, solve_late, masses))
    square = jnp.sum(weights[1] * weights[1], axis=0, keepdims=True)

    @pl.when(gx < owners)
    def _():
        wait_bytes(carry.at[pl.ds(0, owners - 1)], recv_sem.at[2])

    @pl.when(gx >= owners)
    def _():
        wait_bytes(carry, recv_sem.at[2])

    def join_mass(owner, held):
        forward, backward = carry[owner, 0:rows, :], carry[owner, rows : 2 * rows, :]
        here = pl.ds(owner * rows, rows)
        held = held + forward * (square * forward - 2.0 * moments[0, here, :])
        held = held + backward * (square * backward - 2.0 * moments[1, here, :])
        return held + 2.0 * float(width) * edge * forward * backward

    joined = lax.fori_loop(0, owners, join_mass, jnp.zeros((rows, lanes), jnp.float32), unroll=4)
    line_row = lax.broadcasted_iota(jnp.int32, (rows, lanes), 0)
    for c in range(comps):
        more = jnp.sum(jnp.where((line_row & 1) == c, joined, 0.0), axis=0, keepdims=True)
        masses[c] = jnp.sum(masses[c], axis=0, keepdims=True) + more
    own = lane_of(masses)
    mass_send[0] = own
    mass_recv[0] = own
    copy_sums(mass_send, mass_recv, 3, 1, (gx, 1 - gy))

    def send_mass(step, _):
        spread(mass_send, mass_recv, 3, step)
        return 0

    lax.fori_loop(1, groups, send_mass, 0, unroll=3)

    def update_owner(owner, _):
        places = [(c, owner * per + local, local * comps + c) for local in range(per) for c in range(comps)]
        fields = [
            app[c, z]
            - (
                weights[1] * carry[owner, at : at + 1, :]
                + weights[0] * carry[owner, rows + at : rows + at + 1, :]
            )
            for c, z, at in places
        ]
        for (c, z, at), field in zip(places, fields):
            app[c, z] = field
        levels_here = pl.ds(owner * per, per)
        pltpu.make_async_copy(app.at[:, levels_here], out_hbm.at[:, levels_here], out_sem).start()
        return 0

    lax.fori_loop(0, owners, update_owner, 0)
    totals = gathered(mass_recv, 3, comps)
    for c in range(comps):
        ratio = jnp.sqrt(mean_square[c] / (totals[c] / cells + EPS))
        ratio_ref[c : c + 1, :] = jnp.broadcast_to(ratio, (1, lanes))

    @pl.when(gx < owners)
    def _():
        wait_bytes(tip_send.at[pl.ds(0, owners - 1)], send_sem.at[0])
        wait_bytes(orb_tip_send.at[pl.ds(0, owners - 1)], send_sem.at[4])
        wait_bytes(carry_send.at[pl.ds(1, groups - 1)], send_sem.at[2])

    @pl.when(gx >= owners)
    def _():
        wait_bytes(tip_send, send_sem.at[0])
        wait_bytes(orb_tip_send, send_sem.at[4])

    wait_bytes(sums_recv.at[pl.ds(1, devices - 1)], send_sem.at[1])
    wait_bytes(mass_recv.at[pl.ds(1, devices - 1)], send_sem.at[3])
    pltpu.make_async_copy(app, out_hbm, out_sem).wait()


def shards(orbitals, potential, shift_ratio):
    groups = lax.axis_size("gx")
    columns = lax.axis_size("gy")
    comps, levels, width, lanes = orbitals.shape
    assert columns == 2 and lanes == LANES and 2 * comps * levels == lanes
    assert comps == 2 and comps * levels == width
    owners = min(groups, levels)
    rows = comps * (levels // owners)
    early = levels // 2
    planes = comps * levels
    devices = groups * columns
    cells = float(levels * width * groups * lanes * columns)
    f32 = jnp.float32
    update, ratio = pl.pallas_call(
        functools.partial(step_kernel, groups, owners, cells),
        out_shape=(
            jax.ShapeDtypeStruct(orbitals.shape, f32),
            jax.ShapeDtypeStruct((comps, lanes), f32),
        ),
        in_specs=[
            pl.BlockSpec(memory_space=pltpu.SMEM),
            pl.BlockSpec(memory_space=pltpu.HBM),
            pl.BlockSpec(memory_space=pltpu.HBM),
        ],
        out_specs=(
            pl.BlockSpec(memory_space=pl.ANY),
            pl.BlockSpec(memory_space=pltpu.VMEM),
        ),
        scratch_shapes=[
            pltpu.VMEM(orbitals.shape, f32),
            pltpu.VMEM(potential.shape, f32),
            pltpu.VMEM(orbitals.shape, f32),
            pltpu.VMEM((comps, early, width, lanes), f32),
            pltpu.VMEM((width, 3 * width), jnp.bfloat16),
            pltpu.VMEM((2, width, lanes), f32),
            pltpu.VMEM((2, planes, lanes), f32),
            pltpu.VMEM((planes, lanes), f32),
            pltpu.VMEM((width, lanes), f32),
            pltpu.VMEM((width, lanes), f32),
            pltpu.VMEM((2, planes, lanes), f32),
            pltpu.VMEM((2, planes, lanes), f32),
            pltpu.VMEM((owners, 2 * rows, lanes), f32),
            pltpu.VMEM((groups, 2 * rows, lanes), f32),
            pltpu.VMEM((owners, 2 * rows, lanes), f32),
            pltpu.VMEM((groups, 2 * rows, lanes), f32),
            pltpu.VMEM((groups, 2 * rows, lanes), f32),
            pltpu.VMEM((owners, 2 * rows, lanes), f32),
            pltpu.VMEM((1, 1, lanes), f32),
            pltpu.VMEM((devices, 1, lanes), f32),
            pltpu.VMEM((1, 1, lanes), f32),
            pltpu.VMEM((devices, 1, lanes), f32),
            pltpu.SemaphoreType.DMA((CHUNKS + 1,)),
            pltpu.SemaphoreType.DMA((2,)),
            pltpu.SemaphoreType.DMA((2,)),
            pltpu.SemaphoreType.DMA((5,)),
            pltpu.SemaphoreType.DMA((5,)),
            pltpu.SemaphoreType.DMA,
        ],
        compiler_params=pltpu.CompilerParams(
            collective_id=0, has_side_effects=True, vmem_limit_bytes=32 * 1024 * 1024
        ),
        name="power_step",
    )(
        shift_ratio,
        pltpu.with_memory_space_constraint(orbitals, pltpu.HBM),
        pltpu.with_memory_space_constraint(potential, pltpu.HBM),
    )
    return update * ratio[:, None, None, :]


def solution(mesh):
    in_specs = (P(None, None, "gx", "gy"), P(None, "gx", "gy"), P())
    out_specs = P(None, None, "gx", "gy")
    return jax.shard_map(shards, mesh=mesh, in_specs=in_specs, out_specs=out_specs, check_vma=False)
```

```python
import functools

import jax
import jax.numpy as jnp
from jax import lax
from jax.experimental import pallas as pl
from jax.experimental.pallas import tpu as pltpu
from jax.sharding import PartitionSpec as P

TAU = 4.0
EPS = 1e-06
COUPLING_FIRST = 0.06
COUPLING_SECOND = 0.05
COUPLING_CROSS = 0.04
MESH = pl.DeviceIdType.MESH
LANES = 128
CHUNKS = 4
GROUP = 4


def wait_bytes(ref, sem):
    pltpu.make_async_copy(ref, ref, sem).wait()


def step_kernel(
    groups,
    owners,
    cells,
    shift_ratio,
    orb_hbm,
    pot_hbm,
    out_hbm,
    ratio_ref,
    orb,
    pot,
    app,
    shift,
    table,
    weights,
    x_send,
    x_halo,
    y_send,
    y_halo,
    tips_ref,
    moments,
    tip_send,
    tip_recv,
    orb_tip_send,
    orb_tip_recv,
    carry_send,
    carry,
    sums_near,
    sums_far,
    mass_near,
    mass_far,
    load_sem,
    halo_send_sem,
    halo_recv_sem,
    send_sem,
    recv_sem,
    out_sem,
):
    comps, levels, width, lanes = orb.shape
    per = levels // owners
    early = shift.shape[1]
    rows = comps * per
    gx = lax.axis_index("gx")
    gy = lax.axis_index("gy")
    lane = lax.broadcasted_iota(jnp.int32, (width, lanes), 1)
    row = lax.broadcasted_iota(jnp.int32, (width, lanes), 0)
    plane_of = lax.shift_right_logical(lane, 1)
    odd_lane = lane & 1
    lane_row = lax.broadcasted_iota(jnp.int32, (1, lanes), 1)

    def peer(step):
        other = gx + step
        return jnp.where(other >= groups, other - groups, other)

    pairs = groups // 2
    core = lax.rem(gx, 2)

    def near_device(code):
        other = gx + 1 - 2 * core if code % 2 else gx
        return (other, 1 - gy if code >= 2 else gy)

    def far_device(step):
        other = lax.div(gx, 2) + step
        return (2 * jnp.where(other >= pairs, other - pairs, other) + core, gy)

    chunk = levels // CHUNKS
    loads = [
        pltpu.make_async_copy(
            orb_hbm.at[:, pl.ds(i * chunk, chunk)], orb.at[:, pl.ds(i * chunk, chunk)], load_sem.at[i]
        )
        for i in range(CHUNKS)
    ]
    loads.append(pltpu.make_async_copy(pot_hbm, pot, load_sem.at[CHUNKS]))
    for copy in loads:
        copy.start()

    barrier = pltpu.get_barrier_semaphore()

    def greet(step, _):
        pl.semaphore_signal(barrier, inc=1, device_id=(peer(step), gy), device_id_type=MESH)
        return 0

    for code in (2, 3):
        pl.semaphore_signal(barrier, inc=1, device_id=near_device(code), device_id_type=MESH)
    lax.fori_loop(1, groups, greet, 0, unroll=3)

    line_cells = width * groups
    sigma_wide = jnp.full((1, 2 * lanes), shift_ratio[0] / float(line_cells * line_cells), jnp.float32)
    decay_wide = jnp.log1p(sigma_wide + jnp.sqrt(sigma_wide * (sigma_wide + 2.0)))
    gain_wide = TAU * jnp.sqrt(sigma_wide / (sigma_wide + 2.0))
    sigma, decay, gain = (x[:, :lanes] for x in (sigma_wide, decay_wide, gain_wide))
    tip_gain = gain * jnp.exp(-decay)
    block = jnp.exp(-decay * float(width))
    inv_wrap = 1.0 / (1.0 - jnp.exp(-decay * float(line_cells)))
    edge = jnp.exp(-decay * float(width - 1))
    eight = jnp.exp(-8.0 * decay)
    keep = 1.0 - TAU * sigma
    position = row.astype(jnp.float32)
    weights[0] = jnp.exp(-decay * (float(width - 1) - position))
    weights[1] = jnp.exp(-decay * position)
    near_last = weights[0, width - 8 : width, :]
    near_first = weights[1, 0:8, :]
    t_row = lax.broadcasted_iota(jnp.int32, (width, 3 * width), 0)
    t_col = lax.broadcasted_iota(jnp.int32, (width, 3 * width), 1)
    t_mod = jnp.where(t_col >= 2 * width, t_col - 2 * width, jnp.where(t_col >= width, t_col - width, t_col))
    distance = jnp.abs(t_row - t_mod).astype(jnp.float32)
    green = gain_wide[:, : 3 * width] * jnp.exp(-decay_wide[:, : 3 * width] * distance)
    high = green.astype(jnp.bfloat16)
    low = (green - high.astype(jnp.float32)).astype(jnp.bfloat16)
    table[...] = jnp.where(t_col >= 2 * width, low.astype(jnp.float32), high.astype(jnp.float32)).astype(jnp.bfloat16)

    def groups_of(size, first, last, body, held):
        return lax.fori_loop(0, (last - first) // size, lambda i, x: body(first + i * size, x), held)

    def weighted(x):
        parts = [x[i : i + 8] for i in range(0, width, 8)]
        to_last, to_first = parts[0], parts[-1]
        for i in range(1, len(parts)):
            to_last = to_last * eight + parts[i]
            to_first = to_first * eight + parts[-1 - i]
        return (
            jnp.sum(to_last * near_last, axis=0, keepdims=True),
            jnp.sum(to_first * near_first, axis=0, keepdims=True),
        )

    def copy_tips(source, target, which, step):
        def go():
            pltpu.make_async_remote_copy(
                source.at[peer(step)],
                target.at[groups - step],
                send_sem.at[which],
                recv_sem.at[which],
                device_id=(peer(step), gy),
                device_id_type=MESH,
            ).start()

        if owners == groups:
            go()
        else:
            pl.when(peer(step) < owners)(go)

    def pack(start, held):
        rows_out = []
        ends = []
        for i in range(GROUP):
            z = start + i
            for c in range(comps):
                plane = orb[c, z]
                index = z * comps + c
                held = jnp.where(plane_of == index, pltpu.roll(plane, 2 * index + 1, 1), held)
                rows_out.append((index, plane[width - 1 : width], plane[0:1]))
                ends.append((lax.div(start, per) + i // per, i % per * comps + c, weighted(plane)))
        for index, last, first in rows_out:
            x_send[0, pl.ds(index, 1), :] = last
            x_send[1, pl.ds(index, 1), :] = first
        for owner, at, tips in ends:
            for j, tip in enumerate(tips):
                orb_tip_send[owner, j * rows + at : j * rows + at + 1, :] = tip
        return held

    held = jnp.zeros((width, lanes), jnp.float32)
    for i in range(CHUNKS):
        loads[i].wait()
        held = groups_of(GROUP, i * chunk, (i + 1) * chunk, pack, held)
    y_send[...] = held

    pl.semaphore_wait(barrier, groups + 1)
    halos = [
        pltpu.make_async_remote_copy(
            src, dst, halo_send_sem.at[i], halo_recv_sem.at[i], device_id=target, device_id_type=MESH
        )
        for i, (src, dst, target) in enumerate(
            (
                (y_send, y_halo, (gx, 1 - gy)),
                (x_send.at[1], x_halo, (peer(groups - 1), gy)),
            )
        )
    ]
    for copy in halos:
        copy.start()
    loads[CHUNKS].wait()

    def fold(x):
        total = x[0:8]
        for i in range(8, width, 8):
            total = total + x[i : i + 8]
        return total

    def apply_level(z, sums, stores):
        o = [orb[c, z] for c in range(comps)]
        before = lax.rem(z + levels - 1, levels)
        after = lax.rem(z + 1, levels)
        squares = [x * x for x in o]
        density = (
            COUPLING_FIRST * squares[0] + COUPLING_CROSS * squares[1],
            COUPLING_CROSS * squares[0] + COUPLING_SECOND * squares[1],
        )
        trap = pot[z] + 2.0
        result = []
        for c in range(comps):
            mine = o[c]
            near = pltpu.roll(mine, 1, 1) + pltpu.roll(mine, lanes - 1, 1)
            near = near + orb[c, before] + orb[c, after]
            applied = (trap + density[c]) * mine - 0.5 * near
            stores.append((c, z, applied, weighted(applied)))
            along = mine - pltpu.roll(mine, width - 1, 0)
            result.append(sums[2 * c] + fold(mine * (applied + along)))
            result.append(sums[2 * c + 1] + fold(squares[c]))
        return tuple(result)

    def apply_pair(start, sums):
        stores = []
        for i in range(2):
            sums = apply_level(start + i, sums, stores)
        for c, z, applied, tips in stores:
            app[c, z] = applied
            for q, tip in enumerate(tips):
                tips_ref[q, pl.ds(z * comps + c, 1), :] = tip
        return sums

    zero = jnp.zeros((8, lanes), jnp.float32)
    sums = (zero,) * (2 * comps)
    if owners == groups and levels == 2 * groups:

        def apply_and_send(step, sums):
            copy_tips(orb_tip_send, orb_tip_recv, 4, step)
            return apply_pair(2 * step, sums)

        sums = lax.fori_loop(1, groups, apply_and_send, apply_pair(0, sums))
    else:

        def send_early(step, _):
            copy_tips(orb_tip_send, orb_tip_recv, 4, step)
            return 0

        lax.fori_loop(1, groups, send_early, 0)
        sums = groups_of(2, 0, levels, apply_pair, sums)
    sums = list(sums)

    for copy in halos:
        copy.wait()
    lack = y_halo[...] - y_send[...]
    lack = jnp.where(odd_lane == 0, pltpu.roll(lack, lanes - 1, 1), pltpu.roll(lack, 1, 1))
    y_halo[...] = lack
    x_cross = x_send[0] * (x_halo[...] - x_send[1])
    y_cross = y_send[...] * lack
    for c in range(comps):
        sums[2 * c] = sums[2 * c] - fold(jnp.where((row & 1) == c, x_cross, 0.0))
        sums[2 * c] = sums[2 * c] - 0.5 * fold(jnp.where((plane_of & 1) == c, y_cross, 0.0))
    for j in range(2):
        ends = jnp.sum(fold(weights[j] * lack), axis=0, keepdims=True)
        last = jnp.sum(jnp.where((plane_of == row) & (odd_lane == 0), ends, 0.0), axis=1, keepdims=True)
        first = jnp.sum(jnp.where((plane_of == row) & (odd_lane == 1), ends, 0.0), axis=1, keepdims=True)
        more = jnp.where(lane == 0, first, jnp.where(lane == lanes - 1, last, 0.0))
        tips_ref[j] = tips_ref[j] - 0.5 * more

    def lane_of(values):
        packed = jnp.zeros((1, lanes), jnp.float32)
        for i, x in enumerate(values):
            whole = jnp.sum(jnp.sum(x, axis=0, keepdims=True), axis=1, keepdims=True)
            packed = jnp.where(lane_row == i, whole, packed)
        return packed

    def send_row(ref, here, there, which, device):
        pltpu.make_async_remote_copy(
            ref.at[here],
            ref.at[there],
            send_sem.at[which],
            recv_sem.at[which],
            device_id=device,
            device_id_type=MESH,
        ).start()

    def spread_near(values, near, which):
        near[0] = lane_of(values)
        for code in range(1, 4):
            send_row(near, 0, code, which, near_device(code))

    def spread_far(near, near_which, far, which):
        wait_bytes(near.at[pl.ds(1, 3)], recv_sem.at[near_which])
        far[0] = jnp.sum(near[...], axis=0)

        def send(step, _):
            send_row(far, 0, pairs - step, which, far_device(step))
            return 0

        lax.fori_loop(1, pairs, send, 0, unroll=7)

    def gathered(far, which, count):
        wait_bytes(far.at[pl.ds(1, pairs - 1)], recv_sem.at[which])
        total = jnp.sum(far[...], axis=0)
        return [
            jnp.sum(jnp.where(lane_row == i, total, 0.0), axis=1, keepdims=True) for i in range(count)
        ]

    spread_near(sums, sums_near, 1)

    def fill_tips(owner, _):
        for j in range(2):
            tip_send[owner, j * rows : (j + 1) * rows, :] = tips_ref[j, pl.ds(owner * rows, rows), :]
        return 0

    lax.fori_loop(0, owners, fill_tips, 0, unroll=4)

    def send_tips(step, _):
        copy_tips(tip_send, tip_recv, 0, step)
        return 0

    lax.fori_loop(1, groups, send_tips, 0, unroll=3)
    spread_far(sums_near, 1, sums_far, 5)

    @pl.when(gx < owners)
    def _():
        tip_recv[0] = tip_send[lax.rem(gx, owners)]
        orb_tip_recv[0] = orb_tip_send[lax.rem(gx, owners)]

    def split_dot(fields):
        wide = jnp.concatenate(fields, axis=1)
        high = wide.astype(jnp.bfloat16)
        low = (wide - high.astype(jnp.float32)).astype(jnp.bfloat16)
        local = jnp.dot(
            table[...], jnp.concatenate([high, low, high], axis=0), preferred_element_type=jnp.float32
        )
        return [local[:, i * lanes : (i + 1) * lanes] for i in range(len(fields))]

    side = jnp.where((lane == 0) | (lane == lanes - 1), -0.5, 0.0)

    def whole_applied(c, z):
        index = z * comps + c
        return app[c, z] + side * pltpu.roll(y_halo[...], lanes - 1 - 2 * index, 1)

    def solve_early(start, _):
        places = [(c, start + i) for i in range(GROUP) for c in range(comps)]
        o = [orb[c, z] for c, z in places]
        local = split_dot([whole_applied(c, z) for c, z in places] + o)
        for i, (c, z) in enumerate(places):
            app[c, z] = keep * o[i] - local[i]
            shift[c, z] = local[len(places) + i]
        return 0

    groups_of(GROUP, 0, early, solve_early, 0)

    totals = gathered(sums_far, 5, 2 * comps)
    mean_square = [totals[2 * c + 1] / cells for c in range(comps)]
    energy = [totals[2 * c] / cells / (mean_square[c] + EPS) + sigma for c in range(comps)]

    @pl.when(gx < owners)
    def _():
        wait_bytes(tip_recv.at[pl.ds(1, groups - 1)], recv_sem.at[0])
        wait_bytes(orb_tip_recv.at[pl.ds(1, groups - 1)], recv_sem.at[4])
        tip_row = lax.broadcasted_iota(jnp.int32, (2 * rows, lanes), 0)
        scale = jnp.where((tip_row & 1) == 0, energy[0], energy[1])

        def tips(k):
            return tip_recv[k] - scale * orb_tip_recv[k]

        def collect(k, held):
            ahead, behind = held
            return block * ahead + tips(k), block * behind + tips(groups - 1 - k)

        start = jnp.zeros((2 * rows, lanes), jnp.float32)
        ahead, behind = lax.fori_loop(0, groups, collect, (start, start), unroll=4)

        def hand_out(k, held):
            ahead, behind = held
            back = groups - 1 - k
            carry_send[k, 0:rows, :] = ahead[0:rows]
            carry_send[back, rows : 2 * rows, :] = behind[rows : 2 * rows]
            return block * ahead + tip_gain * tips(k), block * behind + tip_gain * tips(back)

        factor = tip_gain * inv_wrap
        lax.fori_loop(0, groups, hand_out, (factor * ahead, factor * behind), unroll=4)

        def send(step, _):
            pltpu.make_async_remote_copy(
                carry_send.at[step],
                carry.at[gx],
                send_sem.at[2],
                recv_sem.at[2],
                device_id=(peer(step), gy),
                device_id_type=MESH,
            ).start()
            return 0

        lax.fori_loop(1, groups, send, 0, unroll=3)
        carry[lax.rem(gx, owners)] = carry_send[0]

    def finish(places, fields, masses):
        masses = list(masses)
        ends = []
        for (c, z), own in zip(places, fields):
            ends.append(weighted(own))
            masses[c] = masses[c] + fold(own * own)
        for (c, z), own, (to_last, to_first) in zip(places, fields, ends):
            app[c, z] = own
            moments[0, pl.ds(z * comps + c, 1), :] = to_first
            moments[1, pl.ds(z * comps + c, 1), :] = to_last
        return tuple(masses)

    def finish_early(start, masses):
        places = [(c, start + i) for i in range(2) for c in range(comps)]
        return finish(places, [app[c, z] + energy[c] * shift[c, z] for c, z in places], masses)

    def solve_late(start, masses):
        places = [(c, start + i) for i in range(GROUP) for c in range(comps)]
        o = [orb[c, z] for c, z in places]
        local = split_dot([whole_applied(c, z) - energy[c] * x for (c, z), x in zip(places, o)])
        return finish(places, [keep * x - y for x, y in zip(o, local)], masses)

    masses = groups_of(2, 0, early, finish_early, (zero,) * comps)
    masses = list(groups_of(GROUP, early, levels, solve_late, masses))
    square = jnp.sum(weights[1] * weights[1], axis=0, keepdims=True)

    @pl.when(gx < owners)
    def _():
        wait_bytes(carry.at[pl.ds(0, owners - 1)], recv_sem.at[2])

    @pl.when(gx >= owners)
    def _():
        wait_bytes(carry, recv_sem.at[2])

    def join_mass(owner, held):
        forward, backward = carry[owner, 0:rows, :], carry[owner, rows : 2 * rows, :]
        here = pl.ds(owner * rows, rows)
        held = held + forward * (square * forward - 2.0 * moments[0, here, :])
        held = held + backward * (square * backward - 2.0 * moments[1, here, :])
        return held + 2.0 * float(width) * edge * forward * backward

    joined = lax.fori_loop(0, owners, join_mass, jnp.zeros((rows, lanes), jnp.float32), unroll=4)
    line_row = lax.broadcasted_iota(jnp.int32, (rows, lanes), 0)
    for c in range(comps):
        more = jnp.sum(jnp.where((line_row & 1) == c, joined, 0.0), axis=0, keepdims=True)
        masses[c] = jnp.sum(masses[c], axis=0, keepdims=True) + more
    spread_near(masses, mass_near, 3)

    def update_owner(owner, _):
        places = [(c, owner * per + local, local * comps + c) for local in range(per) for c in range(comps)]
        fields = [
            app[c, z]
            - (
                weights[1] * carry[owner, at : at + 1, :]
                + weights[0] * carry[owner, rows + at : rows + at + 1, :]
            )
            for c, z, at in places
        ]
        for (c, z, at), field in zip(places, fields):
            app[c, z] = field
        levels_here = pl.ds(owner * per, per)
        pltpu.make_async_copy(app.at[:, levels_here], out_hbm.at[:, levels_here], out_sem).start()
        return 0

    lax.fori_loop(0, owners // 2, update_owner, 0)
    spread_far(mass_near, 3, mass_far, 6)
    lax.fori_loop(owners // 2, owners, update_owner, 0)
    totals = gathered(mass_far, 6, comps)
    for c in range(comps):
        ratio = jnp.sqrt(mean_square[c] / (totals[c] / cells + EPS))
        ratio_ref[c : c + 1, :] = jnp.broadcast_to(ratio, (1, lanes))

    @pl.when(gx < owners)
    def _():
        wait_bytes(tip_send.at[pl.ds(0, owners - 1)], send_sem.at[0])
        wait_bytes(orb_tip_send.at[pl.ds(0, owners - 1)], send_sem.at[4])
        wait_bytes(carry_send.at[pl.ds(1, groups - 1)], send_sem.at[2])

    @pl.when(gx >= owners)
    def _():
        wait_bytes(tip_send, send_sem.at[0])
        wait_bytes(orb_tip_send, send_sem.at[4])

    for near, far, near_which, far_which in ((sums_near, sums_far, 1, 5), (mass_near, mass_far, 3, 6)):
        wait_bytes(near.at[pl.ds(1, 3)], send_sem.at[near_which])
        wait_bytes(far.at[pl.ds(1, pairs - 1)], send_sem.at[far_which])
    pltpu.make_async_copy(app, out_hbm, out_sem).wait()


def shards(orbitals, potential, shift_ratio):
    groups = lax.axis_size("gx")
    columns = lax.axis_size("gy")
    comps, levels, width, lanes = orbitals.shape
    assert columns == 2 and lanes == LANES and 2 * comps * levels == lanes
    assert comps == 2 and comps * levels == width
    owners = min(groups, levels)
    rows = comps * (levels // owners)
    early = levels // 2
    planes = comps * levels
    cells = float(levels * width * groups * lanes * columns)
    f32 = jnp.float32
    update, ratio = pl.pallas_call(
        functools.partial(step_kernel, groups, owners, cells),
        out_shape=(
            jax.ShapeDtypeStruct(orbitals.shape, f32),
            jax.ShapeDtypeStruct((comps, lanes), f32),
        ),
        in_specs=[
            pl.BlockSpec(memory_space=pltpu.SMEM),
            pl.BlockSpec(memory_space=pltpu.HBM),
            pl.BlockSpec(memory_space=pltpu.HBM),
        ],
        out_specs=(
            pl.BlockSpec(memory_space=pl.ANY),
            pl.BlockSpec(memory_space=pltpu.VMEM),
        ),
        scratch_shapes=[
            pltpu.VMEM(orbitals.shape, f32),
            pltpu.VMEM(potential.shape, f32),
            pltpu.VMEM(orbitals.shape, f32),
            pltpu.VMEM((comps, early, width, lanes), f32),
            pltpu.VMEM((width, 3 * width), jnp.bfloat16),
            pltpu.VMEM((2, width, lanes), f32),
            pltpu.VMEM((2, planes, lanes), f32),
            pltpu.VMEM((planes, lanes), f32),
            pltpu.VMEM((width, lanes), f32),
            pltpu.VMEM((width, lanes), f32),
            pltpu.VMEM((2, planes, lanes), f32),
            pltpu.VMEM((2, planes, lanes), f32),
            pltpu.VMEM((owners, 2 * rows, lanes), f32),
            pltpu.VMEM((groups, 2 * rows, lanes), f32),
            pltpu.VMEM((owners, 2 * rows, lanes), f32),
            pltpu.VMEM((groups, 2 * rows, lanes), f32),
            pltpu.VMEM((groups, 2 * rows, lanes), f32),
            pltpu.VMEM((owners, 2 * rows, lanes), f32),
            pltpu.VMEM((4, 1, lanes), f32),
            pltpu.VMEM((groups // 2, 1, lanes), f32),
            pltpu.VMEM((4, 1, lanes), f32),
            pltpu.VMEM((groups // 2, 1, lanes), f32),
            pltpu.SemaphoreType.DMA((CHUNKS + 1,)),
            pltpu.SemaphoreType.DMA((2,)),
            pltpu.SemaphoreType.DMA((2,)),
            pltpu.SemaphoreType.DMA((7,)),
            pltpu.SemaphoreType.DMA((7,)),
            pltpu.SemaphoreType.DMA,
        ],
        compiler_params=pltpu.CompilerParams(
            collective_id=0, has_side_effects=True, vmem_limit_bytes=32 * 1024 * 1024
        ),
        name="power_step",
    )(
        shift_ratio,
        pltpu.with_memory_space_constraint(orbitals, pltpu.HBM),
        pltpu.with_memory_space_constraint(potential, pltpu.HBM),
    )
    return update * ratio[:, None, None, :]


def solution(mesh):
    in_specs = (P(None, None, "gx", "gy"), P(None, "gx", "gy"), P())
    out_specs = P(None, None, "gx", "gy")
    return jax.shard_map(shards, mesh=mesh, in_specs=in_specs, out_specs=out_specs, check_vma=False)
```

```python
import functools

import jax
import jax.numpy as jnp
from jax import lax
from jax.experimental import pallas as pl
from jax.experimental.pallas import tpu as pltpu
from jax.sharding import PartitionSpec as P

TAU = 4.0
EPS = 1e-06
COUPLING_FIRST = 0.06
COUPLING_SECOND = 0.05
COUPLING_CROSS = 0.04
MESH = pl.DeviceIdType.MESH
LANES = 128
CHUNKS = 4
GROUP = 4
SCALE_PARTS = 4


def wait_bytes(ref, sem):
    pltpu.make_async_copy(ref, ref, sem).wait()


def step_kernel(
    groups,
    owners,
    cells,
    shift_ratio,
    orb_hbm,
    pot_hbm,
    out_hbm,
    ratio_ref,
    orb,
    pot,
    app,
    shift,
    table,
    weights,
    x_send,
    x_halo,
    y_send,
    y_halo,
    tips_ref,
    moments,
    tip_send,
    tip_recv,
    orb_tip_send,
    orb_tip_recv,
    carry_send,
    carry,
    sums_send,
    sums_recv,
    mass_send,
    mass_recv,
    load_sem,
    halo_send_sem,
    halo_recv_sem,
    send_sem,
    recv_sem,
    out_sem,
):
    comps, levels, width, lanes = orb.shape
    per = levels // owners
    early = shift.shape[1]
    rows = comps * per
    devices = 2 * groups
    gx = lax.axis_index("gx")
    gy = lax.axis_index("gy")
    lane = lax.broadcasted_iota(jnp.int32, (width, lanes), 1)
    row = lax.broadcasted_iota(jnp.int32, (width, lanes), 0)
    lane_row = lax.broadcasted_iota(jnp.int32, (1, lanes), 1)

    def peer(step):
        other = gx + step
        return jnp.where(other >= groups, other - groups, other)

    def device_at(step, side):
        return (peer(step), gy if side == 0 else 1 - gy)

    chunk = levels // CHUNKS
    loads = [
        pltpu.make_async_copy(
            orb_hbm.at[:, pl.ds(i * chunk, chunk)], orb.at[:, pl.ds(i * chunk, chunk)], load_sem.at[i]
        )
        for i in range(CHUNKS)
    ]
    loads.append(pltpu.make_async_copy(pot_hbm, pot, load_sem.at[CHUNKS]))
    for copy in loads:
        copy.start()

    barrier = pltpu.get_barrier_semaphore()

    def greet(step, _):
        for side in range(2):
            pl.semaphore_signal(barrier, inc=1, device_id=device_at(step, side), device_id_type=MESH)
        return 0

    pl.semaphore_signal(barrier, inc=1, device_id=(gx, 1 - gy), device_id_type=MESH)
    lax.fori_loop(1, groups, greet, 0)

    line_cells = width * groups
    sigma_wide = jnp.full((1, 2 * lanes), shift_ratio[0] / float(line_cells * line_cells), jnp.float32)
    decay_wide = jnp.log1p(sigma_wide + jnp.sqrt(sigma_wide * (sigma_wide + 2.0)))
    gain_wide = TAU * jnp.sqrt(sigma_wide / (sigma_wide + 2.0))
    sigma, decay, gain = (x[:, :lanes] for x in (sigma_wide, decay_wide, gain_wide))
    tip_gain = gain * jnp.exp(-decay)
    block = jnp.exp(-decay * float(width))
    inv_wrap = 1.0 / (1.0 - jnp.exp(-decay * float(line_cells)))
    edge = jnp.exp(-decay * float(width - 1))
    eight = jnp.exp(-8.0 * decay)
    keep = 1.0 - TAU * sigma
    position = row.astype(jnp.float32)
    weights[0] = jnp.exp(-decay * (float(width - 1) - position))
    weights[1] = jnp.exp(-decay * position)
    near_last = weights[0, width - 8 : width, :]
    near_first = weights[1, 0:8, :]
    t_row = lax.broadcasted_iota(jnp.int32, (width, 3 * width), 0)
    t_col = lax.broadcasted_iota(jnp.int32, (width, 3 * width), 1)
    t_mod = jnp.where(t_col >= 2 * width, t_col - 2 * width, jnp.where(t_col >= width, t_col - width, t_col))
    distance = jnp.abs(t_row - t_mod).astype(jnp.float32)
    green = gain_wide[:, : 3 * width] * jnp.exp(-decay_wide[:, : 3 * width] * distance)
    high = green.astype(jnp.bfloat16)
    low = (green - high.astype(jnp.float32)).astype(jnp.bfloat16)
    table[...] = jnp.where(t_col >= 2 * width, low.astype(jnp.float32), high.astype(jnp.float32)).astype(jnp.bfloat16)

    def groups_of(size, first, last, body, held):
        return lax.fori_loop(0, (last - first) // size, lambda i, x: body(first + i * size, x), held)

    def weighted(x):
        parts = [x[i : i + 8] for i in range(0, width, 8)]
        to_last, to_first = parts[0], parts[-1]
        for i in range(1, len(parts)):
            to_last = to_last * eight + parts[i]
            to_first = to_first * eight + parts[-1 - i]
        return (
            jnp.sum(to_last * near_last, axis=0, keepdims=True),
            jnp.sum(to_first * near_first, axis=0, keepdims=True),
        )

    def copy_tips(source, target, which, step):
        def go():
            pltpu.make_async_remote_copy(
                source.at[peer(step)],
                target.at[groups - step],
                send_sem.at[which],
                recv_sem.at[which],
                device_id=device_at(step, 0),
                device_id_type=MESH,
            ).start()

        if owners == groups:
            go()
        else:
            pl.when(peer(step) < owners)(go)

    def pack(start, held):
        rows_out = []
        ends = []
        for i in range(GROUP):
            z = start + i
            for c in range(comps):
                plane = orb[c, z]
                index = z * comps + c
                held = jnp.where(lane // 2 == index, pltpu.roll(plane, 2 * index + 1, 1), held)
                rows_out.append((index, plane[width - 1 : width], plane[0:1]))
                ends.append((lax.div(start, per) + i // per, i % per * comps + c, weighted(plane)))
        for index, last, first in rows_out:
            x_send[0, pl.ds(index, 1), :] = last
            x_send[1, pl.ds(index, 1), :] = first
        for owner, at, tips in ends:
            for j, tip in enumerate(tips):
                orb_tip_send[owner, j * rows + at : j * rows + at + 1, :] = tip
        return held

    held = jnp.zeros((width, lanes), jnp.float32)
    for i in range(CHUNKS):
        loads[i].wait()
        held = groups_of(GROUP, i * chunk, (i + 1) * chunk, pack, held)
    y_send[...] = held

    pl.semaphore_wait(barrier, devices - 1)
    halos = [
        pltpu.make_async_remote_copy(
            src, dst, halo_send_sem.at[i], halo_recv_sem.at[i], device_id=target, device_id_type=MESH
        )
        for i, (src, dst, target) in enumerate(
            (
                (y_send, y_halo, (gx, 1 - gy)),
                (x_send.at[1], x_halo, (peer(groups - 1), gy)),
            )
        )
    ]
    for copy in halos:
        copy.start()
    loads[CHUNKS].wait()

    def fold(x):
        total = x[0:8]
        for i in range(8, width, 8):
            total = total + x[i : i + 8]
        return total

    def apply_level(z, sums, stores):
        o = [orb[c, z] for c in range(comps)]
        before = lax.rem(z + levels - 1, levels)
        after = lax.rem(z + 1, levels)
        squares = [x * x for x in o]
        density = (
            COUPLING_FIRST * squares[0] + COUPLING_CROSS * squares[1],
            COUPLING_CROSS * squares[0] + COUPLING_SECOND * squares[1],
        )
        trap = pot[z] + 2.0
        result = []
        for c in range(comps):
            mine = o[c]
            near = pltpu.roll(mine, 1, 1) + pltpu.roll(mine, lanes - 1, 1)
            near = near + orb[c, before] + orb[c, after]
            applied = (trap + density[c]) * mine - 0.5 * near
            stores.append((c, z, applied, weighted(applied)))
            along = mine - pltpu.roll(mine, width - 1, 0)
            result.append(sums[2 * c] + fold(mine * (applied + along)))
            result.append(sums[2 * c + 1] + fold(squares[c]))
        return tuple(result)

    def apply_pair(start, sums):
        stores = []
        for i in range(2):
            sums = apply_level(start + i, sums, stores)
        for c, z, applied, tips in stores:
            app[c, z] = applied
            for q, tip in enumerate(tips):
                tips_ref[q, pl.ds(z * comps + c, 1), :] = tip
        return sums

    zero = jnp.zeros((8, lanes), jnp.float32)
    sums = (zero,) * (2 * comps)
    if owners == groups and levels == 2 * groups:

        def apply_and_send(step, sums):
            copy_tips(orb_tip_send, orb_tip_recv, 4, step)
            return apply_pair(2 * step, sums)

        sums = lax.fori_loop(1, groups, apply_and_send, apply_pair(0, sums))
    else:

        def send_early(step, _):
            copy_tips(orb_tip_send, orb_tip_recv, 4, step)
            return 0

        lax.fori_loop(1, groups, send_early, 0)
        sums = groups_of(2, 0, levels, apply_pair, sums)
    sums = list(sums)

    for copy in halos:
        copy.wait()
    lack = y_halo[...] - y_send[...]
    lack = jnp.where(lane % 2 == 0, pltpu.roll(lack, lanes - 1, 1), pltpu.roll(lack, 1, 1))
    y_halo[...] = lack
    x_cross = x_send[0] * (x_halo[...] - x_send[1])
    y_cross = y_send[...] * lack
    for c in range(comps):
        sums[2 * c] = sums[2 * c] - fold(jnp.where(row % comps == c, x_cross, 0.0))
        sums[2 * c] = sums[2 * c] - 0.5 * fold(jnp.where(lane // 2 % comps == c, y_cross, 0.0))
    for j in range(2):
        ends = jnp.sum(fold(weights[j] * lack), axis=0, keepdims=True)
        last = jnp.sum(jnp.where(lane == 2 * row, ends, 0.0), axis=1, keepdims=True)
        first = jnp.sum(jnp.where(lane == 2 * row + 1, ends, 0.0), axis=1, keepdims=True)
        more = jnp.where(lane == 0, first, jnp.where(lane == lanes - 1, last, 0.0))
        tips_ref[j] = tips_ref[j] - 0.5 * more

    def lane_of(values):
        packed = jnp.zeros((1, lanes), jnp.float32)
        for i, x in enumerate(values):
            whole = jnp.sum(jnp.sum(x, axis=0, keepdims=True), axis=1, keepdims=True)
            packed = jnp.where(lane_row == i, whole, packed)
        return packed

    def copy_sums(source, target, which, slot, device):
        pltpu.make_async_remote_copy(
            source.at[0],
            target.at[slot],
            send_sem.at[which],
            recv_sem.at[which],
            device_id=device,
            device_id_type=MESH,
        ).start()

    def spread(source, target, which, step):
        for side in range(2):
            copy_sums(source, target, which, 2 * (groups - step) + side, device_at(step, side))

    def gathered(target, which, count):
        wait_bytes(target.at[pl.ds(1, devices - 1)], recv_sem.at[which])
        total = jnp.sum(target[...], axis=0)
        return [
            jnp.sum(jnp.where(lane_row == i, total, 0.0), axis=1, keepdims=True) for i in range(count)
        ]

    own = lane_of(sums)
    sums_send[0] = own
    sums_recv[0] = own
    def fill_tips(owner, _):
        for j in range(2):
            tip_send[owner, j * rows : (j + 1) * rows, :] = tips_ref[j, pl.ds(owner * rows, rows), :]
        return 0

    lax.fori_loop(0, owners, fill_tips, 0, unroll=4)

    def send_line_ends(step, _):
        copy_tips(tip_send, tip_recv, 0, step)
        spread(sums_send, sums_recv, 1, step)
        return 0

    copy_sums(sums_send, sums_recv, 1, 1, (gx, 1 - gy))
    lax.fori_loop(1, groups, send_line_ends, 0)

    @pl.when(gx < owners)
    def _():
        tip_recv[0] = tip_send[lax.rem(gx, owners)]
        orb_tip_recv[0] = orb_tip_send[lax.rem(gx, owners)]

    def split_dot(fields):
        wide = jnp.concatenate(fields, axis=1)
        high = wide.astype(jnp.bfloat16)
        low = (wide - high.astype(jnp.float32)).astype(jnp.bfloat16)
        local = jnp.dot(
            table[...], jnp.concatenate([high, low, high], axis=0), preferred_element_type=jnp.float32
        )
        return [local[:, i * lanes : (i + 1) * lanes] for i in range(len(fields))]

    def whole_applied(c, z):
        index = z * comps + c
        ends = pltpu.roll(y_halo[...], lanes - 1 - 2 * index, 1)
        ends = jnp.where((lane == 0) | (lane == lanes - 1), ends, 0.0)
        return app[c, z] - 0.5 * ends

    def solve_early(start, _):
        places = [(c, start + i) for i in range(GROUP) for c in range(comps)]
        o = [orb[c, z] for c, z in places]
        local = split_dot([whole_applied(c, z) for c, z in places] + o)
        for i, (c, z) in enumerate(places):
            app[c, z] = keep * o[i] - local[i]
            shift[c, z] = local[len(places) + i]
        return 0

    groups_of(GROUP, 0, early, solve_early, 0)

    totals = gathered(sums_recv, 1, 2 * comps)
    mean_square = [totals[2 * c + 1] / cells for c in range(comps)]
    energy = [totals[2 * c] / cells / (mean_square[c] + EPS) + sigma for c in range(comps)]

    @pl.when(gx < owners)
    def _():
        wait_bytes(tip_recv.at[pl.ds(1, groups - 1)], recv_sem.at[0])
        wait_bytes(orb_tip_recv.at[pl.ds(1, groups - 1)], recv_sem.at[4])
        tip_row = lax.broadcasted_iota(jnp.int32, (2 * rows, lanes), 0)
        scale = jnp.where(tip_row % 2 == 0, energy[0], energy[1])

        def tips(k):
            return tip_recv[k] - scale * orb_tip_recv[k]

        def collect(k, held):
            ahead, behind = held
            return block * ahead + tips(k), block * behind + tips(groups - 1 - k)

        start = jnp.zeros((2 * rows, lanes), jnp.float32)
        ahead, behind = lax.fori_loop(0, groups, collect, (start, start), unroll=4)

        def hand_out(k, held):
            ahead, behind = held
            back = groups - 1 - k
            carry_send[k, 0:rows, :] = ahead[0:rows]
            carry_send[back, rows : 2 * rows, :] = behind[rows : 2 * rows]
            return block * ahead + tip_gain * tips(k), block * behind + tip_gain * tips(back)

        factor = tip_gain * inv_wrap
        lax.fori_loop(0, groups, hand_out, (factor * ahead, factor * behind), unroll=4)

        def send(step, _):
            pltpu.make_async_remote_copy(
                carry_send.at[step],
                carry.at[gx],
                send_sem.at[2],
                recv_sem.at[2],
                device_id=(peer(step), gy),
                device_id_type=MESH,
            ).start()
            return 0

        lax.fori_loop(1, groups, send, 0)
        carry[lax.rem(gx, owners)] = carry_send[0]

    def finish(places, fields, masses):
        masses = list(masses)
        ends = []
        for (c, z), own in zip(places, fields):
            ends.append(weighted(own))
            masses[c] = masses[c] + fold(own * own)
        for (c, z), own, (to_last, to_first) in zip(places, fields, ends):
            app[c, z] = own
            moments[0, pl.ds(z * comps + c, 1), :] = to_first
            moments[1, pl.ds(z * comps + c, 1), :] = to_last
        return tuple(masses)

    def finish_early(start, masses):
        places = [(c, start + i) for i in range(2) for c in range(comps)]
        return finish(places, [app[c, z] + energy[c] * shift[c, z] for c, z in places], masses)

    def solve_late(start, masses):
        places = [(c, start + i) for i in range(GROUP) for c in range(comps)]
        o = [orb[c, z] for c, z in places]
        local = split_dot([whole_applied(c, z) - energy[c] * x for (c, z), x in zip(places, o)])
        return finish(places, [keep * x - y for x, y in zip(o, local)], masses)

    masses = groups_of(2, 0, early, finish_early, (zero,) * comps)
    masses = list(groups_of(GROUP, early, levels, solve_late, masses))
    square = jnp.sum(weights[1] * weights[1], axis=0, keepdims=True)

    @pl.when(gx < owners)
    def _():
        wait_bytes(carry.at[pl.ds(0, owners - 1)], recv_sem.at[2])

    @pl.when(gx >= owners)
    def _():
        wait_bytes(carry, recv_sem.at[2])

    def join_mass(owner, held):
        forward, backward = carry[owner, 0:rows, :], carry[owner, rows : 2 * rows, :]
        here = pl.ds(owner * rows, rows)
        held = held + forward * (square * forward - 2.0 * moments[0, here, :])
        held = held + backward * (square * backward - 2.0 * moments[1, here, :])
        return held + 2.0 * float(width) * edge * forward * backward

    joined = lax.fori_loop(0, owners, join_mass, jnp.zeros((rows, lanes), jnp.float32), unroll=4)
    line_row = lax.broadcasted_iota(jnp.int32, (rows, lanes), 0)
    for c in range(comps):
        more = jnp.sum(jnp.where(line_row % comps == c, joined, 0.0), axis=0, keepdims=True)
        masses[c] = jnp.sum(masses[c], axis=0, keepdims=True) + more
    own = lane_of(masses)
    mass_send[0] = own
    mass_recv[0] = own
    copy_sums(mass_send, mass_recv, 3, 1, (gx, 1 - gy))

    def send_mass(step, _):
        spread(mass_send, mass_recv, 3, step)
        return 0

    lax.fori_loop(1, groups, send_mass, 0)

    def update_owner(owner, _):
        places = [(c, owner * per + local, local * comps + c) for local in range(per) for c in range(comps)]
        fields = [
            app[c, z]
            - (
                weights[1] * carry[owner, at : at + 1, :]
                + weights[0] * carry[owner, rows + at : rows + at + 1, :]
            )
            for c, z, at in places
        ]
        for (c, z, at), field in zip(places, fields):
            app[c, z] = field
        levels_here = pl.ds(owner * per, per)
        pltpu.make_async_copy(app.at[:, levels_here], out_hbm.at[:, levels_here], out_sem).start()
        return 0

    lax.fori_loop(0, owners, update_owner, 0)
    totals = gathered(mass_recv, 3, comps)
    for c in range(comps):
        ratio = jnp.sqrt(mean_square[c] / (totals[c] / cells + EPS))
        ratio_ref[c : c + 1, :] = jnp.broadcast_to(ratio, (1, lanes))

    @pl.when(gx < owners)
    def _():
        wait_bytes(tip_send.at[pl.ds(0, owners - 1)], send_sem.at[0])
        wait_bytes(orb_tip_send.at[pl.ds(0, owners - 1)], send_sem.at[4])
        wait_bytes(carry_send.at[pl.ds(1, groups - 1)], send_sem.at[2])

    @pl.when(gx >= owners)
    def _():
        wait_bytes(tip_send, send_sem.at[0])
        wait_bytes(orb_tip_send, send_sem.at[4])

    wait_bytes(sums_recv.at[pl.ds(1, devices - 1)], send_sem.at[1])
    wait_bytes(mass_recv.at[pl.ds(1, devices - 1)], send_sem.at[3])
    pltpu.make_async_copy(app, out_hbm, out_sem).wait()


def scale_kernel(update, ratio, out_hbm, stage, sem):
    comps, levels = update.shape[:2]
    part = levels // SCALE_PARTS
    for c in range(comps):
        for i in range(SCALE_PARTS):
            here = pl.ds(i * part, part)
            stage[c, here] = update[c, here] * ratio[c : c + 1, :]
            pltpu.make_async_copy(stage.at[c, here], out_hbm.at[c, here], sem).start()
    pltpu.make_async_copy(stage, out_hbm, sem).wait()


def shards(orbitals, potential, shift_ratio):
    groups = lax.axis_size("gx")
    columns = lax.axis_size("gy")
    comps, levels, width, lanes = orbitals.shape
    assert columns == 2 and lanes == LANES and 2 * comps * levels == lanes
    assert comps * levels == width
    owners = min(groups, levels)
    rows = comps * (levels // owners)
    early = levels // 2
    planes = comps * levels
    devices = groups * columns
    cells = float(levels * width * groups * lanes * columns)
    f32 = jnp.float32
    update, ratio = pl.pallas_call(
        functools.partial(step_kernel, groups, owners, cells),
        out_shape=(
            jax.ShapeDtypeStruct(orbitals.shape, f32),
            jax.ShapeDtypeStruct((comps, lanes), f32),
        ),
        in_specs=[
            pl.BlockSpec(memory_space=pltpu.SMEM),
            pl.BlockSpec(memory_space=pltpu.HBM),
            pl.BlockSpec(memory_space=pltpu.HBM),
        ],
        out_specs=(
            pl.BlockSpec(memory_space=pl.ANY),
            pl.BlockSpec(memory_space=pltpu.VMEM),
        ),
        scratch_shapes=[
            pltpu.VMEM(orbitals.shape, f32),
            pltpu.VMEM(potential.shape, f32),
            pltpu.VMEM(orbitals.shape, f32),
            pltpu.VMEM((comps, early, width, lanes), f32),
            pltpu.VMEM((width, 3 * width), jnp.bfloat16),
            pltpu.VMEM((2, width, lanes), f32),
            pltpu.VMEM((2, planes, lanes), f32),
            pltpu.VMEM((planes, lanes), f32),
            pltpu.VMEM((width, lanes), f32),
            pltpu.VMEM((width, lanes), f32),
            pltpu.VMEM((2, planes, lanes), f32),
            pltpu.VMEM((2, planes, lanes), f32),
            pltpu.VMEM((owners, 2 * rows, lanes), f32),
            pltpu.VMEM((groups, 2 * rows, lanes), f32),
            pltpu.VMEM((owners, 2 * rows, lanes), f32),
            pltpu.VMEM((groups, 2 * rows, lanes), f32),
            pltpu.VMEM((groups, 2 * rows, lanes), f32),
            pltpu.VMEM((owners, 2 * rows, lanes), f32),
            pltpu.VMEM((1, 1, lanes), f32),
            pltpu.VMEM((devices, 1, lanes), f32),
            pltpu.VMEM((1, 1, lanes), f32),
            pltpu.VMEM((devices, 1, lanes), f32),
            pltpu.SemaphoreType.DMA((CHUNKS + 1,)),
            pltpu.SemaphoreType.DMA((2,)),
            pltpu.SemaphoreType.DMA((2,)),
            pltpu.SemaphoreType.DMA((5,)),
            pltpu.SemaphoreType.DMA((5,)),
            pltpu.SemaphoreType.DMA,
        ],
        compiler_params=pltpu.CompilerParams(
            collective_id=0, has_side_effects=True, vmem_limit_bytes=32 * 1024 * 1024
        ),
        name="power_step",
    )(
        shift_ratio,
        pltpu.with_memory_space_constraint(orbitals, pltpu.HBM),
        pltpu.with_memory_space_constraint(potential, pltpu.HBM),
    )
    return pl.pallas_call(
        scale_kernel,
        out_shape=jax.ShapeDtypeStruct(orbitals.shape, f32),
        in_specs=[pl.BlockSpec(memory_space=pltpu.VMEM), pl.BlockSpec(memory_space=pltpu.VMEM)],
        out_specs=pl.BlockSpec(memory_space=pl.ANY),
        scratch_shapes=[pltpu.VMEM(orbitals.shape, f32), pltpu.SemaphoreType.DMA],
        compiler_params=pltpu.CompilerParams(vmem_limit_bytes=32 * 1024 * 1024),
        name="scale",
    )(
        pltpu.with_memory_space_constraint(update, pltpu.VMEM),
        pltpu.with_memory_space_constraint(ratio, pltpu.VMEM),
    )


def solution(mesh):
    in_specs = (P(None, None, "gx", "gy"), P(None, "gx", "gy"), P())
    out_specs = P(None, None, "gx", "gy")
    return jax.shard_map(shards, mesh=mesh, in_specs=in_specs, out_specs=out_specs, check_vma=False)
```

```python
import functools

import jax
import jax.numpy as jnp
from jax import lax
from jax.experimental import pallas as pl
from jax.experimental.pallas import tpu as pltpu
from jax.sharding import PartitionSpec as P

TAU = 4.0
EPS = 1e-06
COUPLING_FIRST = 0.06
COUPLING_SECOND = 0.05
COUPLING_CROSS = 0.04
MESH = pl.DeviceIdType.MESH
LANES = 128
CHUNKS = 4
GROUP = 4
SCALE_PARTS = 4


def wait_bytes(ref, sem):
    pltpu.make_async_copy(ref, ref, sem).wait()


def step_kernel(
    groups,
    owners,
    cells,
    shift_ratio,
    orb_hbm,
    pot_hbm,
    out_hbm,
    ratio_ref,
    orb,
    pot,
    app,
    shift,
    table,
    weights,
    x_send,
    x_halo,
    y_send,
    y_halo,
    tips_ref,
    moments,
    tip_send,
    tip_recv,
    orb_tip_send,
    orb_tip_recv,
    carry_send,
    carry,
    sums_send,
    sums_recv,
    mass_send,
    mass_recv,
    load_sem,
    halo_send_sem,
    halo_recv_sem,
    send_sem,
    recv_sem,
    out_sem,
):
    comps, levels, width, lanes = orb.shape
    per = levels // owners
    early = shift.shape[1]
    rows = comps * per
    devices = 2 * groups
    gx = lax.axis_index("gx")
    gy = lax.axis_index("gy")
    lane = lax.broadcasted_iota(jnp.int32, (width, lanes), 1)
    row = lax.broadcasted_iota(jnp.int32, (width, lanes), 0)
    lane_row = lax.broadcasted_iota(jnp.int32, (1, lanes), 1)

    def peer(step):
        other = gx + step
        return jnp.where(other >= groups, other - groups, other)

    def device_at(step, side):
        return (peer(step), gy if side == 0 else 1 - gy)

    chunk = levels // CHUNKS
    loads = [
        pltpu.make_async_copy(
            orb_hbm.at[:, pl.ds(i * chunk, chunk)], orb.at[:, pl.ds(i * chunk, chunk)], load_sem.at[i]
        )
        for i in range(CHUNKS)
    ]
    loads.append(pltpu.make_async_copy(pot_hbm, pot, load_sem.at[CHUNKS]))
    for copy in loads:
        copy.start()

    barrier = pltpu.get_barrier_semaphore()

    def greet(step, _):
        for side in range(2):
            pl.semaphore_signal(barrier, inc=1, device_id=device_at(step, side), device_id_type=MESH)
        return 0

    pl.semaphore_signal(barrier, inc=1, device_id=(gx, 1 - gy), device_id_type=MESH)
    lax.fori_loop(1, groups, greet, 0)

    line_cells = width * groups
    sigma_wide = jnp.full((1, 2 * lanes), shift_ratio[0] / float(line_cells * line_cells), jnp.float32)
    decay_wide = jnp.log1p(sigma_wide + jnp.sqrt(sigma_wide * (sigma_wide + 2.0)))
    gain_wide = TAU * jnp.sqrt(sigma_wide / (sigma_wide + 2.0))
    sigma, decay, gain = (x[:, :lanes] for x in (sigma_wide, decay_wide, gain_wide))
    tip_gain = gain * jnp.exp(-decay)
    block = jnp.exp(-decay * float(width))
    inv_wrap = 1.0 / (1.0 - jnp.exp(-decay * float(line_cells)))
    edge = jnp.exp(-decay * float(width - 1))
    eight = jnp.exp(-8.0 * decay)
    keep = 1.0 - TAU * sigma
    position = row.astype(jnp.float32)
    weights[0] = jnp.exp(-decay * (float(width - 1) - position))
    weights[1] = jnp.exp(-decay * position)
    near_last = weights[0, width - 8 : width, :]
    near_first = weights[1, 0:8, :]
    t_row = lax.broadcasted_iota(jnp.int32, (width, 3 * width), 0)
    t_col = lax.broadcasted_iota(jnp.int32, (width, 3 * width), 1)
    t_mod = jnp.where(t_col >= 2 * width, t_col - 2 * width, jnp.where(t_col >= width, t_col - width, t_col))
    distance = jnp.abs(t_row - t_mod).astype(jnp.float32)
    green = gain_wide[:, : 3 * width] * jnp.exp(-decay_wide[:, : 3 * width] * distance)
    high = green.astype(jnp.bfloat16)
    low = (green - high.astype(jnp.float32)).astype(jnp.bfloat16)
    table[...] = jnp.where(t_col >= 2 * width, low.astype(jnp.float32), high.astype(jnp.float32)).astype(jnp.bfloat16)

    def groups_of(size, first, last, body, held):
        return lax.fori_loop(0, (last - first) // size, lambda i, x: body(first + i * size, x), held)

    def weighted(x):
        parts = [x[i : i + 8] for i in range(0, width, 8)]
        to_last, to_first = parts[0], parts[-1]
        for i in range(1, len(parts)):
            to_last = to_last * eight + parts[i]
            to_first = to_first * eight + parts[-1 - i]
        return (
            jnp.sum(to_last * near_last, axis=0, keepdims=True),
            jnp.sum(to_first * near_first, axis=0, keepdims=True),
        )

    def copy_tips(source, target, which, step):
        def go():
            pltpu.make_async_remote_copy(
                source.at[peer(step)],
                target.at[groups - step],
                send_sem.at[which],
                recv_sem.at[which],
                device_id=device_at(step, 0),
                device_id_type=MESH,
            ).start()

        if owners == groups:
            go()
        else:
            pl.when(peer(step) < owners)(go)

    def pack(start, held):
        rows_out = []
        ends = []
        for i in range(GROUP):
            z = start + i
            for c in range(comps):
                plane = orb[c, z]
                index = z * comps + c
                held = jnp.where(lane // 2 == index, pltpu.roll(plane, 2 * index + 1, 1), held)
                rows_out.append((index, plane[width - 1 : width], plane[0:1]))
                ends.append((lax.div(start, per) + i // per, i % per * comps + c, weighted(plane)))
        for index, last, first in rows_out:
            x_send[0, pl.ds(index, 1), :] = last
            x_send[1, pl.ds(index, 1), :] = first
        for owner, at, tips in ends:
            for j, tip in enumerate(tips):
                orb_tip_send[owner, j * rows + at : j * rows + at + 1, :] = tip
        return held

    held = jnp.zeros((width, lanes), jnp.float32)
    for i in range(CHUNKS):
        loads[i].wait()
        held = groups_of(GROUP, i * chunk, (i + 1) * chunk, pack, held)
    y_send[...] = held

    pl.semaphore_wait(barrier, devices - 1)
    halos = [
        pltpu.make_async_remote_copy(
            src, dst, halo_send_sem.at[i], halo_recv_sem.at[i], device_id=target, device_id_type=MESH
        )
        for i, (src, dst, target) in enumerate(
            (
                (y_send, y_halo, (gx, 1 - gy)),
                (x_send.at[1], x_halo, (peer(groups - 1), gy)),
            )
        )
    ]
    for copy in halos:
        copy.start()
    loads[CHUNKS].wait()

    def fold(x):
        total = x[0:8]
        for i in range(8, width, 8):
            total = total + x[i : i + 8]
        return total

    def apply_level(z, sums, stores):
        o = [orb[c, z] for c in range(comps)]
        before = lax.rem(z + levels - 1, levels)
        after = lax.rem(z + 1, levels)
        squares = [x * x for x in o]
        density = (
            COUPLING_FIRST * squares[0] + COUPLING_CROSS * squares[1],
            COUPLING_CROSS * squares[0] + COUPLING_SECOND * squares[1],
        )
        trap = pot[z] + 2.0
        result = []
        for c in range(comps):
            mine = o[c]
            near = pltpu.roll(mine, 1, 1) + pltpu.roll(mine, lanes - 1, 1)
            near = near + orb[c, before] + orb[c, after]
            applied = (trap + density[c]) * mine - 0.5 * near
            stores.append((c, z, applied, weighted(applied)))
            along = mine - pltpu.roll(mine, width - 1, 0)
            result.append(sums[2 * c] + fold(mine * (applied + along)))
            result.append(sums[2 * c + 1] + fold(squares[c]))
        return tuple(result)

    def apply_pair(start, sums):
        stores = []
        for i in range(2):
            sums = apply_level(start + i, sums, stores)
        for c, z, applied, tips in stores:
            app[c, z] = applied
            for q, tip in enumerate(tips):
                tips_ref[q, pl.ds(z * comps + c, 1), :] = tip
        return sums

    zero = jnp.zeros((8, lanes), jnp.float32)
    sums = (zero,) * (2 * comps)
    if owners == groups and levels == 2 * groups:

        def apply_and_send(step, sums):
            copy_tips(orb_tip_send, orb_tip_recv, 4, step)
            return apply_pair(2 * step, sums)

        sums = lax.fori_loop(1, groups, apply_and_send, apply_pair(0, sums))
    else:

        def send_early(step, _):
            copy_tips(orb_tip_send, orb_tip_recv, 4, step)
            return 0

        lax.fori_loop(1, groups, send_early, 0)
        sums = groups_of(2, 0, levels, apply_pair, sums)
    sums = list(sums)

    for copy in halos:
        copy.wait()
    lack = y_halo[...] - y_send[...]
    lack = jnp.where(lane % 2 == 0, pltpu.roll(lack, lanes - 1, 1), pltpu.roll(lack, 1, 1))
    y_halo[...] = lack
    x_cross = x_send[0] * (x_halo[...] - x_send[1])
    y_cross = y_send[...] * lack
    for c in range(comps):
        sums[2 * c] = sums[2 * c] - fold(jnp.where(row % comps == c, x_cross, 0.0))
        sums[2 * c] = sums[2 * c] - 0.5 * fold(jnp.where(lane // 2 % comps == c, y_cross, 0.0))
    for j in range(2):
        ends = jnp.sum(fold(weights[j] * lack), axis=0, keepdims=True)
        last = jnp.sum(jnp.where(lane == 2 * row, ends, 0.0), axis=1, keepdims=True)
        first = jnp.sum(jnp.where(lane == 2 * row + 1, ends, 0.0), axis=1, keepdims=True)
        more = jnp.where(lane == 0, first, jnp.where(lane == lanes - 1, last, 0.0))
        tips_ref[j] = tips_ref[j] - 0.5 * more

    def lane_of(values):
        packed = jnp.zeros((1, lanes), jnp.float32)
        for i, x in enumerate(values):
            whole = jnp.sum(jnp.sum(x, axis=0, keepdims=True), axis=1, keepdims=True)
            packed = jnp.where(lane_row == i, whole, packed)
        return packed

    def copy_sums(source, target, which, slot, device):
        pltpu.make_async_remote_copy(
            source.at[0],
            target.at[slot],
            send_sem.at[which],
            recv_sem.at[which],
            device_id=device,
            device_id_type=MESH,
        ).start()

    def spread(source, target, which, step):
        for side in range(2):
            copy_sums(source, target, which, 2 * (groups - step) + side, device_at(step, side))

    def gathered(target, which, count):
        wait_bytes(target.at[pl.ds(1, devices - 1)], recv_sem.at[which])
        total = jnp.sum(target[...], axis=0)
        return [
            jnp.sum(jnp.where(lane_row == i, total, 0.0), axis=1, keepdims=True) for i in range(count)
        ]

    own = lane_of(sums)
    sums_send[0] = own
    sums_recv[0] = own
    def fill_tips(owner, _):
        for j in range(2):
            tip_send[owner, j * rows : (j + 1) * rows, :] = tips_ref[j, pl.ds(owner * rows, rows), :]
        return 0

    lax.fori_loop(0, owners, fill_tips, 0, unroll=4)

    def send_line_ends(step, _):
        copy_tips(tip_send, tip_recv, 0, step)
        spread(sums_send, sums_recv, 1, step)
        return 0

    copy_sums(sums_send, sums_recv, 1, 1, (gx, 1 - gy))
    lax.fori_loop(1, groups, send_line_ends, 0)

    @pl.when(gx < owners)
    def _():
        tip_recv[0] = tip_send[lax.rem(gx, owners)]
        orb_tip_recv[0] = orb_tip_send[lax.rem(gx, owners)]

    def split_dot(fields):
        wide = jnp.concatenate(fields, axis=1)
        high = wide.astype(jnp.bfloat16)
        low = (wide - high.astype(jnp.float32)).astype(jnp.bfloat16)
        local = jnp.dot(
            table[...], jnp.concatenate([high, low, high], axis=0), preferred_element_type=jnp.float32
        )
        return [local[:, i * lanes : (i + 1) * lanes] for i in range(len(fields))]

    def whole_applied(c, z):
        index = z * comps + c
        ends = pltpu.roll(y_halo[...], lanes - 1 - 2 * index, 1)
        ends = jnp.where((lane == 0) | (lane == lanes - 1), ends, 0.0)
        return app[c, z] - 0.5 * ends

    def solve_early(start, _):
        places = [(c, start + i) for i in range(GROUP) for c in range(comps)]
        o = [orb[c, z] for c, z in places]
        local = split_dot([whole_applied(c, z) for c, z in places] + o)
        for i, (c, z) in enumerate(places):
            app[c, z] = keep * o[i] - local[i]
            shift[c, z] = local[len(places) + i]
        return 0

    groups_of(GROUP, 0, early, solve_early, 0)

    totals = gathered(sums_recv, 1, 2 * comps)
    mean_square = [totals[2 * c + 1] / cells for c in range(comps)]
    energy = [totals[2 * c] / cells / (mean_square[c] + EPS) + sigma for c in range(comps)]

    @pl.when(gx < owners)
    def _():
        wait_bytes(tip_recv.at[pl.ds(1, groups - 1)], recv_sem.at[0])
        wait_bytes(orb_tip_recv.at[pl.ds(1, groups - 1)], recv_sem.at[4])
        tip_row = lax.broadcasted_iota(jnp.int32, (2 * rows, lanes), 0)
        scale = jnp.where(tip_row % 2 == 0, energy[0], energy[1])

        def tips(k):
            return tip_recv[k] - scale * orb_tip_recv[k]

        def collect(k, held):
            ahead, behind = held
            return block * ahead + tips(k), block * behind + tips(groups - 1 - k)

        start = jnp.zeros((2 * rows, lanes), jnp.float32)
        ahead, behind = lax.fori_loop(0, groups, collect, (start, start), unroll=4)

        def hand_out(k, held):
            ahead, behind = held
            back = groups - 1 - k
            carry_send[k, 0:rows, :] = ahead[0:rows]
            carry_send[back, rows : 2 * rows, :] = behind[rows : 2 * rows]
            return block * ahead + tip_gain * tips(k), block * behind + tip_gain * tips(back)

        factor = tip_gain * inv_wrap
        lax.fori_loop(0, groups, hand_out, (factor * ahead, factor * behind), unroll=4)

        def send(step, _):
            pltpu.make_async_remote_copy(
                carry_send.at[step],
                carry.at[gx],
                send_sem.at[2],
                recv_sem.at[2],
                device_id=(peer(step), gy),
                device_id_type=MESH,
            ).start()
            return 0

        lax.fori_loop(1, groups, send, 0)
        carry[lax.rem(gx, owners)] = carry_send[0]

    def finish(places, fields, masses):
        masses = list(masses)
        ends = []
        for (c, z), own in zip(places, fields):
            ends.append(weighted(own))
            masses[c] = masses[c] + fold(own * own)
        for (c, z), own, (to_last, to_first) in zip(places, fields, ends):
            app[c, z] = own
            moments[0, pl.ds(z * comps + c, 1), :] = to_first
            moments[1, pl.ds(z * comps + c, 1), :] = to_last
        return tuple(masses)

    def finish_early(start, masses):
        places = [(c, start + i) for i in range(2) for c in range(comps)]
        return finish(places, [app[c, z] + energy[c] * shift[c, z] for c, z in places], masses)

    def solve_late(start, masses):
        places = [(c, start + i) for i in range(GROUP) for c in range(comps)]
        o = [orb[c, z] for c, z in places]
        local = split_dot([whole_applied(c, z) - energy[c] * x for (c, z), x in zip(places, o)])
        return finish(places, [keep * x - y for x, y in zip(o, local)], masses)

    masses = groups_of(2, 0, early, finish_early, (zero,) * comps)
    masses = list(groups_of(GROUP, early, levels, solve_late, masses))
    square = jnp.sum(weights[1] * weights[1], axis=0, keepdims=True)

    @pl.when(gx < owners)
    def _():
        wait_bytes(carry.at[pl.ds(0, owners - 1)], recv_sem.at[2])

    @pl.when(gx >= owners)
    def _():
        wait_bytes(carry, recv_sem.at[2])

    def join_mass(owner, held):
        forward, backward = carry[owner, 0:rows, :], carry[owner, rows : 2 * rows, :]
        here = pl.ds(owner * rows, rows)
        held = held + forward * (square * forward - 2.0 * moments[0, here, :])
        held = held + backward * (square * backward - 2.0 * moments[1, here, :])
        return held + 2.0 * float(width) * edge * forward * backward

    joined = lax.fori_loop(0, owners, join_mass, jnp.zeros((rows, lanes), jnp.float32), unroll=4)
    line_row = lax.broadcasted_iota(jnp.int32, (rows, lanes), 0)
    for c in range(comps):
        more = jnp.sum(jnp.where(line_row % comps == c, joined, 0.0), axis=0, keepdims=True)
        masses[c] = jnp.sum(masses[c], axis=0, keepdims=True) + more
    own = lane_of(masses)
    mass_send[0] = own
    mass_recv[0] = own
    copy_sums(mass_send, mass_recv, 3, 1, (gx, 1 - gy))

    def send_mass(step, _):
        spread(mass_send, mass_recv, 3, step)
        return 0

    lax.fori_loop(1, groups, send_mass, 0)

    def update_owner(owner, _):
        places = [(c, owner * per + local, local * comps + c) for local in range(per) for c in range(comps)]
        fields = [
            app[c, z]
            - (
                weights[1] * carry[owner, at : at + 1, :]
                + weights[0] * carry[owner, rows + at : rows + at + 1, :]
            )
            for c, z, at in places
        ]
        for (c, z, at), field in zip(places, fields):
            app[c, z] = field
        levels_here = pl.ds(owner * per, per)
        pltpu.make_async_copy(app.at[:, levels_here], out_hbm.at[:, levels_here], out_sem).start()
        return 0

    lax.fori_loop(0, owners, update_owner, 0)
    totals = gathered(mass_recv, 3, comps)
    for c in range(comps):
        ratio = jnp.sqrt(mean_square[c] / (totals[c] / cells + EPS))
        ratio_ref[c : c + 1, :] = jnp.broadcast_to(ratio, (1, lanes))

    @pl.when(gx < owners)
    def _():
        wait_bytes(tip_send.at[pl.ds(0, owners - 1)], send_sem.at[0])
        wait_bytes(orb_tip_send.at[pl.ds(0, owners - 1)], send_sem.at[4])
        wait_bytes(carry_send.at[pl.ds(1, groups - 1)], send_sem.at[2])

    @pl.when(gx >= owners)
    def _():
        wait_bytes(tip_send, send_sem.at[0])
        wait_bytes(orb_tip_send, send_sem.at[4])

    wait_bytes(sums_recv.at[pl.ds(1, devices - 1)], send_sem.at[1])
    wait_bytes(mass_recv.at[pl.ds(1, devices - 1)], send_sem.at[3])
    pltpu.make_async_copy(app, out_hbm, out_sem).wait()


def scale_kernel(update, ratio, out_hbm, stage, sem):
    comps, levels = update.shape[:2]
    part = levels // SCALE_PARTS
    for c in range(comps):
        for i in range(SCALE_PARTS):
            here = pl.ds(i * part, part)
            stage[c, here] = update[c, here] * ratio[c : c + 1, :]
            pltpu.make_async_copy(stage.at[c, here], out_hbm.at[c, here], sem).start()
    pltpu.make_async_copy(stage, out_hbm, sem).wait()


def shards(orbitals, potential, shift_ratio):
    groups = lax.axis_size("gx")
    columns = lax.axis_size("gy")
    comps, levels, width, lanes = orbitals.shape
    assert columns == 2 and lanes == LANES and 2 * comps * levels == lanes
    assert comps * levels == width
    owners = min(groups, levels)
    rows = comps * (levels // owners)
    early = levels // 4
    planes = comps * levels
    devices = groups * columns
    cells = float(levels * width * groups * lanes * columns)
    f32 = jnp.float32
    update, ratio = pl.pallas_call(
        functools.partial(step_kernel, groups, owners, cells),
        out_shape=(
            jax.ShapeDtypeStruct(orbitals.shape, f32),
            jax.ShapeDtypeStruct((comps, lanes), f32),
        ),
        in_specs=[
            pl.BlockSpec(memory_space=pltpu.SMEM),
            pl.BlockSpec(memory_space=pltpu.HBM),
            pl.BlockSpec(memory_space=pltpu.HBM),
        ],
        out_specs=(
            pl.BlockSpec(memory_space=pl.ANY),
            pl.BlockSpec(memory_space=pltpu.VMEM),
        ),
        scratch_shapes=[
            pltpu.VMEM(orbitals.shape, f32),
            pltpu.VMEM(potential.shape, f32),
            pltpu.VMEM(orbitals.shape, f32),
            pltpu.VMEM((comps, early, width, lanes), f32),
            pltpu.VMEM((width, 3 * width), jnp.bfloat16),
            pltpu.VMEM((2, width, lanes), f32),
            pltpu.VMEM((2, planes, lanes), f32),
            pltpu.VMEM((planes, lanes), f32),
            pltpu.VMEM((width, lanes), f32),
            pltpu.VMEM((width, lanes), f32),
            pltpu.VMEM((2, planes, lanes), f32),
            pltpu.VMEM((2, planes, lanes), f32),
            pltpu.VMEM((owners, 2 * rows, lanes), f32),
            pltpu.VMEM((groups, 2 * rows, lanes), f32),
            pltpu.VMEM((owners, 2 * rows, lanes), f32),
            pltpu.VMEM((groups, 2 * rows, lanes), f32),
            pltpu.VMEM((groups, 2 * rows, lanes), f32),
            pltpu.VMEM((owners, 2 * rows, lanes), f32),
            pltpu.VMEM((1, 1, lanes), f32),
            pltpu.VMEM((devices, 1, lanes), f32),
            pltpu.VMEM((1, 1, lanes), f32),
            pltpu.VMEM((devices, 1, lanes), f32),
            pltpu.SemaphoreType.DMA((CHUNKS + 1,)),
            pltpu.SemaphoreType.DMA((2,)),
            pltpu.SemaphoreType.DMA((2,)),
            pltpu.SemaphoreType.DMA((5,)),
            pltpu.SemaphoreType.DMA((5,)),
            pltpu.SemaphoreType.DMA,
        ],
        compiler_params=pltpu.CompilerParams(
            collective_id=0, has_side_effects=True, vmem_limit_bytes=32 * 1024 * 1024
        ),
        name="power_step",
    )(
        shift_ratio,
        pltpu.with_memory_space_constraint(orbitals, pltpu.HBM),
        pltpu.with_memory_space_constraint(potential, pltpu.HBM),
    )
    return pl.pallas_call(
        scale_kernel,
        out_shape=jax.ShapeDtypeStruct(orbitals.shape, f32),
        in_specs=[pl.BlockSpec(memory_space=pltpu.VMEM), pl.BlockSpec(memory_space=pltpu.VMEM)],
        out_specs=pl.BlockSpec(memory_space=pl.ANY),
        scratch_shapes=[pltpu.VMEM(orbitals.shape, f32), pltpu.SemaphoreType.DMA],
        compiler_params=pltpu.CompilerParams(vmem_limit_bytes=32 * 1024 * 1024),
        name="scale",
    )(
        pltpu.with_memory_space_constraint(update, pltpu.VMEM),
        pltpu.with_memory_space_constraint(ratio, pltpu.VMEM),
    )


def solution(mesh):
    in_specs = (P(None, None, "gx", "gy"), P(None, "gx", "gy"), P())
    out_specs = P(None, None, "gx", "gy")
    return jax.shard_map(shards, mesh=mesh, in_specs=in_specs, out_specs=out_specs, check_vma=False)
```

```python
import functools

import jax
import jax.numpy as jnp
from jax import lax
from jax.experimental import pallas as pl
from jax.experimental.pallas import tpu as pltpu
from jax.sharding import PartitionSpec as P

TAU = 4.0
EPS = 1e-06
COUPLING_FIRST = 0.06
COUPLING_SECOND = 0.05
COUPLING_CROSS = 0.04
MESH = pl.DeviceIdType.MESH
LANES = 128
CHUNKS = 8
GROUP = 4
SCALE_PARTS = 4


def wait_bytes(ref, sem):
    pltpu.make_async_copy(ref, ref, sem).wait()


def step_kernel(
    groups,
    owners,
    cells,
    shift_ratio,
    orb_hbm,
    pot_hbm,
    out_hbm,
    ratio_ref,
    orb,
    pot,
    app,
    shift,
    table,
    weights,
    x_send,
    x_halo,
    y_send,
    y_halo,
    tips_ref,
    moments,
    tip_send,
    tip_recv,
    orb_tip_send,
    orb_tip_recv,
    carry_send,
    carry,
    sums_send,
    sums_recv,
    mass_send,
    mass_recv,
    load_sem,
    halo_send_sem,
    halo_recv_sem,
    send_sem,
    recv_sem,
    out_sem,
):
    comps, levels, width, lanes = orb.shape
    per = levels // owners
    early = shift.shape[1]
    rows = comps * per
    devices = 2 * groups
    gx = lax.axis_index("gx")
    gy = lax.axis_index("gy")
    lane = lax.broadcasted_iota(jnp.int32, (width, lanes), 1)
    row = lax.broadcasted_iota(jnp.int32, (width, lanes), 0)
    lane_row = lax.broadcasted_iota(jnp.int32, (1, lanes), 1)

    def peer(step):
        other = gx + step
        return jnp.where(other >= groups, other - groups, other)

    def device_at(step, side):
        return (peer(step), gy if side == 0 else 1 - gy)

    chunk = levels // CHUNKS
    loads = [
        pltpu.make_async_copy(
            orb_hbm.at[:, pl.ds(i * chunk, chunk)], orb.at[:, pl.ds(i * chunk, chunk)], load_sem.at[i]
        )
        for i in range(CHUNKS)
    ]
    loads.append(pltpu.make_async_copy(pot_hbm, pot, load_sem.at[CHUNKS]))
    for copy in loads:
        copy.start()

    barrier = pltpu.get_barrier_semaphore()

    def greet(step, _):
        for side in range(2):
            pl.semaphore_signal(barrier, inc=1, device_id=device_at(step, side), device_id_type=MESH)
        return 0

    pl.semaphore_signal(barrier, inc=1, device_id=(gx, 1 - gy), device_id_type=MESH)
    lax.fori_loop(1, groups, greet, 0)

    line_cells = width * groups
    sigma_wide = jnp.full((1, 2 * lanes), shift_ratio[0] / float(line_cells * line_cells), jnp.float32)
    decay_wide = jnp.log1p(sigma_wide + jnp.sqrt(sigma_wide * (sigma_wide + 2.0)))
    gain_wide = TAU * jnp.sqrt(sigma_wide / (sigma_wide + 2.0))
    sigma, decay, gain = (x[:, :lanes] for x in (sigma_wide, decay_wide, gain_wide))
    tip_gain = gain * jnp.exp(-decay)
    block = jnp.exp(-decay * float(width))
    inv_wrap = 1.0 / (1.0 - jnp.exp(-decay * float(line_cells)))
    edge = jnp.exp(-decay * float(width - 1))
    eight = jnp.exp(-8.0 * decay)
    keep = 1.0 - TAU * sigma
    position = row.astype(jnp.float32)
    weights[0] = jnp.exp(-decay * (float(width - 1) - position))
    weights[1] = jnp.exp(-decay * position)
    near_last = weights[0, width - 8 : width, :]
    near_first = weights[1, 0:8, :]
    t_row = lax.broadcasted_iota(jnp.int32, (width, 3 * width), 0)
    t_col = lax.broadcasted_iota(jnp.int32, (width, 3 * width), 1)
    t_mod = jnp.where(t_col >= 2 * width, t_col - 2 * width, jnp.where(t_col >= width, t_col - width, t_col))
    distance = jnp.abs(t_row - t_mod).astype(jnp.float32)
    green = gain_wide[:, : 3 * width] * jnp.exp(-decay_wide[:, : 3 * width] * distance)
    high = green.astype(jnp.bfloat16)
    low = (green - high.astype(jnp.float32)).astype(jnp.bfloat16)
    table[...] = jnp.where(t_col >= 2 * width, low.astype(jnp.float32), high.astype(jnp.float32)).astype(jnp.bfloat16)

    def groups_of(size, first, last, body, held):
        return lax.fori_loop(0, (last - first) // size, lambda i, x: body(first + i * size, x), held)

    def weighted(x):
        parts = [x[i : i + 8] for i in range(0, width, 8)]
        to_last, to_first = parts[0], parts[-1]
        for i in range(1, len(parts)):
            to_last = to_last * eight + parts[i]
            to_first = to_first * eight + parts[-1 - i]
        return (
            jnp.sum(to_last * near_last, axis=0, keepdims=True),
            jnp.sum(to_first * near_first, axis=0, keepdims=True),
        )

    def copy_tips(source, target, which, step):
        def go():
            pltpu.make_async_remote_copy(
                source.at[peer(step)],
                target.at[groups - step],
                send_sem.at[which],
                recv_sem.at[which],
                device_id=device_at(step, 0),
                device_id_type=MESH,
            ).start()

        if owners == groups:
            go()
        else:
            pl.when(peer(step) < owners)(go)

    def pack(start, held):
        rows_out = []
        ends = []
        for i in range(GROUP):
            z = start + i
            for c in range(comps):
                plane = orb[c, z]
                index = z * comps + c
                held = jnp.where(lane // 2 == index, pltpu.roll(plane, 2 * index + 1, 1), held)
                rows_out.append((index, plane[width - 1 : width], plane[0:1]))
                ends.append((lax.div(start, per) + i // per, i % per * comps + c, weighted(plane)))
        for index, last, first in rows_out:
            x_send[0, pl.ds(index, 1), :] = last
            x_send[1, pl.ds(index, 1), :] = first
        for owner, at, tips in ends:
            for j, tip in enumerate(tips):
                orb_tip_send[owner, j * rows + at : j * rows + at + 1, :] = tip
        return held

    held = jnp.zeros((width, lanes), jnp.float32)
    for i in range(CHUNKS):
        loads[i].wait()
        held = groups_of(GROUP, i * chunk, (i + 1) * chunk, pack, held)
    y_send[...] = held

    pl.semaphore_wait(barrier, devices - 1)
    halos = [
        pltpu.make_async_remote_copy(
            src, dst, halo_send_sem.at[i], halo_recv_sem.at[i], device_id=target, device_id_type=MESH
        )
        for i, (src, dst, target) in enumerate(
            (
                (y_send, y_halo, (gx, 1 - gy)),
                (x_send.at[1], x_halo, (peer(groups - 1), gy)),
            )
        )
    ]
    for copy in halos:
        copy.start()
    loads[CHUNKS].wait()

    def fold(x):
        total = x[0:8]
        for i in range(8, width, 8):
            total = total + x[i : i + 8]
        return total

    def apply_level(z, sums, stores):
        o = [orb[c, z] for c in range(comps)]
        before = lax.rem(z + levels - 1, levels)
        after = lax.rem(z + 1, levels)
        squares = [x * x for x in o]
        density = (
            COUPLING_FIRST * squares[0] + COUPLING_CROSS * squares[1],
            COUPLING_CROSS * squares[0] + COUPLING_SECOND * squares[1],
        )
        trap = pot[z] + 2.0
        result = []
        for c in range(comps):
            mine = o[c]
            near = pltpu.roll(mine, 1, 1) + pltpu.roll(mine, lanes - 1, 1)
            near = near + orb[c, before] + orb[c, after]
            applied = (trap + density[c]) * mine - 0.5 * near
            stores.append((c, z, applied, weighted(applied)))
            along = mine - pltpu.roll(mine, width - 1, 0)
            result.append(sums[2 * c] + fold(mine * (applied + along)))
            result.append(sums[2 * c + 1] + fold(squares[c]))
        return tuple(result)

    def apply_pair(start, sums):
        stores = []
        for i in range(2):
            sums = apply_level(start + i, sums, stores)
        for c, z, applied, tips in stores:
            app[c, z] = applied
            for q, tip in enumerate(tips):
                tips_ref[q, pl.ds(z * comps + c, 1), :] = tip
        return sums

    zero = jnp.zeros((8, lanes), jnp.float32)
    sums = (zero,) * (2 * comps)
    if owners == groups and levels == 2 * groups:

        def apply_and_send(step, sums):
            copy_tips(orb_tip_send, orb_tip_recv, 4, step)
            return apply_pair(2 * step, sums)

        sums = lax.fori_loop(1, groups, apply_and_send, apply_pair(0, sums))
    else:

        def send_early(step, _):
            copy_tips(orb_tip_send, orb_tip_recv, 4, step)
            return 0

        lax.fori_loop(1, groups, send_early, 0)
        sums = groups_of(2, 0, levels, apply_pair, sums)
    sums = list(sums)

    for copy in halos:
        copy.wait()
    lack = y_halo[...] - y_send[...]
    lack = jnp.where(lane % 2 == 0, pltpu.roll(lack, lanes - 1, 1), pltpu.roll(lack, 1, 1))
    y_halo[...] = lack
    x_cross = x_send[0] * (x_halo[...] - x_send[1])
    y_cross = y_send[...] * lack
    for c in range(comps):
        sums[2 * c] = sums[2 * c] - fold(jnp.where(row % comps == c, x_cross, 0.0))
        sums[2 * c] = sums[2 * c] - 0.5 * fold(jnp.where(lane // 2 % comps == c, y_cross, 0.0))
    for j in range(2):
        ends = jnp.sum(fold(weights[j] * lack), axis=0, keepdims=True)
        last = jnp.sum(jnp.where(lane == 2 * row, ends, 0.0), axis=1, keepdims=True)
        first = jnp.sum(jnp.where(lane == 2 * row + 1, ends, 0.0), axis=1, keepdims=True)
        more = jnp.where(lane == 0, first, jnp.where(lane == lanes - 1, last, 0.0))
        tips_ref[j] = tips_ref[j] - 0.5 * more

    def lane_of(values):
        packed = jnp.zeros((1, lanes), jnp.float32)
        for i, x in enumerate(values):
            whole = jnp.sum(jnp.sum(x, axis=0, keepdims=True), axis=1, keepdims=True)
            packed = jnp.where(lane_row == i, whole, packed)
        return packed

    def copy_sums(source, target, which, slot, device):
        pltpu.make_async_remote_copy(
            source.at[0],
            target.at[slot],
            send_sem.at[which],
            recv_sem.at[which],
            device_id=device,
            device_id_type=MESH,
        ).start()

    def spread(source, target, which, step):
        for side in range(2):
            copy_sums(source, target, which, 2 * (groups - step) + side, device_at(step, side))

    def gathered(target, which, count):
        wait_bytes(target.at[pl.ds(1, devices - 1)], recv_sem.at[which])
        total = jnp.sum(target[...], axis=0)
        return [
            jnp.sum(jnp.where(lane_row == i, total, 0.0), axis=1, keepdims=True) for i in range(count)
        ]

    own = lane_of(sums)
    sums_send[0] = own
    sums_recv[0] = own
    def fill_tips(owner, _):
        for j in range(2):
            tip_send[owner, j * rows : (j + 1) * rows, :] = tips_ref[j, pl.ds(owner * rows, rows), :]
        return 0

    lax.fori_loop(0, owners, fill_tips, 0, unroll=4)

    def send_line_ends(step, _):
        copy_tips(tip_send, tip_recv, 0, step)
        spread(sums_send, sums_recv, 1, step)
        return 0

    copy_sums(sums_send, sums_recv, 1, 1, (gx, 1 - gy))
    lax.fori_loop(1, groups, send_line_ends, 0)

    @pl.when(gx < owners)
    def _():
        tip_recv[0] = tip_send[lax.rem(gx, owners)]
        orb_tip_recv[0] = orb_tip_send[lax.rem(gx, owners)]

    def split_dot(fields):
        wide = jnp.concatenate(fields, axis=1)
        high = wide.astype(jnp.bfloat16)
        low = (wide - high.astype(jnp.float32)).astype(jnp.bfloat16)
        local = jnp.dot(
            table[...], jnp.concatenate([high, low, high], axis=0), preferred_element_type=jnp.float32
        )
        return [local[:, i * lanes : (i + 1) * lanes] for i in range(len(fields))]

    def whole_applied(c, z):
        index = z * comps + c
        ends = pltpu.roll(y_halo[...], lanes - 1 - 2 * index, 1)
        ends = jnp.where((lane == 0) | (lane == lanes - 1), ends, 0.0)
        return app[c, z] - 0.5 * ends

    def solve_early(start, _):
        places = [(c, start + i) for i in range(GROUP) for c in range(comps)]
        o = [orb[c, z] for c, z in places]
        local = split_dot([whole_applied(c, z) for c, z in places] + o)
        for i, (c, z) in enumerate(places):
            app[c, z] = keep * o[i] - local[i]
            shift[c, z] = local[len(places) + i]
        return 0

    groups_of(GROUP, 0, early, solve_early, 0)

    totals = gathered(sums_recv, 1, 2 * comps)
    mean_square = [totals[2 * c + 1] / cells for c in range(comps)]
    energy = [totals[2 * c] / cells / (mean_square[c] + EPS) + sigma for c in range(comps)]

    @pl.when(gx < owners)
    def _():
        wait_bytes(tip_recv.at[pl.ds(1, groups - 1)], recv_sem.at[0])
        wait_bytes(orb_tip_recv.at[pl.ds(1, groups - 1)], recv_sem.at[4])
        tip_row = lax.broadcasted_iota(jnp.int32, (2 * rows, lanes), 0)
        scale = jnp.where(tip_row % 2 == 0, energy[0], energy[1])

        def tips(k):
            return tip_recv[k] - scale * orb_tip_recv[k]

        def collect(k, held):
            ahead, behind = held
            return block * ahead + tips(k), block * behind + tips(groups - 1 - k)

        start = jnp.zeros((2 * rows, lanes), jnp.float32)
        ahead, behind = lax.fori_loop(0, groups, collect, (start, start), unroll=4)

        def hand_out(k, held):
            ahead, behind = held
            back = groups - 1 - k
            carry_send[k, 0:rows, :] = ahead[0:rows]
            carry_send[back, rows : 2 * rows, :] = behind[rows : 2 * rows]
            return block * ahead + tip_gain * tips(k), block * behind + tip_gain * tips(back)

        factor = tip_gain * inv_wrap
        lax.fori_loop(0, groups, hand_out, (factor * ahead, factor * behind), unroll=4)

        def send(step, _):
            pltpu.make_async_remote_copy(
                carry_send.at[step],
                carry.at[gx],
                send_sem.at[2],
                recv_sem.at[2],
                device_id=(peer(step), gy),
                device_id_type=MESH,
            ).start()
            return 0

        lax.fori_loop(1, groups, send, 0)
        carry[lax.rem(gx, owners)] = carry_send[0]

    def finish(places, fields, masses):
        masses = list(masses)
        ends = []
        for (c, z), own in zip(places, fields):
            ends.append(weighted(own))
            masses[c] = masses[c] + fold(own * own)
        for (c, z), own, (to_last, to_first) in zip(places, fields, ends):
            app[c, z] = own
            moments[0, pl.ds(z * comps + c, 1), :] = to_first
            moments[1, pl.ds(z * comps + c, 1), :] = to_last
        return tuple(masses)

    def finish_early(start, masses):
        places = [(c, start + i) for i in range(2) for c in range(comps)]
        return finish(places, [app[c, z] + energy[c] * shift[c, z] for c, z in places], masses)

    def solve_late(start, masses):
        places = [(c, start + i) for i in range(GROUP) for c in range(comps)]
        o = [orb[c, z] for c, z in places]
        local = split_dot([whole_applied(c, z) - energy[c] * x for (c, z), x in zip(places, o)])
        return finish(places, [keep * x - y for x, y in zip(o, local)], masses)

    masses = groups_of(2, 0, early, finish_early, (zero,) * comps)
    masses = list(groups_of(GROUP, early, levels, solve_late, masses))
    square = jnp.sum(weights[1] * weights[1], axis=0, keepdims=True)

    @pl.when(gx < owners)
    def _():
        wait_bytes(carry.at[pl.ds(0, owners - 1)], recv_sem.at[2])

    @pl.when(gx >= owners)
    def _():
        wait_bytes(carry, recv_sem.at[2])

    def join_mass(owner, held):
        forward, backward = carry[owner, 0:rows, :], carry[owner, rows : 2 * rows, :]
        here = pl.ds(owner * rows, rows)
        held = held + forward * (square * forward - 2.0 * moments[0, here, :])
        held = held + backward * (square * backward - 2.0 * moments[1, here, :])
        return held + 2.0 * float(width) * edge * forward * backward

    joined = lax.fori_loop(0, owners, join_mass, jnp.zeros((rows, lanes), jnp.float32), unroll=4)
    line_row = lax.broadcasted_iota(jnp.int32, (rows, lanes), 0)
    for c in range(comps):
        more = jnp.sum(jnp.where(line_row % comps == c, joined, 0.0), axis=0, keepdims=True)
        masses[c] = jnp.sum(masses[c], axis=0, keepdims=True) + more
    own = lane_of(masses)
    mass_send[0] = own
    mass_recv[0] = own
    copy_sums(mass_send, mass_recv, 3, 1, (gx, 1 - gy))

    def send_mass(step, _):
        spread(mass_send, mass_recv, 3, step)
        return 0

    lax.fori_loop(1, groups, send_mass, 0)

    def update_owner(owner, _):
        places = [(c, owner * per + local, local * comps + c) for local in range(per) for c in range(comps)]
        fields = [
            app[c, z]
            - (
                weights[1] * carry[owner, at : at + 1, :]
                + weights[0] * carry[owner, rows + at : rows + at + 1, :]
            )
            for c, z, at in places
        ]
        for (c, z, at), field in zip(places, fields):
            app[c, z] = field
        levels_here = pl.ds(owner * per, per)
        pltpu.make_async_copy(app.at[:, levels_here], out_hbm.at[:, levels_here], out_sem).start()
        return 0

    lax.fori_loop(0, owners, update_owner, 0)
    totals = gathered(mass_recv, 3, comps)
    for c in range(comps):
        ratio = jnp.sqrt(mean_square[c] / (totals[c] / cells + EPS))
        ratio_ref[c : c + 1, :] = jnp.broadcast_to(ratio, (1, lanes))

    @pl.when(gx < owners)
    def _():
        wait_bytes(tip_send.at[pl.ds(0, owners - 1)], send_sem.at[0])
        wait_bytes(orb_tip_send.at[pl.ds(0, owners - 1)], send_sem.at[4])
        wait_bytes(carry_send.at[pl.ds(1, groups - 1)], send_sem.at[2])

    @pl.when(gx >= owners)
    def _():
        wait_bytes(tip_send, send_sem.at[0])
        wait_bytes(orb_tip_send, send_sem.at[4])

    wait_bytes(sums_recv.at[pl.ds(1, devices - 1)], send_sem.at[1])
    wait_bytes(mass_recv.at[pl.ds(1, devices - 1)], send_sem.at[3])
    pltpu.make_async_copy(app, out_hbm, out_sem).wait()


def scale_kernel(update, ratio, out_hbm, stage, sem):
    comps, levels = update.shape[:2]
    part = levels // SCALE_PARTS
    for c in range(comps):
        for i in range(SCALE_PARTS):
            here = pl.ds(i * part, part)
            stage[c, here] = update[c, here] * ratio[c : c + 1, :]
            pltpu.make_async_copy(stage.at[c, here], out_hbm.at[c, here], sem).start()
    pltpu.make_async_copy(stage, out_hbm, sem).wait()


def shards(orbitals, potential, shift_ratio):
    groups = lax.axis_size("gx")
    columns = lax.axis_size("gy")
    comps, levels, width, lanes = orbitals.shape
    assert columns == 2 and lanes == LANES and 2 * comps * levels == lanes
    assert comps * levels == width
    owners = min(groups, levels)
    rows = comps * (levels // owners)
    early = levels // 2
    planes = comps * levels
    devices = groups * columns
    cells = float(levels * width * groups * lanes * columns)
    f32 = jnp.float32
    update, ratio = pl.pallas_call(
        functools.partial(step_kernel, groups, owners, cells),
        out_shape=(
            jax.ShapeDtypeStruct(orbitals.shape, f32),
            jax.ShapeDtypeStruct((comps, lanes), f32),
        ),
        in_specs=[
            pl.BlockSpec(memory_space=pltpu.SMEM),
            pl.BlockSpec(memory_space=pltpu.HBM),
            pl.BlockSpec(memory_space=pltpu.HBM),
        ],
        out_specs=(
            pl.BlockSpec(memory_space=pl.ANY),
            pl.BlockSpec(memory_space=pltpu.VMEM),
        ),
        scratch_shapes=[
            pltpu.VMEM(orbitals.shape, f32),
            pltpu.VMEM(potential.shape, f32),
            pltpu.VMEM(orbitals.shape, f32),
            pltpu.VMEM((comps, early, width, lanes), f32),
            pltpu.VMEM((width, 3 * width), jnp.bfloat16),
            pltpu.VMEM((2, width, lanes), f32),
            pltpu.VMEM((2, planes, lanes), f32),
            pltpu.VMEM((planes, lanes), f32),
            pltpu.VMEM((width, lanes), f32),
            pltpu.VMEM((width, lanes), f32),
            pltpu.VMEM((2, planes, lanes), f32),
            pltpu.VMEM((2, planes, lanes), f32),
            pltpu.VMEM((owners, 2 * rows, lanes), f32),
            pltpu.VMEM((groups, 2 * rows, lanes), f32),
            pltpu.VMEM((owners, 2 * rows, lanes), f32),
            pltpu.VMEM((groups, 2 * rows, lanes), f32),
            pltpu.VMEM((groups, 2 * rows, lanes), f32),
            pltpu.VMEM((owners, 2 * rows, lanes), f32),
            pltpu.VMEM((1, 1, lanes), f32),
            pltpu.VMEM((devices, 1, lanes), f32),
            pltpu.VMEM((1, 1, lanes), f32),
            pltpu.VMEM((devices, 1, lanes), f32),
            pltpu.SemaphoreType.DMA((CHUNKS + 1,)),
            pltpu.SemaphoreType.DMA((2,)),
            pltpu.SemaphoreType.DMA((2,)),
            pltpu.SemaphoreType.DMA((5,)),
            pltpu.SemaphoreType.DMA((5,)),
            pltpu.SemaphoreType.DMA,
        ],
        compiler_params=pltpu.CompilerParams(
            collective_id=0, has_side_effects=True, vmem_limit_bytes=32 * 1024 * 1024
        ),
        name="power_step",
    )(
        shift_ratio,
        pltpu.with_memory_space_constraint(orbitals, pltpu.HBM),
        pltpu.with_memory_space_constraint(potential, pltpu.HBM),
    )
    return pl.pallas_call(
        scale_kernel,
        out_shape=jax.ShapeDtypeStruct(orbitals.shape, f32),
        in_specs=[pl.BlockSpec(memory_space=pltpu.VMEM), pl.BlockSpec(memory_space=pltpu.VMEM)],
        out_specs=pl.BlockSpec(memory_space=pl.ANY),
        scratch_shapes=[pltpu.VMEM(orbitals.shape, f32), pltpu.SemaphoreType.DMA],
        compiler_params=pltpu.CompilerParams(vmem_limit_bytes=32 * 1024 * 1024),
        name="scale",
    )(
        pltpu.with_memory_space_constraint(update, pltpu.VMEM),
        pltpu.with_memory_space_constraint(ratio, pltpu.VMEM),
    )


def solution(mesh):
    in_specs = (P(None, None, "gx", "gy"), P(None, "gx", "gy"), P())
    out_specs = P(None, None, "gx", "gy")
    return jax.shard_map(shards, mesh=mesh, in_specs=in_specs, out_specs=out_specs, check_vma=False)
```
